32 devices in a mesh: groups: 2 (over x), rows: 8 (over z, y), fsdp: 2 (over core).
Axes of the slice: x: 2, y: 2, z: 4, core: 2. Of those that a mesh axis runs over, the one named last changes fastest.
Arguments:
- image: bfloat16 [32, 256, 512], P(('groups', 'rows'), 'fsdp'), parts along dimension 0, may hold values from -81 to 81
- deconv_weight: bfloat16 [4, 4, 512, 256], P(None, None, None, 'fsdp'), may hold values from -0.125 to 0.125
- norm_gain: float32 [256], replicated, may hold values from 0.1 to 1.9
- norm_shift: float32 [256], replicated, may hold values from -3 to 3
- first_weight: bfloat16 [3, 3, 256, 256], P(None, None, None, 'fsdp'), may hold values from -0.125 to 0.125
- first_bias: float32 [256], replicated, may hold values from -3 to 3
- second_weight: bfloat16 [3, 3, 256, 256], P(None, None, None, 'fsdp'), may hold values from -0.125 to 0.125
- second_bias: float32 [256], replicated, may hold values from -3 to 3
Outputs:
- result: bfloat16 [64, 512, 256], P(('groups', 'rows'), 'fsdp'), parts along dimension 0
The draws below stay inside these ranges and needn't reach their ends.
There are 2 independent parts, one for each index of `groups`. The reference program is written for one: setup_inputs(seed, part) draws one part's arguments, and reference() takes and returns one part's arrays. A program takes and returns all parts, laid end to end along the dimension named above; an argument that names none is the same for every part. Nothing has to cross between parts.
All inputs are finite; a program needn't handle non-finite values.
Results may differ from the reference program's by a relative error of at most 0.0055.
Values may be sent and summed in bfloat16 or wider, within the bound.
No kernel may reach another device: no remote copies, remote signals or barrier semaphores. Data moves between devices by JAX's collectives and lax.ppermute only.
A program may use at most 64 MiB of HBM per device.

```python
import jax
import jax.numpy as jnp
from jax import lax

CIN = 512
COUT = 256
NORM_GROUPS = 32
IN_ROWS = 16
IN_COLS = 256


def draw_image(key, part):
    first_key, second_key = jax.random.split(key, 2)
    position = jnp.arange(IN_ROWS, dtype=jnp.float32) / max(IN_ROWS - 1, 1)
    offset = jax.random.uniform(second_key, (CIN,), jnp.float32, -1.0, 1.0)
    base = jnp.clip(jax.random.normal(first_key, (IN_ROWS, IN_COLS, CIN), jnp.float32), -6.0, 6.0)
    values = (base + offset) * (1.0 + 2.0 * position)[:, None, None]
    return values.astype(jnp.bfloat16)


def levels(own_key, dims, cuts, low, largest):
    def one(dim, blocks):
        heights = jax.random.uniform(jax.random.fold_in(jax.random.fold_in(own_key, 6), dim), (blocks,), jnp.float32, low / len(cuts), largest / len(cuts))
        return jnp.repeat(jnp.exp(heights), dims[dim] // blocks).reshape((-1,) + (1,) * (len(dims) - dim - 1))

    loudness = one(*cuts[0])
    for cut in cuts[1:]:
        loudness = loudness * one(*cut)
    return loudness


def bell_draw(key, extent, scale, bound, shards=(), kind=jnp.bfloat16):
    gain = levels(key, extent, shards, -0.22, 0.18) if shards else 1.0
    values = jax.random.normal(key, extent, jnp.float32) * scale * gain
    return jnp.minimum(jnp.maximum(values, -bound), bound).astype(kind)


def setup_inputs(seed: int = 0, part: int = 0) -> dict:
    splits = jax.random.split(jax.random.key(seed), 9)
    part_splits = jax.random.split(jax.random.fold_in(splits[8], part), 9)
    return {
        "image": draw_image(jax.random.fold_in(jax.random.fold_in(splits[8], part), 71), part),
        "deconv_weight": bell_draw(splits[1], (4, 4, CIN, COUT), (4 * CIN) ** -0.5, 0.125, ((3, 2),)),
        "norm_gain": jnp.clip(1.0 + 0.18 * jax.random.normal(splits[2], (COUT,), jnp.float32), 0.1, 1.9),
        "norm_shift": bell_draw(splits[3], (COUT,), 0.5, 3.0, (), jnp.float32),
        "first_weight": bell_draw(splits[4], (3, 3, COUT, COUT), (9 * COUT) ** -0.5, 0.125, ((3, 2),)),
        "first_bias": bell_draw(splits[5], (COUT,), 0.5, 3.0, (), jnp.float32),
        "second_weight": bell_draw(splits[6], (3, 3, COUT, COUT), (9 * COUT) ** -0.5, 0.125, ((3, 2),)),
        "second_bias": bell_draw(splits[7], (COUT,), 0.5, 3.0, (), jnp.float32),
    }


TAP_TABLE = (((0, 3), (1, 1)), ((1, 2), (2, 0)))

def upsample(padded, weight):
    height = padded.shape[0] - 2
    breadth = padded.shape[1] - 2
    inputs = padded.shape[2]
    outputs = weight.shape[3]
    phases = []
    for phase_row in range(2):
        line = []
        for phase_col in range(2):
            total = jnp.zeros((height * breadth, outputs), jnp.float32)
            for row_off, row_tap in TAP_TABLE[phase_row]:
                for col_off, col_tap in TAP_TABLE[phase_col]:
                    patch = padded[row_off:row_off + height, col_off:col_off + breadth].reshape(height * breadth, inputs)
                    total = total + jnp.dot(patch, weight[row_tap, col_tap], preferred_element_type=jnp.float32)
            line.append(total.reshape(height, breadth, outputs))
        phases.append(jnp.stack(line, axis=2))
    stacked = jnp.stack(phases, axis=1)
    return stacked.reshape(2 * height, 2 * breadth, outputs)

def convolve(padded, weight):
    height = padded.shape[0] - 2
    breadth = padded.shape[1] - 2
    inputs = padded.shape[2]
    outputs = weight.shape[3]
    total = jnp.zeros((height * breadth, outputs), jnp.float32)
    for row_tap in range(3):
        for col_tap in range(3):
            patch = padded[row_tap:row_tap + height, col_tap:col_tap + breadth].reshape(height * breadth, inputs)
            total = total + jnp.dot(patch, weight[row_tap, col_tap], preferred_element_type=jnp.float32)
    return total.reshape(height, breadth, outputs)

def reference(image, deconv_weight, norm_gain, norm_shift, first_weight, first_bias, second_weight, second_bias):
    padded = jnp.pad(image, ((1, 1), (1, 1), (0, 0)))
    upsampled = upsample(padded, deconv_weight).astype(jnp.bfloat16)
    values = upsampled.astype(jnp.float32)
    width = COUT // NORM_GROUPS
    grouped = values.reshape(-1, NORM_GROUPS, width)
    count = grouped.shape[0] * width
    mean = lax.optimization_barrier(jnp.sum(grouped, axis=(0, 2))) / count
    centered = grouped - mean[None, :, None]
    spread = lax.optimization_barrier(jnp.sum(centered * centered, axis=(0, 2))) / count
    scale = jnp.repeat(lax.rsqrt(spread + 1e-05), width) * norm_gain
    shift = norm_shift - jnp.repeat(mean, width) * scale
    hidden = jax.nn.silu(values * scale + shift).astype(jnp.bfloat16)
    first = convolve(jnp.pad(hidden, ((1, 1), (1, 1), (0, 0))), first_weight) + first_bias
    activated = jax.nn.silu(first).astype(jnp.bfloat16)
    second = convolve(jnp.pad(activated, ((1, 1), (1, 1), (0, 0))), second_weight) + second_bias
    return second.astype(jnp.bfloat16)
```

```python
import functools

import jax
import jax.numpy as jnp
from jax import lax
from jax.experimental import pallas as pl
from jax.experimental.pallas import tpu as pltpu
from jax.sharding import PartitionSpec as P

NORM_GROUPS = 32
HALO = 2
EDGE = 16
VMEM_BYTES = 40 * 2**20


def silu(v):
    h = 0.5 * v
    return h + h * jnp.tanh(h)


def edge_mask(width):
    column = lax.axis_index("fsdp")
    last = lax.axis_size("fsdp") - 1
    cell = lax.broadcasted_iota(jnp.int32, (width + EDGE, 1), 0) - width
    right = (cell < EDGE // 2) & (column < last)
    left = (cell >= EDGE // 2) & (column > 0)
    return (cell < 0) | right | left


def deconv_kernel(own_ref, up_ref, down_ref, edge_ref, own_w, other_w, u_ref, stats_ref, xs, wd, sems):
    rows, width, cin = own_ref.shape
    lanes = own_w.shape[-1]
    taps = own_w.shape[0]
    column = lax.axis_index("fsdp")
    copies = []
    for kr in range(taps):
        for phase in range(2):
            for side, ref in enumerate((own_w, other_w)):
                place = column if side == 0 else 1 - column
                copies.append(
                    pltpu.make_async_copy(
                        ref.at[kr, :, 1 - phase],
                        wd.at[kr, phase, :, :, pl.ds(pl.multiple_of(place * lanes, lanes), lanes)],
                        sems.at[kr, phase, side],
                    )
                )
    for copy in copies:
        copy.start()

    cell = lax.broadcasted_iota(jnp.int32, (EDGE, 1), 0)
    keep = jnp.where(column == 0, cell, EDGE - 1 - cell) < EDGE // 2
    for row in range(rows + 2 * HALO):
        if row < HALO:
            main = up_ref[row]
        elif row < HALO + rows:
            main = own_ref[row - HALO]
        else:
            main = down_ref[row - HALO - rows]
        edge = jnp.where(keep, edge_ref[row].astype(jnp.float32), 0.0)
        line = jnp.concatenate([main.astype(jnp.float32), edge], axis=0)
        total = width + EDGE
        xs[row, :, 0:cin] = pltpu.roll(line, total - 1, 0).astype(jnp.bfloat16)
        xs[row, :, cin : 2 * cin] = line.astype(jnp.bfloat16)
        xs[row, :, 2 * cin : 3 * cin] = pltpu.roll(line, 1, 0).astype(jnp.bfloat16)
    for copy in copies:
        copy.wait()

    total = width + EDGE
    lines = rows + 2
    cout = u_ref.shape[-1]
    sums = jnp.zeros((1, cout), jnp.float32)
    squares = jnp.zeros((1, cout), jnp.float32)
    for phase_row in range(2):
        first, second = ((3, 1), (2, 0))[phase_row]
        for phase in range(2):
            low = (1 - phase) * cin
            part = slice(low, low + 2 * cin)
            acc = jnp.dot(
                xs[phase_row : phase_row + lines, :, part].reshape(lines * total, 2 * cin),
                wd[first, phase].reshape(2 * cin, cout),
                preferred_element_type=jnp.float32,
            ) + jnp.dot(
                xs[phase_row + 1 : phase_row + 1 + lines, :, part].reshape(lines * total, 2 * cin),
                wd[second, phase].reshape(2 * cin, cout),
                preferred_element_type=jnp.float32,
            )
            acc = acc.astype(jnp.bfloat16).reshape(lines, total, cout)
            for line in range(lines):
                u_ref[2 * line + phase_row, phase] = acc[line]
                if 1 <= line < 1 + rows:
                    values = acc[line, :width].astype(jnp.float32)
                    sums += jnp.sum(values, axis=0, keepdims=True)
                    squares += jnp.sum(values * values, axis=0, keepdims=True)
    half = cout // 2
    block = jnp.concatenate(
        [sums[:, :half], sums[:, half:], squares[:, :half], squares[:, half:]]
        + [jnp.zeros((4, half), jnp.float32)],
        axis=0,
    )
    for peer in range(stats_ref.shape[0]):
        stats_ref[peer] = block


def group_sum(v, width):
    lane = lax.broadcasted_iota(jnp.int32, v.shape, 1)
    size = v.shape[1]
    step = 1
    while step < width:
        v = v + jnp.where(
            (lane & step) == 0, pltpu.roll(v, size - step, 1), pltpu.roll(v, step, 1)
        )
        step *= 2
    return v


def fill(ref, row, even, odd):
    total, channels = even.shape
    ref[row, :, 0:channels] = pltpu.roll(odd, 1, 0).astype(jnp.bfloat16)
    ref[row, :, channels : 2 * channels] = even.astype(jnp.bfloat16)
    ref[row, :, 2 * channels : 3 * channels] = odd.astype(jnp.bfloat16)
    ref[row, :, 3 * channels : 4 * channels] = pltpu.roll(even, total - 1, 0).astype(jnp.bfloat16)


def conv_kernel(count, u_ref, stats_ref, params_ref, w1_ref, w2_ref, out_ref, g, act, w1, w2, mixed, sems):
    lines, _, total, cout = u_ref.shape
    width = total - EDGE
    lanes = w1_ref.shape[-1]
    copies = []
    for index, (src, dst) in enumerate(((w1_ref, w1), (w2_ref, w2))):
        for side in range(src.shape[0]):
            copies.append(
                pltpu.make_async_copy(
                    src.at[side],
                    dst.at[:, :, :, side * lanes : (side + 1) * lanes],
                    sems.at[index, side],
                )
            )
    for copy in copies:
        copy.start()

    block = stats_ref[0]
    for peer in range(1, stats_ref.shape[0]):
        block += stats_ref[peer]
    width_group = cout // NORM_GROUPS
    sums = jnp.concatenate([block[0:1], block[1:2]], axis=1)
    squares = jnp.concatenate([block[2:3], block[3:4]], axis=1)
    mean = group_sum(sums, width_group) / count
    spread = group_sum(squares, width_group) / count - mean * mean
    scale = lax.rsqrt(spread + 1e-05) * params_ref[0:1]
    shift = params_ref[1:2] - mean * scale

    mask = edge_mask(width)
    place = lax.axis_index("rows")
    last = lax.axis_size("rows") - 1

    def inside(row, beyond):
        if row < beyond:
            return mask & (place > 0)
        if row >= lines - 2 * HALO + beyond:
            return mask & (place < last)
        return mask

    for row in range(lines):
        seen = inside(row, HALO)
        pair = [
            jnp.where(seen, silu(u_ref[row, phase].astype(jnp.float32) * scale + shift), 0.0)
            for phase in range(2)
        ]
        fill(g, row, *pair)
    for copy in copies[:2]:
        copy.wait()
    bias = params_ref[2:3]
    chunk = 2
    for start in range(0, lines - 2, chunk):
        results = []
        for phase in range(2):
            acc = bias
            for a in range(3):
                acc = acc + jnp.dot(
                    g[start + a : start + a + chunk, :, phase * cout : (phase + 3) * cout].reshape(
                        chunk * total, 3 * cout
                    ),
                    w1[a].reshape(3 * cout, cout),
                    preferred_element_type=jnp.float32,
                )
            results.append(silu(acc).reshape(chunk, total, cout))
        for row in range(chunk):
            seen = inside(start + row, 1)
            fill(act, start + row, *[jnp.where(seen, r[row], 0.0) for r in results])
    for copy in copies[2:]:
        copy.wait()
    bias = params_ref[3:4]
    for start in range(0, lines - 4, chunk):
        for phase in range(2):
            acc = bias
            for a in range(3):
                acc = acc + jnp.dot(
                    act[start + a : start + a + chunk, 0:width, phase * cout : (phase + 3) * cout].reshape(
                        chunk * width, 3 * cout
                    ),
                    w2[a].reshape(3 * cout, cout),
                    preferred_element_type=jnp.float32,
                )
            acc = acc.reshape(chunk, width, cout)
            for row in range(chunk):
                for side in range(0, cout, 128):
                    mixed[side // 128, start + row, pl.ds(phase, width, stride=2), :] = acc[row, :, side : side + 128]
    for row in range(lines - 4):
        for side in range(0, cout, 128):
            out_ref[row, :, side : side + 128] = mixed[side // 128, row].astype(jnp.bfloat16)


def local(image, deconv_weight, norm_gain, norm_shift, first_weight, first_bias, second_weight, second_bias):
    rows, width, cin = image.shape
    taps, _, _, lanes = deconv_weight.shape
    columns = lax.axis_size("fsdp")
    cout = lanes * columns
    assert columns == 2 and rows >= HALO and width % EDGE == 0
    n_rows = lax.axis_size("rows")
    n = n_rows * columns
    count = float(2 * rows * n_rows * 2 * width * columns * (cout // NORM_GROUPS))
    swap = [(0, 1), (1, 0)]

    up = lax.ppermute(image[rows - HALO :], "rows", [(i, i + 1) for i in range(n_rows - 1)])
    down = lax.ppermute(image[:HALO], "rows", [(i + 1, i) for i in range(n_rows - 1)])
    other_w = lax.ppermute(deconv_weight, "fsdp", swap)
    first_all = lax.all_gather(first_weight, "fsdp")
    second_all = lax.all_gather(second_weight, "fsdp")
    rimmed = jnp.concatenate([up, image, down], axis=0)
    sent = jnp.where(lax.axis_index("fsdp") == 0, rimmed[:, width - EDGE :], rimmed[:, :EDGE])
    edge = lax.ppermute(sent, "fsdp", swap)

    total = width + EDGE
    any_spec = pl.BlockSpec(memory_space=pl.ANY)
    vmem = pl.BlockSpec(memory_space=pltpu.VMEM)
    shape_w = (taps, taps // 2, 2, cin, lanes)
    u, stats = pl.pallas_call(
        deconv_kernel,
        out_shape=(
            jax.ShapeDtypeStruct((2 * rows + 2 * HALO, 2, total, cout), jnp.bfloat16),
            jax.ShapeDtypeStruct((n, 8, cout // 2), jnp.float32),
        ),
        in_specs=[vmem] * 4 + [any_spec] * 2,
        out_specs=(vmem, vmem),
        scratch_shapes=[
            pltpu.VMEM((rows + 2 * HALO, total, 3 * cin), jnp.bfloat16),
            pltpu.VMEM((taps, 2, taps // 2, cin, cout), jnp.bfloat16),
            pltpu.SemaphoreType.DMA((taps, 2, 2)),
        ],
        compiler_params=pltpu.CompilerParams(vmem_limit_bytes=VMEM_BYTES),
        name="deconv",
    )(image, up, down, edge, deconv_weight.reshape(shape_w), other_w.reshape(shape_w))

    gathered = lax.all_to_all(stats, ("rows", "fsdp"), split_axis=0, concat_axis=0)
    params = jnp.stack([norm_gain, norm_shift, first_bias, second_bias])
    out = pl.pallas_call(
        functools.partial(conv_kernel, count),
        out_shape=jax.ShapeDtypeStruct((2 * rows, 2 * width, cout), jnp.bfloat16),
        in_specs=[vmem] * 3 + [any_spec] * 2,
        out_specs=vmem,
        scratch_shapes=[
            pltpu.VMEM((2 * rows + 2 * HALO, total, 4 * cout), jnp.bfloat16),
            pltpu.VMEM((2 * rows + 2, total, 4 * cout), jnp.bfloat16),
            pltpu.VMEM((3, 3, cout, cout), jnp.bfloat16),
            pltpu.VMEM((3, 3, cout, cout), jnp.bfloat16),
            pltpu.VMEM((cout // 128, 2 * rows, 2 * width, 128), jnp.float32),
            pltpu.SemaphoreType.DMA((2, 2)),
        ],
        compiler_params=pltpu.CompilerParams(vmem_limit_bytes=VMEM_BYTES),
        name="convs",
    )(u, gathered, params, first_all, second_all)
    return out


def solution(mesh):
    placed = (
        P(("groups", "rows"), "fsdp", None),
        P(None, None, None, "fsdp"),
        P(),
        P(),
        P(None, None, None, "fsdp"),
        P(),
        P(None, None, None, "fsdp"),
        P(),
    )
    return jax.shard_map(
        local,
        mesh=mesh,
        in_specs=placed,
        out_specs=P(("groups", "rows"), "fsdp", None),
        check_vma=False,
    )
```

```python
import functools

import jax
import jax.numpy as jnp
from jax import lax
from jax.experimental import pallas as pl
from jax.experimental.pallas import tpu as pltpu
from jax.sharding import PartitionSpec as P

NORM_GROUPS = 32
HALO = 2
EDGE = 16
VMEM_BYTES = 40 * 2**20


def silu(v):
    h = 0.5 * v
    return h + h * jnp.tanh(h)


def edge_mask(width):
    column = lax.axis_index("fsdp")
    last = lax.axis_size("fsdp") - 1
    cell = lax.broadcasted_iota(jnp.int32, (width + EDGE, 1), 0) - width
    right = (cell < EDGE // 2) & (column < last)
    left = (cell >= EDGE // 2) & (column > 0)
    return (cell < 0) | right | left


def load_deconv(own_w, other_w, wd, sems):
    lanes = own_w.shape[-1]
    column = lax.axis_index("fsdp")
    copies = []
    for kr in range(own_w.shape[0]):
        for phase in range(2):
            for side, ref in enumerate((own_w, other_w)):
                place = column if side == 0 else 1 - column
                copies.append(
                    pltpu.make_async_copy(
                        ref.at[kr, :, 1 - phase],
                        wd.at[kr, phase, :, :, pl.ds(pl.multiple_of(place * lanes, lanes), lanes)],
                        sems.at[kr, phase, side],
                    )
                )
    for copy in copies:
        copy.start()
    return copies


def spread_line(xs, index, main, edge):
    cin = main.shape[-1]
    cell = lax.broadcasted_iota(jnp.int32, (EDGE, 1), 0)
    keep = jnp.where(lax.axis_index("fsdp") == 0, cell, EDGE - 1 - cell) < EDGE // 2
    edge = jnp.where(keep, edge.astype(jnp.float32), 0.0)
    line = jnp.concatenate([main.astype(jnp.float32), edge], axis=0)
    xs[index, :, 0:cin] = pltpu.roll(line, line.shape[0] - 1, 0).astype(jnp.bfloat16)
    xs[index, :, cin : 2 * cin] = line.astype(jnp.bfloat16)
    xs[index, :, 2 * cin : 3 * cin] = pltpu.roll(line, 1, 0).astype(jnp.bfloat16)


def tap_dot(xs, lines, phase, weight):
    _, total, lanes = xs.shape
    cin = lanes // 3
    low = (1 - phase) * cin
    part = xs[lines, :, low : low + 2 * cin]
    count = part.shape[0]
    out = jnp.dot(
        part.reshape(count * total, 2 * cin),
        weight.reshape(2 * cin, weight.shape[-1]),
        preferred_element_type=jnp.float32,
    )
    return out.reshape(count, total, weight.shape[-1])


def main_kernel(own_ref, edge_ref, next_ref, next_edge_ref, own_w, other_w, u_ref, part_ref, stats_ref, xs, wd, sems):
    rows, width, cin = own_ref.shape
    cout = u_ref.shape[-1]
    copies = load_deconv(own_w, other_w, wd, sems)
    for row in range(rows):
        spread_line(xs, row, own_ref[row], edge_ref[row])
    spread_line(xs, rows, next_ref[0], next_edge_ref[0])
    for copy in copies:
        copy.wait()

    place = lax.axis_index("rows")
    first_here = place == 0
    last_here = place == lax.axis_size("rows") - 1
    sums = jnp.zeros((1, cout), jnp.float32)
    squares = jnp.zeros((1, cout), jnp.float32)
    for phase in range(2):
        upper = tap_dot(xs, slice(0, rows + 1), phase, wd[1, phase])
        even = upper[1:] + tap_dot(xs, slice(0, rows), phase, wd[3, phase])
        part_ref[phase] = upper[0]
        odd = tap_dot(xs, slice(0, rows), phase, wd[2, phase]) + tap_dot(
            xs, slice(1, rows + 1), phase, wd[0, phase]
        )
        lines = []
        for row in range(rows):
            lines += [odd[row].astype(jnp.bfloat16), even[row].astype(jnp.bfloat16)]
        for row, line in enumerate(lines):
            u_ref[row, phase] = line
        edge_line = jnp.where(first_here, upper[0].astype(jnp.bfloat16).astype(jnp.float32), 0.0)
        final_line = jnp.where(last_here, 0.0, lines[-1].astype(jnp.float32))
        for line in lines[:-1] + [edge_line, final_line]:
            values = line[:width].astype(jnp.float32)
            sums += jnp.sum(values, axis=0, keepdims=True)
            squares += jnp.sum(values * values, axis=0, keepdims=True)
    half = cout // 2
    stats_ref[...] = jnp.concatenate(
        [sums[:, :half], sums[:, half:], squares[:, :half], squares[:, half:]]
        + [jnp.zeros((4, half), jnp.float32)],
        axis=0,
    )


def halo_kernel(above_ref, own_ref, edge_ref, next_ref, next_edge_ref, below_ref, part_ref, own_w, other_w, u_ref, xs, wd, sems):
    rows, width, cin = own_ref.shape
    copies = load_deconv(own_w, other_w, wd, sems)
    spread_line(xs, 0, above_ref[0, :width], above_ref[0, width:])
    spread_line(xs, 1, above_ref[1, :width], above_ref[1, width:])
    spread_line(xs, 2, next_ref[0], next_edge_ref[0])
    spread_line(xs, 3, own_ref[0], edge_ref[0])
    spread_line(xs, 4, below_ref[0, :width], below_ref[0, width:])
    for copy in copies:
        copy.wait()
    for phase in range(2):
        outer = tap_dot(xs, slice(0, 2), phase, wd[3, phase])
        u_ref[0, phase] = (outer[0] + tap_dot(xs, slice(1, 2), phase, wd[1, phase])[0]).astype(jnp.bfloat16)
        u_ref[2, phase] = (outer[1] + part_ref[phase]).astype(jnp.bfloat16)
        odd = tap_dot(xs, slice(1, 3), phase, wd[2, phase]) + tap_dot(xs, slice(3, 5), phase, wd[0, phase])
        u_ref[1, phase] = odd[0].astype(jnp.bfloat16)
        u_ref[3, phase] = odd[1].astype(jnp.bfloat16)


def group_sum(v, width):
    lane = lax.broadcasted_iota(jnp.int32, v.shape, 1)
    size = v.shape[1]
    step = 1
    while step < width:
        v = v + jnp.where(
            (lane & step) == 0, pltpu.roll(v, size - step, 1), pltpu.roll(v, step, 1)
        )
        step *= 2
    return v


def fill(ref, row, even, odd):
    total, channels = even.shape
    ref[row, :, 0:channels] = pltpu.roll(odd, 1, 0).astype(jnp.bfloat16)
    ref[row, :, channels : 2 * channels] = even.astype(jnp.bfloat16)
    ref[row, :, 2 * channels : 3 * channels] = odd.astype(jnp.bfloat16)
    ref[row, :, 3 * channels : 4 * channels] = pltpu.roll(even, total - 1, 0).astype(jnp.bfloat16)


def conv_kernel(
    count, u_ref, halo_ref, stats_ref, params_ref, own_w1, other_w1, own_w2, other_w2, out_ref, g, act, w1, w2, mixed, sems
):
    main, _, total, cout = u_ref.shape
    lines = main + 2 * HALO
    width = total - EDGE
    lanes = own_w1.shape[-1]
    column = lax.axis_index("fsdp")
    copies = []
    for index, (own, other, dst) in enumerate(((own_w1, other_w1, w1), (own_w2, other_w2, w2))):
        for side, src in enumerate((own, other)):
            place = column if side == 0 else 1 - column
            copies.append(
                pltpu.make_async_copy(
                    src,
                    dst.at[:, :, :, pl.ds(pl.multiple_of(place * lanes, lanes), lanes)],
                    sems.at[index, side],
                )
            )
    for copy in copies:
        copy.start()

    block = stats_ref[...]
    width_group = cout // NORM_GROUPS
    sums = jnp.concatenate([block[0:1], block[1:2]], axis=1)
    squares = jnp.concatenate([block[2:3], block[3:4]], axis=1)
    mean = group_sum(sums, width_group) / count
    spread = group_sum(squares, width_group) / count - mean * mean
    scale = lax.rsqrt(spread + 1e-05) * params_ref[0:1]
    shift = params_ref[1:2] - mean * scale

    mask = edge_mask(width)
    place = lax.axis_index("rows")
    last = lax.axis_size("rows") - 1

    def inside(row, beyond):
        if row < beyond:
            return mask & (place > 0)
        if row >= lines - 2 * HALO + beyond:
            return mask & (place < last)
        return mask

    for row in range(lines):
        seen = inside(row, HALO)
        if row < 3:
            source = halo_ref.at[row]
        elif row < 3 + main:
            source = u_ref.at[row - 3]
        else:
            source = halo_ref.at[3]
        pair = [
            jnp.where(seen, silu(source[phase].astype(jnp.float32) * scale + shift), 0.0)
            for phase in range(2)
        ]
        fill(g, row, *pair)
    for copy in copies[:2]:
        copy.wait()
    bias = params_ref[2:3]
    chunk = 2
    for start in range(0, lines - 2, chunk):
        results = []
        for phase in range(2):
            acc = bias
            for a in range(3):
                acc = acc + jnp.dot(
                    g[start + a : start + a + chunk, :, phase * cout : (phase + 3) * cout].reshape(
                        chunk * total, 3 * cout
                    ),
                    w1[a].reshape(3 * cout, cout),
                    preferred_element_type=jnp.float32,
                )
            results.append(silu(acc).reshape(chunk, total, cout))
        for row in range(chunk):
            seen = inside(start + row, 1)
            fill(act, start + row, *[jnp.where(seen, r[row], 0.0) for r in results])
    for copy in copies[2:]:
        copy.wait()
    bias = params_ref[3:4]
    for start in range(0, lines - 4, chunk):
        for phase in range(2):
            acc = bias
            for a in range(3):
                acc = acc + jnp.dot(
                    act[start + a : start + a + chunk, 0:width, phase * cout : (phase + 3) * cout].reshape(
                        chunk * width, 3 * cout
                    ),
                    w2[a].reshape(3 * cout, cout),
                    preferred_element_type=jnp.float32,
                )
            acc = acc.reshape(chunk, width, cout)
            for row in range(chunk):
                for side in range(0, cout, 128):
                    mixed[side // 128, start + row, pl.ds(phase, width, stride=2), :] = acc[row, :, side : side + 128]
    for row in range(lines - 4):
        for side in range(0, cout, 128):
            out_ref[row, :, side : side + 128] = mixed[side // 128, row].astype(jnp.bfloat16)


def total_over(block, axes):
    for axis in axes:
        size = lax.axis_size(axis)
        if size & (size - 1):
            block = lax.psum(block, axis)
            continue
        step = 1
        while step < size:
            block = block + lax.ppermute(block, axis, [(i, i ^ step) for i in range(size)])
            step *= 2
    return block


def local(image, deconv_weight, norm_gain, norm_shift, first_weight, first_bias, second_weight, second_bias):
    rows, width, cin = image.shape
    taps, _, _, lanes = deconv_weight.shape
    columns = lax.axis_size("fsdp")
    cout = lanes * columns
    assert columns == 2 and rows >= HALO and width % EDGE == 0
    n_rows = lax.axis_size("rows")
    count = float(2 * rows * n_rows * 2 * width * columns * (cout // NORM_GROUPS))
    swap = [(0, 1), (1, 0)]
    to_next = [(i, i + 1) for i in range(n_rows - 1)]
    to_previous = [(i + 1, i) for i in range(n_rows - 1)]
    to_previous_swapped = [(2 * i + 2 + k, 2 * i + 1 - k) for i in range(n_rows - 1) for k in range(2)]

    edges = jnp.where(lax.axis_index("fsdp") == 0, image[:, width - EDGE :], image[:, :EDGE])
    following = lax.ppermute(image[:1], "rows", to_previous)
    following_edge = lax.ppermute(edges[:1], ("rows", "fsdp"), to_previous_swapped)
    edge = lax.ppermute(edges, "fsdp", swap)
    other_w = lax.ppermute(deconv_weight, "fsdp", swap)
    first_other = lax.ppermute(first_weight, "fsdp", swap)
    second_other = lax.ppermute(second_weight, "fsdp", swap)

    total = width + EDGE
    hbm = pl.BlockSpec(memory_space=pltpu.HBM)
    vmem = pl.BlockSpec(memory_space=pltpu.VMEM)
    shape_w = (taps, taps // 2, 2, cin, lanes)
    own_w, other_w = deconv_weight.reshape(shape_w), other_w.reshape(shape_w)
    deconv_scratch = [
        pltpu.VMEM((taps, 2, taps // 2, cin, cout), jnp.bfloat16),
        pltpu.SemaphoreType.DMA((taps, 2, 2)),
    ]
    u, part, stats = pl.pallas_call(
        main_kernel,
        out_shape=(
            jax.ShapeDtypeStruct((2 * rows, 2, total, cout), jnp.bfloat16),
            jax.ShapeDtypeStruct((2, total, cout), jnp.float32),
            jax.ShapeDtypeStruct((8, cout // 2), jnp.float32),
        ),
        in_specs=[vmem] * 4 + [hbm] * 2,
        out_specs=(vmem, vmem, vmem),
        scratch_shapes=[pltpu.VMEM((rows + 1, total, 3 * cin), jnp.bfloat16)] + deconv_scratch,
        compiler_params=pltpu.CompilerParams(vmem_limit_bytes=VMEM_BYTES),
        cost_estimate=pl.CostEstimate(flops=2 * 2 * (2 * rows) * total * 4 * cin * cout, bytes_accessed=2**22, transcendentals=0),
        name="deconv_main",
    )(image, edge, following, following_edge, own_w, other_w)

    lines, _ = lax.optimization_barrier((jnp.concatenate([image, edge], axis=1), following))
    above = lax.ppermute(lines[rows - HALO :], "rows", to_next)
    below = lax.ppermute(lines[1:HALO], "rows", to_previous)
    halo = pl.pallas_call(
        halo_kernel,
        out_shape=jax.ShapeDtypeStruct((4, 2, total, cout), jnp.bfloat16),
        in_specs=[vmem] * 7 + [hbm] * 2,
        out_specs=vmem,
        scratch_shapes=[pltpu.VMEM((5, total, 3 * cin), jnp.bfloat16)] + deconv_scratch,
        compiler_params=pltpu.CompilerParams(vmem_limit_bytes=VMEM_BYTES),
        cost_estimate=pl.CostEstimate(flops=2 * 2 * 4 * total * 4 * cin * cout, bytes_accessed=2**22, transcendentals=0),
        name="deconv_halo",
    )(above, image, edge, following, following_edge, below, part, own_w, other_w)

    totals = total_over(stats, ("fsdp", "rows"))
    params = jnp.stack([norm_gain, norm_shift, first_bias, second_bias])
    out = pl.pallas_call(
        functools.partial(conv_kernel, count),
        out_shape=jax.ShapeDtypeStruct((2 * rows, 2 * width, cout), jnp.bfloat16),
        in_specs=[vmem] * 4 + [hbm] * 4,
        out_specs=vmem,
        scratch_shapes=[
            pltpu.VMEM((2 * rows + 2 * HALO, total, 4 * cout), jnp.bfloat16),
            pltpu.VMEM((2 * rows + 2, total, 4 * cout), jnp.bfloat16),
            pltpu.VMEM((3, 3, cout, cout), jnp.bfloat16),
            pltpu.VMEM((3, 3, cout, cout), jnp.bfloat16),
            pltpu.VMEM((cout // 128, 2 * rows, 2 * width, 128), jnp.float32),
            pltpu.SemaphoreType.DMA((2, 2)),
        ],
        compiler_params=pltpu.CompilerParams(vmem_limit_bytes=VMEM_BYTES),
        cost_estimate=pl.CostEstimate(flops=5 * 10**9, bytes_accessed=2**22, transcendentals=0),
        name="convs",
    )(u, halo, totals, params, first_weight, first_other, second_weight, second_other)
    return out


def solution(mesh):
    placed = (
        P(("groups", "rows"), "fsdp", None),
        P(None, None, None, "fsdp"),
        P(),
        P(),
        P(None, None, None, "fsdp"),
        P(),
        P(None, None, None, "fsdp"),
        P(),
    )
    return jax.shard_map(
        local,
        mesh=mesh,
        in_specs=placed,
        out_specs=P(("groups", "rows"), "fsdp", None),
        check_vma=False,
    )
```

```python
import functools

import jax
import jax.numpy as jnp
from jax import lax
from jax.experimental import pallas as pl
from jax.experimental.pallas import tpu as pltpu
from jax.sharding import PartitionSpec as P

NORM_GROUPS = 32
HALO = 2
EDGE = 16
LANES = 128
VMEM_BYTES = 24 * 2**20


def silu(v):
    h = 0.5 * v
    return h + h * jnp.tanh(h)


def edge_mask(width):
    column = lax.axis_index("fsdp")
    last = lax.axis_size("fsdp") - 1
    cell = lax.broadcasted_iota(jnp.int32, (width + EDGE, 1), 0) - width
    right = (cell < EDGE // 2) & (column < last)
    left = (cell >= EDGE // 2) & (column > 0)
    return (cell < 0) | right | left


def cut_kernel(image_ref, line_ref, edges_ref, sems):
    width = image_ref.shape[1]
    start = pl.multiple_of((1 - lax.axis_index("fsdp")) * (width - EDGE), EDGE)
    copies = [
        pltpu.make_async_copy(image_ref.at[0:1], line_ref, sems.at[0]),
        pltpu.make_async_copy(image_ref.at[:, pl.ds(start, EDGE), :], edges_ref, sems.at[1]),
    ]
    for copy in copies:
        copy.start()
    for copy in copies:
        copy.wait()


def spread_line(out, main, edge):
    cin = main.shape[-1]
    cell = lax.broadcasted_iota(jnp.int32, (EDGE, 1), 0)
    keep = jnp.where(lax.axis_index("fsdp") == 0, cell, EDGE - 1 - cell) < EDGE // 2
    edge = jnp.where(keep, edge.astype(jnp.float32), 0.0)
    line = jnp.concatenate([main.astype(jnp.float32), edge], axis=0)
    out[:, 0:cin] = pltpu.roll(line, line.shape[0] - 1, 0).astype(jnp.bfloat16)
    out[:, cin : 2 * cin] = line.astype(jnp.bfloat16)
    out[:, 2 * cin : 3 * cin] = pltpu.roll(line, 1, 0).astype(jnp.bfloat16)


def own_kernel(image_ref, edge_ref, weight_ref, xs_ref, lines_ref, own_w_ref, held, sems):
    rows, width, _ = image_ref.shape
    copies = [
        pltpu.make_async_copy(image_ref, held, sems.at[0]),
        pltpu.make_async_copy(weight_ref, own_w_ref, sems.at[1]),
    ]
    for copy in copies:
        copy.start()
    copies[0].wait()
    for row in range(rows):
        spread_line(xs_ref.at[row], held[row], edge_ref[row])
        lines_ref[row, :width] = held[row]
        lines_ref[row, width:] = edge_ref[row]
    copies[1].wait()


def tap_dot(lines, phase, kr, own_w, other_w):
    count, total, lanes = lines.shape
    cin = lanes // 3
    low = (1 - phase) * cin
    weight = jnp.concatenate(
        [ref[kr, :, 1 - phase].reshape(2 * cin, ref.shape[-1]) for ref in (own_w, other_w)], axis=1
    )
    out = jnp.dot(
        lines[:, :, low : low + 2 * cin].reshape(count * total, 2 * cin),
        weight,
        preferred_element_type=jnp.float32,
    )
    return out.reshape(count, total, weight.shape[-1])


def main_kernel(xs_ref, next_ref, next_edge_ref, own_w, other_w, u_ref, part_ref, xs_next_ref, stats_ref):
    rows, total, _ = xs_ref.shape
    width = total - EDGE
    cout = u_ref.shape[-1]
    spread_line(xs_next_ref.at[0], next_ref[0], next_edge_ref[0])
    column = lax.axis_index("fsdp")
    place = lax.axis_index("rows")
    first_here = place == 0
    last_here = place == lax.axis_size("rows") - 1
    sums = jnp.zeros((1, cout), jnp.float32)
    squares = jnp.zeros((1, cout), jnp.float32)
    for phase in range(2):
        dot = functools.partial(tap_dot, phase=phase, own_w=own_w, other_w=other_w)
        upper = dot(xs_ref[...], kr=1)
        lower = dot(xs_ref[...], kr=3)
        part_ref[phase] = upper[0]
        even = [upper[row + 1] + lower[row] for row in range(rows - 1)]
        even.append(lower[rows - 1] + dot(xs_next_ref[...], kr=1)[0])
        upper = dot(xs_ref[...], kr=2)
        lower = dot(xs_ref[1:], kr=0)
        odd = [upper[row] + lower[row] for row in range(rows - 1)]
        odd.append(upper[rows - 1] + dot(xs_next_ref[...], kr=0)[0])
        lines = []
        for row in range(rows):
            lines += [odd[row].astype(jnp.bfloat16), even[row].astype(jnp.bfloat16)]
        for row, line in enumerate(lines):
            u_ref[row, phase] = line
        edge_line = jnp.where(first_here, part_ref[phase].astype(jnp.bfloat16).astype(jnp.float32), 0.0)
        final_line = jnp.where(last_here, 0.0, lines[-1].astype(jnp.float32))
        for line in lines[:-1] + [edge_line, final_line]:
            values = line[:width].astype(jnp.float32)
            sums += jnp.sum(values, axis=0, keepdims=True)
            squares += jnp.sum(values * values, axis=0, keepdims=True)
    half = cout // 2
    halves = []
    for row in (sums, squares):
        own, other = row[:, :half], row[:, half:]
        halves += [jnp.where(column == 0, own, other), jnp.where(column == 0, other, own)]
    stats_ref[...] = jnp.concatenate(halves + [jnp.zeros((4, half), jnp.float32)], axis=0)


def halo_kernel(above_ref, below_ref, xs_ref, xs_next_ref, part_ref, own_w, other_w, u_ref, xs_above, xs_below):
    width = above_ref.shape[1] - EDGE
    for row in range(HALO):
        spread_line(xs_above.at[row], above_ref[row, :width], above_ref[row, width:])
    spread_line(xs_below.at[0], below_ref[0, :width], below_ref[0, width:])
    for phase in range(2):
        dot = functools.partial(tap_dot, phase=phase, own_w=own_w, other_w=other_w)
        outer = dot(xs_above[...], kr=3)
        u_ref[0, phase] = (outer[0] + dot(xs_above[1:2], kr=1)[0]).astype(jnp.bfloat16)
        u_ref[2, phase] = (outer[1] + part_ref[phase]).astype(jnp.bfloat16)
        u_ref[1, phase] = (dot(xs_above[1:2], kr=2)[0] + dot(xs_ref[0:1], kr=0)[0]).astype(jnp.bfloat16)
        u_ref[3, phase] = (dot(xs_next_ref[...], kr=2)[0] + dot(xs_below[...], kr=0)[0]).astype(jnp.bfloat16)


def group_sum(v, width):
    lane = lax.broadcasted_iota(jnp.int32, v.shape, 1)
    size = v.shape[1]
    step = 1
    while step < width:
        v = v + jnp.where(
            (lane & step) == 0, pltpu.roll(v, size - step, 1), pltpu.roll(v, step, 1)
        )
        step *= 2
    return v


def fill(ref, row, even, odd):
    total, channels = even.shape
    ref[row, :, 0:channels] = pltpu.roll(odd, 1, 0).astype(jnp.bfloat16)
    ref[row, :, channels : 2 * channels] = even.astype(jnp.bfloat16)
    ref[row, :, 2 * channels : 3 * channels] = odd.astype(jnp.bfloat16)
    ref[row, :, 3 * channels : 4 * channels] = pltpu.roll(even, total - 1, 0).astype(jnp.bfloat16)


def conv_kernel(
    count, u_ref, halo_ref, stats_ref, params_ref, own_w1, other_w1, own_w2, other_w2, out_ref, g, act, mixed
):
    main, _, total, cout = u_ref.shape
    lines = main + 2 * HALO
    width = total - EDGE
    half = own_w1.shape[-1]
    column = lax.axis_index("fsdp")
    own_at = pl.multiple_of(column * half, half)
    other_at = pl.multiple_of((1 - column) * half, half)

    def own_first(row):
        low, high = row[:, :half], row[:, half:]
        return jnp.concatenate([jnp.where(column == 0, low, high), jnp.where(column == 0, high, low)], axis=1)

    def kernel_row(a, own, other):
        return jnp.concatenate(
            [
                jnp.concatenate([ref[a, b, pl.ds(at, half), :] for b in range(3) for at in (own_at, other_at)], axis=0)
                for ref in (own, other)
            ],
            axis=1,
        )

    block = stats_ref[...]
    width_group = cout // NORM_GROUPS
    sums = jnp.concatenate([block[0:1], block[1:2]], axis=1)
    squares = jnp.concatenate([block[2:3], block[3:4]], axis=1)
    mean = group_sum(sums, width_group) / count
    spread = group_sum(squares, width_group) / count - mean * mean
    scale = lax.rsqrt(spread + 1e-05) * params_ref[0:1]
    shift = own_first(params_ref[1:2] - mean * scale)
    scale = own_first(scale)

    mask = edge_mask(width)
    place = lax.axis_index("rows")
    last = lax.axis_size("rows") - 1

    def inside(row, beyond):
        if row < beyond:
            return mask & (place > 0)
        if row >= lines - 2 * HALO + beyond:
            return mask & (place < last)
        return mask

    def hidden(row):
        if row < 3:
            source = halo_ref.at[row]
        elif row < 3 + main:
            source = u_ref.at[row - 3]
        else:
            source = halo_ref.at[3]
        seen = inside(row, HALO)
        fill(
            g,
            row,
            *[jnp.where(seen, silu(source[phase].astype(jnp.float32) * scale + shift), 0.0) for phase in range(2)],
        )

    def conv(source, start, size, cells, phase, own, other, bias):
        acc = bias
        for a in range(3):
            acc = acc + jnp.dot(
                source[start + a : start + a + size, 0:cells, phase * cout : (phase + 3) * cout].reshape(
                    size * cells, 3 * cout
                ),
                kernel_row(a, own, other),
                preferred_element_type=jnp.float32,
            )
        return acc.reshape(size, cells, cout)

    chunk = 2
    bias1 = own_first(params_ref[2:3])
    bias2 = own_first(params_ref[3:4])

    def first(start):
        results = [silu(conv(g, start, chunk, total, phase, own_w1, other_w1, bias1)) for phase in range(2)]
        for row in range(chunk):
            seen = inside(start + row, 1)
            fill(act, start + row, *[jnp.where(seen, r[row], 0.0) for r in results])

    def second(start):
        for phase in range(2):
            acc = conv(act, start, chunk, width, phase, own_w2, other_w2, bias2)
            for row in range(chunk):
                for side in range(2):
                    mixed[side, start + row, pl.ds(phase, width, stride=2), :] = acc[
                        row, :, side * half : (side + 1) * half
                    ]
        for row in range(start, start + chunk):
            out_ref[row, :, pl.ds(own_at, half)] = mixed[0, row].astype(jnp.bfloat16)
            out_ref[row, :, pl.ds(other_at, half)] = mixed[1, row].astype(jnp.bfloat16)

    for row in range(chunk):
        hidden(row)
    for start in range(0, lines - 2, chunk):
        for row in range(start + chunk, start + 2 * chunk):
            hidden(row)
        first(start)
        if start >= chunk:
            second(start - chunk)


def total_over(block, axis, done=1):
    size = lax.axis_size(axis)
    if size & (size - 1):
        return lax.psum(block, axis)
    step = 1
    if (size.bit_length() - 1) % 2:
        block = block + lax.ppermute(block, axis, [(i, i ^ 1) for i in range(size)])
        step = 2
    while step < size:
        block = block + sum(
            lax.ppermute(block, axis, [(i, i ^ (step * d)) for i in range(size)]) for d in (1, 2, 3)
        )
        step *= 4
    return block


def after(value, *others):
    return lax.optimization_barrier((value, *others))[0]


def local(image, deconv_weight, norm_gain, norm_shift, first_weight, first_bias, second_weight, second_bias):
    rows, width, cin = image.shape
    taps, _, _, lanes = deconv_weight.shape
    columns = lax.axis_size("fsdp")
    cout = lanes * columns
    assert columns == 2 and rows == HALO and width % EDGE == 0 and lanes == LANES
    n_rows = lax.axis_size("rows")
    count = float(2 * rows * n_rows * 2 * width * columns * (cout // NORM_GROUPS))
    swap = [(0, 1), (1, 0)]
    to_next = [(i, i + 1) for i in range(n_rows - 1)]
    to_previous = [(i + 1, i) for i in range(n_rows - 1)]
    to_previous_swapped = [(2 * i + 2 + k, 2 * i + 1 - k) for i in range(n_rows - 1) for k in range(2)]
    total = width + EDGE
    hbm = pl.BlockSpec(memory_space=pltpu.HBM)
    vmem = pl.BlockSpec(memory_space=pltpu.VMEM)
    bf16, f32 = jnp.bfloat16, jnp.float32

    def call(kernel, ins, outs, scratch, name, flops=0):
        return pl.pallas_call(
            kernel,
            out_shape=tuple(jax.ShapeDtypeStruct(*o) for o in outs),
            in_specs=ins,
            out_specs=(vmem,) * len(outs),
            scratch_shapes=scratch,
            compiler_params=pltpu.CompilerParams(vmem_limit_bytes=VMEM_BYTES),
            cost_estimate=pl.CostEstimate(flops=flops, bytes_accessed=2**21, transcendentals=0),
            name=name,
        )

    in_hbm = functools.partial(pltpu.with_memory_space_constraint, memory_space=pltpu.HBM)
    line, edges = call(
        cut_kernel,
        [hbm],
        [((1, width, cin), bf16), ((rows, EDGE, cin), bf16)],
        [pltpu.SemaphoreType.DMA((2,))],
        "cut",
    )(in_hbm(image))
    following = lax.ppermute(line, "rows", to_previous)
    following_edge = lax.ppermute(edges[:1], ("rows", "fsdp"), to_previous_swapped)
    edge = lax.ppermute(edges, "fsdp", swap)
    shape_w = (taps, taps // 2, 2, cin, lanes)
    other_w = lax.ppermute(deconv_weight, "fsdp", swap).reshape(shape_w)

    first_other = lax.ppermute(after(first_weight, edge), "fsdp", swap)
    second_other = lax.ppermute(after(second_weight, edge), "fsdp", swap)
    xs, lines, own_w = call(
        own_kernel,
        [hbm, vmem, hbm],
        [((rows, total, 3 * cin), bf16), ((rows, total, cin), bf16), (shape_w, bf16)],
        [pltpu.VMEM(image.shape, bf16), pltpu.SemaphoreType.DMA((2,))],
        "own_lines",
    )(in_hbm(image), edge, in_hbm(deconv_weight.reshape(shape_w)))
    u, part, xs_next, stats = call(
        main_kernel,
        [vmem] * 5,
        [((2 * rows, 2, total, cout), bf16), ((2, total, cout), f32), ((1, total, 3 * cin), bf16), ((8, cout // 2), f32)],
        [],
        "deconv_main",
        flops=2 * 2 * (2 * rows) * total * 4 * cin * cout,
    )(xs, following, following_edge, own_w, other_w)

    lines = after(lines, stats)
    stats = stats + lax.ppermute(stats, "fsdp", swap)
    above = lax.ppermute(lines, "rows", to_next)
    below = lax.ppermute(lines[1:], "rows", to_previous)
    (halo,) = call(
        halo_kernel,
        [vmem] * 7,
        [((4, 2, total, cout), bf16)],
        [pltpu.VMEM((HALO, total, 3 * cin), bf16), pltpu.VMEM((1, total, 3 * cin), bf16)],
        "deconv_halo",
        flops=2 * 2 * 4 * total * 4 * cin * cout,
    )(above, below, xs, xs_next, part, own_w, other_w)

    totals = total_over(stats, "rows")
    params = jnp.stack([norm_gain, norm_shift, first_bias, second_bias])
    (out,) = call(
        functools.partial(conv_kernel, count),
        [vmem] * 8,
        [((2 * rows, 2 * width, cout), bf16)],
        [
            pltpu.VMEM((2 * rows + 2 * HALO, total, 4 * cout), bf16),
            pltpu.VMEM((2 * rows + 2, total, 4 * cout), bf16),
            pltpu.VMEM((2, 2 * rows, 2 * width, lanes), f32),
        ],
        "convs",
        flops=5 * 10**9,
    )(u, halo, totals, params, first_weight, first_other, second_weight, second_other)
    return out


def solution(mesh):
    placed = (
        P(("groups", "rows"), "fsdp", None),
        P(None, None, None, "fsdp"),
        P(),
        P(),
        P(None, None, None, "fsdp"),
        P(),
        P(None, None, None, "fsdp"),
        P(),
    )
    return jax.shard_map(
        local,
        mesh=mesh,
        in_specs=placed,
        out_specs=P(("groups", "rows"), "fsdp", None),
        check_vma=False,
    )
```

```python
import functools

import jax
import jax.numpy as jnp
from jax import lax
from jax.experimental import pallas as pl
from jax.experimental.pallas import tpu as pltpu
from jax.sharding import PartitionSpec as P

NORM_GROUPS = 32
HALO = 2
EDGE = 16
LANES = 128
VMEM_BYTES = 24 * 2**20


def silu(v):
    h = 0.5 * v
    return h + h * jnp.tanh(h)


def edge_mask(width):
    column = lax.axis_index("fsdp")
    last = lax.axis_size("fsdp") - 1
    cell = lax.broadcasted_iota(jnp.int32, (width + EDGE, 1), 0) - width
    right = (cell < EDGE // 2) & (column < last)
    left = (cell >= EDGE // 2) & (column > 0)
    return (cell < 0) | right | left


def cut_kernel(image_ref, near_ref, edges_ref, sems):
    width = image_ref.shape[1]
    start = pl.multiple_of((1 - lax.axis_index("fsdp")) * (width - EDGE), EDGE)
    copies = [
        pltpu.make_async_copy(image_ref.at[:, pl.ds(start, EDGE), :], edges_ref, sems.at[0]),
        pltpu.make_async_copy(image_ref, near_ref, sems.at[1]),
    ]
    for copy in copies:
        copy.start()
    for copy in copies:
        copy.wait()


def near_kernel(weight_ref, near_ref, sem):
    copy = pltpu.make_async_copy(weight_ref, near_ref, sem)
    copy.start()
    copy.wait()


def spread_line(out, line):
    total, cin = line.shape
    line = jnp.where(edge_mask(total - EDGE), line.astype(jnp.float32), 0.0)
    out[:, 0:cin] = pltpu.roll(line, total - 1, 0).astype(jnp.bfloat16)
    out[:, cin : 2 * cin] = line.astype(jnp.bfloat16)
    out[:, 2 * cin : 3 * cin] = pltpu.roll(line, 1, 0).astype(jnp.bfloat16)


def own_kernel(lines_ref, xs_ref):
    for row in range(lines_ref.shape[0]):
        spread_line(xs_ref.at[row], lines_ref[row])


def tap_dot(lines, phase, kr, own_w, other_w):
    count, total, lanes = lines.shape
    cin = lanes // 3
    low = (1 - phase) * cin
    weight = jnp.concatenate(
        [ref[kr, :, 1 - phase].reshape(2 * cin, ref.shape[-1]) for ref in (own_w, other_w)], axis=1
    )
    out = jnp.dot(
        lines[:, :, low : low + 2 * cin].reshape(count * total, 2 * cin),
        weight,
        preferred_element_type=jnp.float32,
    )
    return out.reshape(count, total, weight.shape[-1])


def main_kernel(xs_ref, next_ref, own_w, other_w, u_ref, part_ref, xs_next_ref, stats_ref):
    rows, total, _ = xs_ref.shape
    width = total - EDGE
    cout = u_ref.shape[-1]
    spread_line(xs_next_ref.at[0], next_ref[0])
    column = lax.axis_index("fsdp")
    place = lax.axis_index("rows")
    first_here = place == 0
    last_here = place == lax.axis_size("rows") - 1
    sums = jnp.zeros((1, cout), jnp.float32)
    squares = jnp.zeros((1, cout), jnp.float32)
    for phase in range(2):
        dot = functools.partial(tap_dot, phase=phase, own_w=own_w, other_w=other_w)
        upper = dot(xs_ref[...], kr=1)
        lower = dot(xs_ref[...], kr=3)
        part_ref[phase] = upper[0]
        even = [upper[row + 1] + lower[row] for row in range(rows - 1)]
        even.append(lower[rows - 1] + dot(xs_next_ref[...], kr=1)[0])
        upper = dot(xs_ref[...], kr=2)
        lower = dot(xs_ref[1:], kr=0)
        odd = [upper[row] + lower[row] for row in range(rows - 1)]
        odd.append(upper[rows - 1] + dot(xs_next_ref[...], kr=0)[0])
        lines = []
        for row in range(rows):
            lines += [odd[row].astype(jnp.bfloat16), even[row].astype(jnp.bfloat16)]
        for row, line in enumerate(lines):
            u_ref[row, phase] = line
        edge_line = jnp.where(first_here, part_ref[phase].astype(jnp.bfloat16).astype(jnp.float32), 0.0)
        final_line = jnp.where(last_here, 0.0, lines[-1].astype(jnp.float32))
        for line in lines[:-1] + [edge_line, final_line]:
            values = line[:width].astype(jnp.float32)
            sums += jnp.sum(values, axis=0, keepdims=True)
            squares += jnp.sum(values * values, axis=0, keepdims=True)
    half = cout // 2
    halves = []
    for row in (sums, squares):
        own, other = row[:, :half], row[:, half:]
        halves += [jnp.where(column == 0, own, other), jnp.where(column == 0, other, own)]
    stats_ref[...] = jnp.concatenate(halves + [jnp.zeros((4, half), jnp.float32)], axis=0)


def halo_kernel(above_ref, below_ref, xs_ref, xs_next_ref, part_ref, own_w, other_w, u_ref, xs_above, xs_below):
    for row in range(HALO):
        spread_line(xs_above.at[row], above_ref[row])
    spread_line(xs_below.at[0], below_ref[0])
    for phase in range(2):
        dot = functools.partial(tap_dot, phase=phase, own_w=own_w, other_w=other_w)
        outer = dot(xs_above[...], kr=3)
        u_ref[0, phase] = (outer[0] + dot(xs_above[1:2], kr=1)[0]).astype(jnp.bfloat16)
        u_ref[2, phase] = (outer[1] + part_ref[phase]).astype(jnp.bfloat16)
        u_ref[1, phase] = (dot(xs_above[1:2], kr=2)[0] + dot(xs_ref[0:1], kr=0)[0]).astype(jnp.bfloat16)
        u_ref[3, phase] = (dot(xs_next_ref[...], kr=2)[0] + dot(xs_below[...], kr=0)[0]).astype(jnp.bfloat16)


def group_sum(v, width):
    lane = lax.broadcasted_iota(jnp.int32, v.shape, 1)
    size = v.shape[1]
    step = 1
    while step < width:
        v = v + jnp.where(
            (lane & step) == 0, pltpu.roll(v, size - step, 1), pltpu.roll(v, step, 1)
        )
        step *= 2
    return v


def fill(ref, row, even, odd):
    total, channels = even.shape
    ref[row, :, 0:channels] = pltpu.roll(odd, 1, 0).astype(jnp.bfloat16)
    ref[row, :, channels : 2 * channels] = even.astype(jnp.bfloat16)
    ref[row, :, 2 * channels : 3 * channels] = odd.astype(jnp.bfloat16)
    ref[row, :, 3 * channels : 4 * channels] = pltpu.roll(even, total - 1, 0).astype(jnp.bfloat16)


def conv_kernel(
    count, u_ref, halo_ref, stats_ref, params_ref, own_w1, other_w1, own_w2, other_w2, out_ref, g, act, mixed
):
    main, _, total, cout = u_ref.shape
    lines = main + 2 * HALO
    width = total - EDGE
    half = own_w1.shape[-1]
    column = lax.axis_index("fsdp")
    own_at = pl.multiple_of(column * half, half)
    other_at = pl.multiple_of((1 - column) * half, half)

    def own_first(row):
        low, high = row[:, :half], row[:, half:]
        return jnp.concatenate([jnp.where(column == 0, low, high), jnp.where(column == 0, high, low)], axis=1)

    def kernel_row(a, own, other):
        return jnp.concatenate(
            [
                jnp.concatenate([ref[a, b, pl.ds(at, half), :] for b in range(3) for at in (own_at, other_at)], axis=0)
                for ref in (own, other)
            ],
            axis=1,
        )

    block = stats_ref[...]
    width_group = cout // NORM_GROUPS
    sums = jnp.concatenate([block[0:1], block[1:2]], axis=1)
    squares = jnp.concatenate([block[2:3], block[3:4]], axis=1)
    mean = group_sum(sums, width_group) / count
    spread = group_sum(squares, width_group) / count - mean * mean
    scale = lax.rsqrt(spread + 1e-05) * params_ref[0:1]
    shift = own_first(params_ref[1:2] - mean * scale)
    scale = own_first(scale)

    mask = edge_mask(width)
    place = lax.axis_index("rows")
    last = lax.axis_size("rows") - 1

    def inside(row, beyond):
        if row < beyond:
            return mask & (place > 0)
        if row >= lines - 2 * HALO + beyond:
            return mask & (place < last)
        return mask

    def hidden(row):
        if row < 3:
            source = halo_ref.at[row]
        elif row < 3 + main:
            source = u_ref.at[row - 3]
        else:
            source = halo_ref.at[3]
        seen = inside(row, HALO)
        fill(
            g,
            row,
            *[jnp.where(seen, silu(source[phase].astype(jnp.float32) * scale + shift), 0.0) for phase in range(2)],
        )

    def conv(source, start, size, cells, phase, own, other, bias):
        acc = bias
        for a in range(3):
            acc = acc + jnp.dot(
                source[start + a : start + a + size, 0:cells, phase * cout : (phase + 3) * cout].reshape(
                    size * cells, 3 * cout
                ),
                kernel_row(a, own, other),
                preferred_element_type=jnp.float32,
            )
        return acc.reshape(size, cells, cout)

    chunk = 2
    bias1 = own_first(params_ref[2:3])
    bias2 = own_first(params_ref[3:4])

    def first(start):
        results = [silu(conv(g, start, chunk, total, phase, own_w1, other_w1, bias1)) for phase in range(2)]
        for row in range(chunk):
            seen = inside(start + row, 1)
            fill(act, start + row, *[jnp.where(seen, r[row], 0.0) for r in results])

    def second(start):
        for phase in range(2):
            acc = conv(act, start, chunk, width, phase, own_w2, other_w2, bias2)
            for row in range(chunk):
                for side in range(2):
                    mixed[side, start + row, pl.ds(phase, width, stride=2), :] = acc[
                        row, :, side * half : (side + 1) * half
                    ]
        for row in range(start, start + chunk):
            out_ref[row, :, pl.ds(own_at, half)] = mixed[0, row].astype(jnp.bfloat16)
            out_ref[row, :, pl.ds(other_at, half)] = mixed[1, row].astype(jnp.bfloat16)

    for row in range(chunk):
        hidden(row)
    for start in range(0, lines - 2, chunk):
        for row in range(start + chunk, start + 2 * chunk):
            hidden(row)
        first(start)
        if start >= chunk:
            second(start - chunk)


def total_over(block, axis):
    size = lax.axis_size(axis)
    if size & (size - 1):
        return lax.psum(block, axis)
    step = 1
    while step < size:
        block = block + lax.ppermute(block, axis, [(i, i ^ step) for i in range(size)])
        step *= 2
    return block


def after(value, *others):
    return lax.optimization_barrier((value, *others))[0]


def local(image, deconv_weight, norm_gain, norm_shift, first_weight, first_bias, second_weight, second_bias):
    rows, width, cin = image.shape
    taps, _, _, lanes = deconv_weight.shape
    columns = lax.axis_size("fsdp")
    cout = lanes * columns
    assert columns == 2 and rows == HALO and width % EDGE == 0 and lanes == LANES
    n_rows = lax.axis_size("rows")
    count = float(2 * rows * n_rows * 2 * width * columns * (cout // NORM_GROUPS))
    swap = [(0, 1), (1, 0)]
    to_next = [(i, i + 1) for i in range(n_rows - 1)]
    to_previous = [(i + 1, i) for i in range(n_rows - 1)]
    total = width + EDGE
    hbm = pl.BlockSpec(memory_space=pltpu.HBM)
    vmem = pl.BlockSpec(memory_space=pltpu.VMEM)
    bf16, f32 = jnp.bfloat16, jnp.float32

    def call(kernel, ins, outs, scratch, name, flops=0):
        return pl.pallas_call(
            kernel,
            out_shape=tuple(jax.ShapeDtypeStruct(*o) for o in outs),
            in_specs=ins,
            out_specs=(vmem,) * len(outs),
            scratch_shapes=scratch,
            compiler_params=pltpu.CompilerParams(vmem_limit_bytes=VMEM_BYTES),
            cost_estimate=pl.CostEstimate(flops=flops, bytes_accessed=2**21, transcendentals=0),
            name=name,
        )

    in_hbm = functools.partial(pltpu.with_memory_space_constraint, memory_space=pltpu.HBM)
    shape_w = (taps, taps // 2, 2, cin, lanes)
    other_w = lax.ppermute(deconv_weight, "fsdp", swap).reshape(shape_w)
    first_other = lax.ppermute(first_weight, "fsdp", swap)
    second_other = lax.ppermute(second_weight, "fsdp", swap)
    near, edges = call(
        cut_kernel,
        [hbm],
        [(image.shape, bf16), ((rows, EDGE, cin), bf16)],
        [pltpu.SemaphoreType.DMA((2,))],
        "cut",
    )(in_hbm(image))
    edge = lax.ppermute(edges, "fsdp", swap)
    (own_w,) = call(near_kernel, [hbm], [(shape_w, bf16)], [pltpu.SemaphoreType.DMA(())], "near_weights")(
        in_hbm(after(deconv_weight, edges).reshape(shape_w))
    )
    lines = jnp.concatenate([near, edge], axis=1)
    following = lax.ppermute(lines[:1], "rows", to_previous)
    above = lax.ppermute(lines, "rows", to_next)
    below = lax.ppermute(lines[1:], "rows", to_previous)
    (xs,) = call(own_kernel, [vmem], [((rows, total, 3 * cin), bf16)], [], "own_lines")(lines)
    u, part, xs_next, stats = call(
        main_kernel,
        [vmem] * 4,
        [((2 * rows, 2, total, cout), bf16), ((2, total, cout), f32), ((1, total, 3 * cin), bf16), ((8, cout // 2), f32)],
        [],
        "deconv_main",
        flops=2 * 2 * (2 * rows) * total * 4 * cin * cout,
    )(xs, following, own_w, other_w)

    (halo,) = call(
        halo_kernel,
        [vmem] * 7,
        [((4, 2, total, cout), bf16)],
        [pltpu.VMEM((HALO, total, 3 * cin), bf16), pltpu.VMEM((1, total, 3 * cin), bf16)],
        "deconv_halo",
        flops=2 * 2 * 4 * total * 4 * cin * cout,
    )(above, below, xs, xs_next, part, own_w, other_w)

    totals = total_over(total_over(stats, "fsdp"), "rows")
    params = jnp.stack([norm_gain, norm_shift, first_bias, second_bias])
    (out,) = call(
        functools.partial(conv_kernel, count),
        [vmem] * 8,
        [((2 * rows, 2 * width, cout), bf16)],
        [
            pltpu.VMEM((2 * rows + 2 * HALO, total, 4 * cout), bf16),
            pltpu.VMEM((2 * rows + 2, total, 4 * cout), bf16),
            pltpu.VMEM((2, 2 * rows, 2 * width, lanes), f32),
        ],
        "convs",
        flops=5 * 10**9,
    )(u, halo, totals, params, first_weight, first_other, second_weight, second_other)
    return out


def solution(mesh):
    placed = (
        P(("groups", "rows"), "fsdp", None),
        P(None, None, None, "fsdp"),
        P(),
        P(),
        P(None, None, None, "fsdp"),
        P(),
        P(None, None, None, "fsdp"),
        P(),
    )
    return jax.shard_map(
        local,
        mesh=mesh,
        in_specs=placed,
        out_specs=P(("groups", "rows"), "fsdp", None),
        check_vma=False,
    )
```

```python
import functools

import jax
import jax.numpy as jnp
from jax import lax
from jax.experimental import pallas as pl
from jax.experimental.pallas import tpu as pltpu
from jax.sharding import PartitionSpec as P

NORM_GROUPS = 32
HALO = 2
EDGE = 16
LANES = 128
VMEM_BYTES = 24 * 2**20


def silu(v):
    h = 0.5 * v
    return h + h * jnp.tanh(h)


def edge_mask(width):
    column = lax.axis_index("fsdp")
    last = lax.axis_size("fsdp") - 1
    cell = lax.broadcasted_iota(jnp.int32, (width + EDGE, 1), 0) - width
    right = (cell < EDGE // 2) & (column < last)
    left = (cell >= EDGE // 2) & (column > 0)
    return (cell < 0) | right | left


def cut_kernel(image_ref, near_ref, edges_ref, sems):
    width = image_ref.shape[1]
    start = pl.multiple_of((1 - lax.axis_index("fsdp")) * (width - EDGE), EDGE)
    copies = [
        pltpu.make_async_copy(image_ref.at[:, pl.ds(start, EDGE), :], edges_ref, sems.at[0]),
        pltpu.make_async_copy(image_ref, near_ref, sems.at[1]),
    ]
    for copy in copies:
        copy.start()
    for copy in copies:
        copy.wait()


def near_kernel(weight_ref, near_ref, sem):
    copy = pltpu.make_async_copy(weight_ref, near_ref, sem)
    copy.start()
    copy.wait()


def spread_line(out, main, edge):
    width, cin = main.shape
    line = jnp.concatenate([main.astype(jnp.float32), edge.astype(jnp.float32)], axis=0)
    line = jnp.where(edge_mask(width), line, 0.0)
    out[:, 0:cin] = pltpu.roll(line, width + EDGE - 1, 0).astype(jnp.bfloat16)
    out[:, cin : 2 * cin] = line.astype(jnp.bfloat16)
    out[:, 2 * cin : 3 * cin] = pltpu.roll(line, 1, 0).astype(jnp.bfloat16)


def tap_dot(lines, phase, kr, own_w, other_w):
    count, total, lanes = lines.shape
    cin = lanes // 3
    low = (1 - phase) * cin
    weight = jnp.concatenate(
        [ref[kr, :, 1 - phase].reshape(2 * cin, ref.shape[-1]) for ref in (own_w, other_w)], axis=1
    )
    out = jnp.dot(
        lines[:, :, low : low + 2 * cin].reshape(count * total, 2 * cin),
        weight,
        preferred_element_type=jnp.float32,
    )
    return out.reshape(count, total, weight.shape[-1])


def add_sums(line, width):
    values = line[:width].astype(jnp.float32)
    return jnp.concatenate(
        [jnp.sum(values, axis=0, keepdims=True), jnp.sum(values * values, axis=0, keepdims=True)], axis=0
    )


def own_kernel(lines_ref, own_w, other_w, xs_ref, u_ref, part_ref, tail_ref, sums_ref):
    rows, total, _ = lines_ref.shape
    width = total - EDGE
    for row in range(rows):
        spread_line(xs_ref.at[row], lines_ref[row, :width], lines_ref[row, width:])
    first_here = lax.axis_index("rows") == 0
    sums = jnp.zeros((2, u_ref.shape[-1]), jnp.float32)
    for phase in range(2):
        dot = functools.partial(tap_dot, phase=phase, own_w=own_w, other_w=other_w)
        upper = dot(xs_ref[...], kr=1)
        lower = dot(xs_ref[...], kr=3)
        part_ref[phase] = upper[0]
        tail_ref[phase, 1] = lower[rows - 1]
        even = [(upper[row + 1] + lower[row]).astype(jnp.bfloat16) for row in range(rows - 1)]
        upper = dot(xs_ref[...], kr=2)
        lower = dot(xs_ref[1:], kr=0)
        tail_ref[phase, 0] = upper[rows - 1]
        odd = [(upper[row] + lower[row]).astype(jnp.bfloat16) for row in range(rows - 1)]
        for row in range(rows - 1):
            u_ref[2 * row, phase] = odd[row]
            u_ref[2 * row + 1, phase] = even[row]
            sums += add_sums(odd[row], width) + add_sums(even[row], width)
        sums += jnp.where(first_here, add_sums(part_ref[phase].astype(jnp.bfloat16), width), 0.0)
    sums_ref[...] = sums


def next_kernel(next_ref, edge_ref, tail_ref, sums_ref, own_w, other_w, u_ref, xs_ref, stats_ref):
    width = next_ref.shape[1]
    spread_line(xs_ref.at[0], next_ref[0], edge_ref[0])
    last_here = lax.axis_index("rows") == lax.axis_size("rows") - 1
    column = lax.axis_index("fsdp")
    sums = sums_ref[...]
    for phase in range(2):
        dot = functools.partial(tap_dot, phase=phase, own_w=own_w, other_w=other_w)
        odd = (tail_ref[phase, 0] + dot(xs_ref[...], kr=0)[0]).astype(jnp.bfloat16)
        even = (tail_ref[phase, 1] + dot(xs_ref[...], kr=1)[0]).astype(jnp.bfloat16)
        u_ref[0, phase] = odd
        u_ref[1, phase] = even
        sums += add_sums(odd, width) + jnp.where(last_here, 0.0, add_sums(even, width))
    half = sums.shape[1] // 2
    halves = []
    for row in range(2):
        own, other = sums[row : row + 1, :half], sums[row : row + 1, half:]
        halves += [jnp.where(column == 0, own, other), jnp.where(column == 0, other, own)]
    stats_ref[...] = jnp.concatenate(halves + [jnp.zeros((4, half), jnp.float32)], axis=0)


def halo_kernel(above_ref, next_ref, next_edge_ref, xs_ref, part_ref, own_w, other_w, u_ref, xs_above, xs_below):
    width = next_ref.shape[1]
    for row in range(HALO):
        spread_line(xs_above.at[row], above_ref[row, :width], above_ref[row, width:])
    for row in range(HALO):
        spread_line(xs_below.at[row], next_ref[row], next_edge_ref[row])
    for phase in range(2):
        dot = functools.partial(tap_dot, phase=phase, own_w=own_w, other_w=other_w)
        outer = dot(xs_above[...], kr=3)
        u_ref[0, phase] = (outer[0] + dot(xs_above[1:2], kr=1)[0]).astype(jnp.bfloat16)
        u_ref[2, phase] = (outer[1] + part_ref[phase]).astype(jnp.bfloat16)
        u_ref[1, phase] = (dot(xs_above[1:2], kr=2)[0] + dot(xs_ref[0:1], kr=0)[0]).astype(jnp.bfloat16)
        u_ref[3, phase] = (dot(xs_below[0:1], kr=2)[0] + dot(xs_below[1:2], kr=0)[0]).astype(jnp.bfloat16)


def group_sum(v, width):
    lane = lax.broadcasted_iota(jnp.int32, v.shape, 1)
    size = v.shape[1]
    step = 1
    while step < width:
        v = v + jnp.where(
            (lane & step) == 0, pltpu.roll(v, size - step, 1), pltpu.roll(v, step, 1)
        )
        step *= 2
    return v


def fill(ref, row, even, odd):
    total, channels = even.shape
    ref[row, :, 0:channels] = pltpu.roll(odd, 1, 0).astype(jnp.bfloat16)
    ref[row, :, channels : 2 * channels] = even.astype(jnp.bfloat16)
    ref[row, :, 2 * channels : 3 * channels] = odd.astype(jnp.bfloat16)
    ref[row, :, 3 * channels : 4 * channels] = pltpu.roll(even, total - 1, 0).astype(jnp.bfloat16)


def conv_kernel(
    count, u_ref, u_next_ref, halo_ref, stats_ref, params_ref, own_w1, other_w1, own_w2, other_w2, out_ref, g, act, mixed
):
    early, _, total, cout = u_ref.shape
    main = early + u_next_ref.shape[0]
    lines = main + 2 * HALO
    width = total - EDGE
    half = own_w1.shape[-1]
    column = lax.axis_index("fsdp")
    own_at = pl.multiple_of(column * half, half)
    other_at = pl.multiple_of((1 - column) * half, half)

    def own_first(row):
        low, high = row[:, :half], row[:, half:]
        return jnp.concatenate([jnp.where(column == 0, low, high), jnp.where(column == 0, high, low)], axis=1)

    def kernel_row(a, own, other):
        return jnp.concatenate(
            [
                jnp.concatenate([ref[a, b, pl.ds(at, half), :] for b in range(3) for at in (own_at, other_at)], axis=0)
                for ref in (own, other)
            ],
            axis=1,
        )

    block = stats_ref[...]
    width_group = cout // NORM_GROUPS
    sums = jnp.concatenate([block[0:1], block[1:2]], axis=1)
    squares = jnp.concatenate([block[2:3], block[3:4]], axis=1)
    mean = group_sum(sums, width_group) / count
    spread = group_sum(squares, width_group) / count - mean * mean
    scale = lax.rsqrt(spread + 1e-05) * params_ref[0:1]
    shift = own_first(params_ref[1:2] - mean * scale)
    scale = own_first(scale)

    mask = edge_mask(width)
    place = lax.axis_index("rows")
    last = lax.axis_size("rows") - 1

    def inside(row, beyond):
        if row < beyond:
            return mask & (place > 0)
        if row >= lines - 2 * HALO + beyond:
            return mask & (place < last)
        return mask

    def hidden(row):
        if row < 3:
            source = halo_ref.at[row]
        elif row < 3 + early:
            source = u_ref.at[row - 3]
        elif row < 3 + main:
            source = u_next_ref.at[row - 3 - early]
        else:
            source = halo_ref.at[3]
        seen = inside(row, HALO)
        fill(
            g,
            row,
            *[jnp.where(seen, silu(source[phase].astype(jnp.float32) * scale + shift), 0.0) for phase in range(2)],
        )

    def conv(source, start, size, cells, phase, own, other, bias):
        acc = bias
        for a in range(3):
            acc = acc + jnp.dot(
                source[start + a : start + a + size, 0:cells, phase * cout : (phase + 3) * cout].reshape(
                    size * cells, 3 * cout
                ),
                kernel_row(a, own, other),
                preferred_element_type=jnp.float32,
            )
        return acc.reshape(size, cells, cout)

    chunk = 2
    bias1 = own_first(params_ref[2:3])
    bias2 = own_first(params_ref[3:4])

    def first(start):
        results = [silu(conv(g, start, chunk, total, phase, own_w1, other_w1, bias1)) for phase in range(2)]
        for row in range(chunk):
            seen = inside(start + row, 1)
            fill(act, start + row, *[jnp.where(seen, r[row], 0.0) for r in results])

    def second(start):
        for phase in range(2):
            acc = conv(act, start, chunk, width, phase, own_w2, other_w2, bias2)
            for row in range(chunk):
                for side in range(2):
                    mixed[side, start + row, pl.ds(phase, width, stride=2), :] = acc[
                        row, :, side * half : (side + 1) * half
                    ]
        for row in range(start, start + chunk):
            out_ref[row, :, pl.ds(own_at, half)] = mixed[0, row].astype(jnp.bfloat16)
            out_ref[row, :, pl.ds(other_at, half)] = mixed[1, row].astype(jnp.bfloat16)

    for row in range(chunk):
        hidden(row)
    for start in range(0, lines - 2, chunk):
        for row in range(start + chunk, start + 2 * chunk):
            hidden(row)
        first(start)
        if start >= chunk:
            second(start - chunk)


def total_over(block, axis):
    size = lax.axis_size(axis)
    if size & (size - 1):
        return lax.psum(block, axis)
    steps = [2**n for n in range(size.bit_length() - 1)]
    for step in steps[1:] + steps[:1]:
        block = block + lax.ppermute(block, axis, [(i, i ^ step) for i in range(size)])
    return block


def after(value, *others):
    return lax.optimization_barrier((value, *others))[0]


def local(image, deconv_weight, norm_gain, norm_shift, first_weight, first_bias, second_weight, second_bias):
    rows, width, cin = image.shape
    taps, _, _, lanes = deconv_weight.shape
    columns = lax.axis_size("fsdp")
    cout = lanes * columns
    assert columns == 2 and rows == HALO and width % EDGE == 0 and lanes == LANES
    n_rows = lax.axis_size("rows")
    count = float(2 * rows * n_rows * 2 * width * columns * (cout // NORM_GROUPS))
    swap = [(0, 1), (1, 0)]
    to_next = [(i, i + 1) for i in range(n_rows - 1)]
    to_previous = [(i + 1, i) for i in range(n_rows - 1)]
    total = width + EDGE
    hbm = pl.BlockSpec(memory_space=pltpu.HBM)
    vmem = pl.BlockSpec(memory_space=pltpu.VMEM)
    bf16, f32 = jnp.bfloat16, jnp.float32

    def call(kernel, ins, outs, scratch, name, flops=0):
        return pl.pallas_call(
            kernel,
            out_shape=tuple(jax.ShapeDtypeStruct(*o) for o in outs),
            in_specs=ins,
            out_specs=(vmem,) * len(outs),
            scratch_shapes=scratch,
            compiler_params=pltpu.CompilerParams(vmem_limit_bytes=VMEM_BYTES),
            cost_estimate=pl.CostEstimate(flops=flops, bytes_accessed=2**21, transcendentals=0),
            name=name,
        )

    in_hbm = functools.partial(pltpu.with_memory_space_constraint, memory_space=pltpu.HBM)
    shape_w = (taps, taps // 2, 2, cin, lanes)
    at_left = lax.axis_index("fsdp") == 0
    following = lax.ppermute(image, "rows", to_previous)
    near, edges = call(
        cut_kernel,
        [hbm],
        [(image.shape, bf16), ((rows, EDGE, cin), bf16)],
        [pltpu.SemaphoreType.DMA((2,))],
        "cut",
    )(in_hbm(image))
    edge = lax.ppermute(edges, "fsdp", swap)
    other_w = lax.ppermute(deconv_weight, "fsdp", swap).reshape(shape_w)
    first_other = lax.ppermute(after(first_weight, edges), "fsdp", swap)
    second_other = lax.ppermute(after(second_weight, edges), "fsdp", swap)
    (own_w,) = call(near_kernel, [hbm], [(shape_w, bf16)], [pltpu.SemaphoreType.DMA(())], "near_weights")(
        in_hbm(after(deconv_weight, edges).reshape(shape_w))
    )
    lines = jnp.concatenate([after(near, own_w), edge], axis=1)
    u_line = (2, total, cout)
    xs, u, part, tail, sums = call(
        own_kernel,
        [vmem] * 3,
        [
            ((rows, total, 3 * cin), bf16),
            ((2 * rows - 2, *u_line), bf16),
            (u_line, f32),
            ((2, *u_line), f32),
            ((2, cout), f32),
        ],
        [],
        "deconv_own",
        flops=2 * 2 * (2 * rows - 1) * total * 4 * cin * cout,
    )(lines, own_w, other_w)
    above = lax.ppermute(after(lines, part), "rows", to_next)
    next_edge = lax.ppermute(
        jnp.where(at_left, following[:, width - EDGE :], following[:, :EDGE]), "fsdp", swap
    )
    u_next, xs_next, stats = call(
        next_kernel,
        [vmem] * 6,
        [((2, *u_line), bf16), ((1, total, 3 * cin), bf16), ((8, cout // 2), f32)],
        [],
        "deconv_next",
        flops=2 * 2 * total * 4 * cin * cout,
    )(following, next_edge, tail, sums, own_w, other_w)
    (halo,) = call(
        halo_kernel,
        [vmem] * 7,
        [((4, *u_line), bf16)],
        [pltpu.VMEM((HALO, total, 3 * cin), bf16), pltpu.VMEM((HALO, total, 3 * cin), bf16)],
        "deconv_halo",
        flops=2 * 2 * 4 * total * 4 * cin * cout,
    )(above, following, next_edge, xs, part, own_w, other_w)

    totals = total_over(total_over(stats, "fsdp"), "rows")
    params = jnp.stack([norm_gain, norm_shift, first_bias, second_bias])
    (out,) = call(
        functools.partial(conv_kernel, count),
        [vmem] * 9,
        [((2 * rows, 2 * width, cout), bf16)],
        [
            pltpu.VMEM((2 * rows + 2 * HALO, total, 4 * cout), bf16),
            pltpu.VMEM((2 * rows + 2, total, 4 * cout), bf16),
            pltpu.VMEM((2, 2 * rows, 2 * width, lanes), f32),
        ],
        "convs",
        flops=5 * 10**9,
    )(u, u_next, halo, totals, params, first_weight, first_other, second_weight, second_other)
    return out


def solution(mesh):
    placed = (
        P(("groups", "rows"), "fsdp", None),
        P(None, None, None, "fsdp"),
        P(),
        P(),
        P(None, None, None, "fsdp"),
        P(),
        P(None, None, None, "fsdp"),
        P(),
    )
    return jax.shard_map(
        local,
        mesh=mesh,
        in_specs=placed,
        out_specs=P(("groups", "rows"), "fsdp", None),
        check_vma=False,
    )
```

```python
import functools

import jax
import jax.numpy as jnp
from jax import lax
from jax.experimental import pallas as pl
from jax.experimental.pallas import tpu as pltpu
from jax.sharding import PartitionSpec as P

NORM_GROUPS = 32
HALO = 2
EDGE = 16
LANES = 128
VMEM_BYTES = 24 * 2**20


def silu(v):
    h = 0.5 * v
    return h + h * jnp.tanh(h)


def edge_mask(width):
    column = lax.axis_index("fsdp")
    last = lax.axis_size("fsdp") - 1
    cell = lax.broadcasted_iota(jnp.int32, (width + EDGE, 1), 0) - width
    right = (cell < EDGE // 2) & (column < last)
    left = (cell >= EDGE // 2) & (column > 0)
    return (cell < 0) | right | left


def cut_kernel(image_ref, near_ref, edges_ref, sems):
    width = image_ref.shape[1]
    start = pl.multiple_of((1 - lax.axis_index("fsdp")) * (width - EDGE), EDGE)
    copies = [
        pltpu.make_async_copy(image_ref.at[:, pl.ds(start, EDGE), :], edges_ref, sems.at[0]),
        pltpu.make_async_copy(image_ref, near_ref, sems.at[1]),
    ]
    for copy in copies:
        copy.start()
    for copy in copies:
        copy.wait()


def near_kernel(weight_ref, near_ref, sem):
    copy = pltpu.make_async_copy(weight_ref, near_ref, sem)
    copy.start()
    copy.wait()


def spread_line(out, main, edge):
    width, cin = main.shape
    line = jnp.concatenate([main.astype(jnp.float32), edge.astype(jnp.float32)], axis=0)
    line = jnp.where(edge_mask(width), line, 0.0)
    out[:, 0:cin] = pltpu.roll(line, width + EDGE - 1, 0).astype(jnp.bfloat16)
    out[:, cin : 2 * cin] = line.astype(jnp.bfloat16)
    out[:, 2 * cin : 3 * cin] = pltpu.roll(line, 1, 0).astype(jnp.bfloat16)


def tap_dot(lines, phase, kr, own_w, other_w):
    count, total, lanes = lines.shape
    cin = lanes // 3
    low = (1 - phase) * cin
    weight = jnp.concatenate(
        [ref[kr, :, 1 - phase].reshape(2 * cin, ref.shape[-1]) for ref in (own_w, other_w)], axis=1
    )
    out = jnp.dot(
        lines[:, :, low : low + 2 * cin].reshape(count * total, 2 * cin),
        weight,
        preferred_element_type=jnp.float32,
    )
    return out.reshape(count, total, weight.shape[-1])


def add_sums(line, width):
    values = line[:width].astype(jnp.float32)
    return jnp.concatenate(
        [jnp.sum(values, axis=0, keepdims=True), jnp.sum(values * values, axis=0, keepdims=True)], axis=0
    )


def own_kernel(lines_ref, own_w, other_w, xs_ref, u_ref, part_ref, tail_ref, sums_ref):
    rows, total, _ = lines_ref.shape
    width = total - EDGE
    for row in range(rows):
        spread_line(xs_ref.at[row], lines_ref[row, :width], lines_ref[row, width:])
    first_here = lax.axis_index("rows") == 0
    sums = jnp.zeros((2, u_ref.shape[-1]), jnp.float32)
    for phase in range(2):
        dot = functools.partial(tap_dot, phase=phase, own_w=own_w, other_w=other_w)
        upper = dot(xs_ref[...], kr=1)
        lower = dot(xs_ref[...], kr=3)
        part_ref[phase] = upper[0]
        tail_ref[phase, 1] = lower[rows - 1]
        even = [(upper[row + 1] + lower[row]).astype(jnp.bfloat16) for row in range(rows - 1)]
        upper = dot(xs_ref[...], kr=2)
        lower = dot(xs_ref[1:], kr=0)
        tail_ref[phase, 0] = upper[rows - 1]
        odd = [(upper[row] + lower[row]).astype(jnp.bfloat16) for row in range(rows - 1)]
        for row in range(rows - 1):
            u_ref[2 * row, phase] = odd[row]
            u_ref[2 * row + 1, phase] = even[row]
            sums += add_sums(odd[row], width) + add_sums(even[row], width)
        sums += jnp.where(first_here, add_sums(part_ref[phase].astype(jnp.bfloat16), width), 0.0)
    sums_ref[...] = sums


def next_kernel(next_ref, edge_ref, tail_ref, sums_ref, own_w, other_w, u_ref, stats_ref, xs_ref):
    width = next_ref.shape[1]
    spread_line(xs_ref.at[0], next_ref[0], edge_ref[0])
    last_here = lax.axis_index("rows") == lax.axis_size("rows") - 1
    column = lax.axis_index("fsdp")
    sums = sums_ref[...]
    for phase in range(2):
        dot = functools.partial(tap_dot, phase=phase, own_w=own_w, other_w=other_w)
        odd = (tail_ref[phase, 0] + dot(xs_ref[...], kr=0)[0]).astype(jnp.bfloat16)
        even = (tail_ref[phase, 1] + dot(xs_ref[...], kr=1)[0]).astype(jnp.bfloat16)
        u_ref[0, phase] = odd
        u_ref[1, phase] = even
        sums += add_sums(odd, width) + jnp.where(last_here, 0.0, add_sums(even, width))
    half = sums.shape[1] // 2
    halves = []
    for row in range(2):
        own, other = sums[row : row + 1, :half], sums[row : row + 1, half:]
        halves += [jnp.where(column == 0, own, other), jnp.where(column == 0, other, own)]
    stats_ref[...] = jnp.concatenate(halves + [jnp.zeros((4, half), jnp.float32)], axis=0)


def halo_kernel(above_ref, next_ref, next_edge_ref, xs_ref, part_ref, own_w, other_w, u_ref, xs_above, xs_below):
    width = next_ref.shape[1]
    for row in range(HALO):
        spread_line(xs_above.at[row], above_ref[row, :width], above_ref[row, width:])
    for row in range(HALO):
        spread_line(xs_below.at[row], next_ref[row], next_edge_ref[row])
    for phase in range(2):
        dot = functools.partial(tap_dot, phase=phase, own_w=own_w, other_w=other_w)
        outer = dot(xs_above[...], kr=3)
        u_ref[0, phase] = (outer[0] + dot(xs_above[1:2], kr=1)[0]).astype(jnp.bfloat16)
        u_ref[2, phase] = (outer[1] + part_ref[phase]).astype(jnp.bfloat16)
        u_ref[1, phase] = (dot(xs_above[1:2], kr=2)[0] + dot(xs_ref[0:1], kr=0)[0]).astype(jnp.bfloat16)
        u_ref[3, phase] = (dot(xs_below[0:1], kr=2)[0] + dot(xs_below[1:2], kr=0)[0]).astype(jnp.bfloat16)


def group_sum(v, width):
    lane = lax.broadcasted_iota(jnp.int32, v.shape, 1)
    size = v.shape[1]
    step = 1
    while step < width:
        v = v + jnp.where(
            (lane & step) == 0, pltpu.roll(v, size - step, 1), pltpu.roll(v, step, 1)
        )
        step *= 2
    return v


def fill(ref, row, even, odd):
    total, channels = even.shape
    ref[row, :, 0:channels] = pltpu.roll(odd, 1, 0).astype(jnp.bfloat16)
    ref[row, :, channels : 2 * channels] = even.astype(jnp.bfloat16)
    ref[row, :, 2 * channels : 3 * channels] = odd.astype(jnp.bfloat16)
    ref[row, :, 3 * channels : 4 * channels] = pltpu.roll(even, total - 1, 0).astype(jnp.bfloat16)


def conv_kernel(
    count, u_ref, u_next_ref, halo_ref, stats_ref, params_ref, own_w1, other_w1, own_w2, other_w2, out_ref, g, act, mixed
):
    early, _, total, cout = u_ref.shape
    main = early + u_next_ref.shape[0]
    lines = main + 2 * HALO
    width = total - EDGE
    half = own_w1.shape[-1]
    column = lax.axis_index("fsdp")
    own_at = pl.multiple_of(column * half, half)
    other_at = pl.multiple_of((1 - column) * half, half)

    def own_first(row):
        low, high = row[:, :half], row[:, half:]
        return jnp.concatenate([jnp.where(column == 0, low, high), jnp.where(column == 0, high, low)], axis=1)

    def kernel_row(a, own, other):
        return jnp.concatenate(
            [
                jnp.concatenate([ref[a, b, pl.ds(at, half), :] for b in range(3) for at in (own_at, other_at)], axis=0)
                for ref in (own, other)
            ],
            axis=1,
        )

    block = jnp.sum(stats_ref[...], axis=0)
    width_group = cout // NORM_GROUPS
    sums = jnp.concatenate([block[0:1], block[1:2]], axis=1)
    squares = jnp.concatenate([block[2:3], block[3:4]], axis=1)
    mean = group_sum(sums, width_group) / count
    spread = group_sum(squares, width_group) / count - mean * mean
    scale = lax.rsqrt(spread + 1e-05) * params_ref[0:1]
    shift = own_first(params_ref[1:2] - mean * scale)
    scale = own_first(scale)

    mask = edge_mask(width)
    place = lax.axis_index("rows")
    last = lax.axis_size("rows") - 1

    def inside(row, beyond):
        if row < beyond:
            return mask & (place > 0)
        if row >= lines - 2 * HALO + beyond:
            return mask & (place < last)
        return mask

    def hidden(row):
        if row < 3:
            source = halo_ref.at[row]
        elif row < 3 + early:
            source = u_ref.at[row - 3]
        elif row < 3 + main:
            source = u_next_ref.at[row - 3 - early]
        else:
            source = halo_ref.at[3]
        seen = inside(row, HALO)
        fill(
            g,
            row,
            *[jnp.where(seen, silu(source[phase].astype(jnp.float32) * scale + shift), 0.0) for phase in range(2)],
        )

    def conv(source, start, size, cells, phase, own, other, bias):
        acc = bias
        for a in range(3):
            acc = acc + jnp.dot(
                source[start + a : start + a + size, 0:cells, phase * cout : (phase + 3) * cout].reshape(
                    size * cells, 3 * cout
                ),
                kernel_row(a, own, other),
                preferred_element_type=jnp.float32,
            )
        return acc.reshape(size, cells, cout)

    chunk = 2
    bias1 = own_first(params_ref[2:3])
    bias2 = own_first(params_ref[3:4])

    def first(start):
        results = [silu(conv(g, start, chunk, total, phase, own_w1, other_w1, bias1)) for phase in range(2)]
        for row in range(chunk):
            seen = inside(start + row, 1)
            fill(act, start + row, *[jnp.where(seen, r[row], 0.0) for r in results])

    def second(start):
        for phase in range(2):
            acc = conv(act, start, chunk, width, phase, own_w2, other_w2, bias2)
            for row in range(chunk):
                for side in range(2):
                    mixed[side, start + row, pl.ds(phase, width, stride=2), :] = acc[
                        row, :, side * half : (side + 1) * half
                    ]
        for row in range(start, start + chunk):
            out_ref[row, :, pl.ds(own_at, half)] = mixed[0, row].astype(jnp.bfloat16)
            out_ref[row, :, pl.ds(other_at, half)] = mixed[1, row].astype(jnp.bfloat16)

    for row in range(chunk):
        hidden(row)
    for start in range(0, lines - 2, chunk):
        for row in range(start + chunk, start + 2 * chunk):
            hidden(row)
        first(start)
        if start >= chunk:
            second(start - chunk)


def after(value, *others):
    return lax.optimization_barrier((value, *others))[0]


def local(image, deconv_weight, norm_gain, norm_shift, first_weight, first_bias, second_weight, second_bias):
    rows, width, cin = image.shape
    taps, _, _, lanes = deconv_weight.shape
    columns = lax.axis_size("fsdp")
    cout = lanes * columns
    assert columns == 2 and rows == HALO and width % EDGE == 0 and lanes == LANES
    n_rows = lax.axis_size("rows")
    count = float(2 * rows * n_rows * 2 * width * columns * (cout // NORM_GROUPS))
    swap = [(0, 1), (1, 0)]
    to_next = [(i, i + 1) for i in range(n_rows - 1)]
    to_previous = [(i + 1, i) for i in range(n_rows - 1)]
    total = width + EDGE
    hbm = pl.BlockSpec(memory_space=pltpu.HBM)
    vmem = pl.BlockSpec(memory_space=pltpu.VMEM)
    bf16, f32 = jnp.bfloat16, jnp.float32

    def call(kernel, ins, outs, scratch, name, flops=0):
        return pl.pallas_call(
            kernel,
            out_shape=tuple(jax.ShapeDtypeStruct(*o) for o in outs),
            in_specs=ins,
            out_specs=(vmem,) * len(outs),
            scratch_shapes=scratch,
            compiler_params=pltpu.CompilerParams(vmem_limit_bytes=VMEM_BYTES),
            cost_estimate=pl.CostEstimate(flops=flops, bytes_accessed=2**21, transcendentals=0),
            name=name,
        )

    in_hbm = functools.partial(pltpu.with_memory_space_constraint, memory_space=pltpu.HBM)
    in_vmem = functools.partial(pltpu.with_memory_space_constraint, memory_space=pltpu.VMEM)
    shape_w = (taps, taps // 2, 2, cin, lanes)
    at_left = lax.axis_index("fsdp") == 0
    following = lax.ppermute(image, "rows", to_previous)
    near, edges = call(
        cut_kernel,
        [hbm],
        [(image.shape, bf16), ((rows, EDGE, cin), bf16)],
        [pltpu.SemaphoreType.DMA((2,))],
        "cut",
    )(in_hbm(image))
    edge = lax.ppermute(edges, "fsdp", swap)
    other_w = lax.ppermute(deconv_weight, "fsdp", swap).reshape(shape_w)
    first_other = lax.ppermute(after(first_weight, edges), "fsdp", swap)
    second_other = lax.ppermute(after(second_weight, edges), "fsdp", swap)
    (own_w,) = call(near_kernel, [hbm], [(shape_w, bf16)], [pltpu.SemaphoreType.DMA(())], "near_weights")(
        in_hbm(after(deconv_weight, edges).reshape(shape_w))
    )
    lines = jnp.concatenate([after(near, own_w), edge], axis=1)
    u_line = (2, total, cout)
    xs, u, part, tail, sums = call(
        own_kernel,
        [vmem] * 3,
        [
            ((rows, total, 3 * cin), bf16),
            ((2 * rows - 2, *u_line), bf16),
            (u_line, f32),
            ((2, *u_line), f32),
            ((2, cout), f32),
        ],
        [],
        "deconv_own",
        flops=2 * 2 * (2 * rows - 1) * total * 4 * cin * cout,
    )(lines, own_w, in_vmem(other_w))
    above = lax.ppermute(after(lines, part), "rows", to_next)
    next_edge = lax.ppermute(
        jnp.where(at_left, following[:, width - EDGE :], following[:, :EDGE]), "fsdp", swap
    )
    u_next, stats = call(
        next_kernel,
        [vmem] * 6,
        [((2, *u_line), bf16), ((8, cout // 2), f32)],
        [pltpu.VMEM((1, total, 3 * cin), bf16)],
        "deconv_next",
        flops=2 * 2 * total * 4 * cin * cout,
    )(following, next_edge, tail, sums, own_w, in_vmem(other_w))
    (halo,) = call(
        halo_kernel,
        [vmem] * 7,
        [((4, *u_line), bf16)],
        [pltpu.VMEM((HALO, total, 3 * cin), bf16), pltpu.VMEM((HALO, total, 3 * cin), bf16)],
        "deconv_halo",
        flops=2 * 2 * 4 * total * 4 * cin * cout,
    )(above, following, next_edge, xs, part, own_w, in_vmem(other_w))

    stats = stats + lax.ppermute(stats, "fsdp", swap)
    stats = lax.all_to_all(jnp.broadcast_to(stats, (n_rows, *stats.shape)), "rows", split_axis=0, concat_axis=0)
    params = jnp.stack([norm_gain, norm_shift, first_bias, second_bias])
    (out,) = call(
        functools.partial(conv_kernel, count),
        [vmem] * 9,
        [((2 * rows, 2 * width, cout), bf16)],
        [
            pltpu.VMEM((2 * rows + 2 * HALO, total, 4 * cout), bf16),
            pltpu.VMEM((2 * rows + 2, total, 4 * cout), bf16),
            pltpu.VMEM((2, 2 * rows, 2 * width, lanes), f32),
        ],
        "convs",
        flops=5 * 10**9,
    )(u, u_next, halo, stats, params, first_weight, in_vmem(first_other), second_weight, in_vmem(second_other))
    return out


def solution(mesh):
    placed = (
        P(("groups", "rows"), "fsdp", None),
        P(None, None, None, "fsdp"),
        P(),
        P(),
        P(None, None, None, "fsdp"),
        P(),
        P(None, None, None, "fsdp"),
        P(),
    )
    return jax.shard_map(
        local,
        mesh=mesh,
        in_specs=placed,
        out_specs=P(("groups", "rows"), "fsdp", None),
        check_vma=False,
    )
```

```python
import functools

import jax
import jax.numpy as jnp
from jax import lax
from jax.experimental import pallas as pl
from jax.experimental.pallas import tpu as pltpu
from jax.sharding import PartitionSpec as P

NORM_GROUPS = 32
HALO = 2
EDGE = 16
LANES = 128
VMEM_BYTES = 24 * 2**20


def silu(v):
    h = 0.5 * v
    return h + h * jnp.tanh(h)


def edge_mask(width):
    column = lax.axis_index("fsdp")
    last = lax.axis_size("fsdp") - 1
    cell = lax.broadcasted_iota(jnp.int32, (width + EDGE, 1), 0) - width
    right = (cell < EDGE // 2) & (column < last)
    left = (cell >= EDGE // 2) & (column > 0)
    return (cell < 0) | right | left


def cut_kernel(image_ref, near_ref, edges_ref, sems):
    width = image_ref.shape[1]
    start = pl.multiple_of((1 - lax.axis_index("fsdp")) * (width - EDGE), EDGE)
    copies = [
        pltpu.make_async_copy(image_ref.at[:, pl.ds(start, EDGE), :], edges_ref, sems.at[0]),
        pltpu.make_async_copy(image_ref, near_ref, sems.at[1]),
    ]
    for copy in copies:
        copy.start()
    for copy in copies:
        copy.wait()


def near_kernel(weight_ref, near_ref, sem):
    copy = pltpu.make_async_copy(weight_ref, near_ref, sem)
    copy.start()
    copy.wait()


def spread_line(out, main, edge):
    width, cin = main.shape
    line = jnp.concatenate([main.astype(jnp.float32), edge.astype(jnp.float32)], axis=0)
    line = jnp.where(edge_mask(width), line, 0.0)
    out[:, 0:cin] = pltpu.roll(line, width + EDGE - 1, 0).astype(jnp.bfloat16)
    out[:, cin : 2 * cin] = line.astype(jnp.bfloat16)
    out[:, 2 * cin : 3 * cin] = pltpu.roll(line, 1, 0).astype(jnp.bfloat16)


def tap_dot(lines, phase, kr, own_w, other_w):
    count, total, lanes = lines.shape
    cin = lanes // 3
    low = (1 - phase) * cin
    weight = jnp.concatenate(
        [ref[kr, :, 1 - phase].reshape(2 * cin, ref.shape[-1]) for ref in (own_w, other_w)], axis=1
    )
    out = jnp.dot(
        lines[:, :, low : low + 2 * cin].reshape(count * total, 2 * cin),
        weight,
        preferred_element_type=jnp.float32,
    )
    return out.reshape(count, total, weight.shape[-1])


def add_sums(line, width):
    values = line[:width].astype(jnp.float32)
    return jnp.concatenate(
        [jnp.sum(values, axis=0, keepdims=True), jnp.sum(values * values, axis=0, keepdims=True)], axis=0
    )


def own_kernel(lines_ref, xs_ref):
    rows, total, _ = lines_ref.shape
    width = total - EDGE
    for row in range(rows):
        spread_line(xs_ref.at[row], lines_ref[row, :width], lines_ref[row, width:])


def main_kernel(xs_ref, next_ref, next_edge_ref, own_w, other_w, u_ref, part_ref, xs_next_ref, stats_ref):
    rows, total, _ = xs_ref.shape
    width = total - EDGE
    spread_line(xs_next_ref.at[0], next_ref[0], next_edge_ref[0])
    column = lax.axis_index("fsdp")
    place = lax.axis_index("rows")
    first_here = place == 0
    last_here = place == lax.axis_size("rows") - 1
    sums = jnp.zeros((2, u_ref.shape[-1]), jnp.float32)
    for phase in range(2):
        dot = functools.partial(tap_dot, phase=phase, own_w=own_w, other_w=other_w)
        upper = dot(xs_ref[...], kr=1)
        lower = dot(xs_ref[...], kr=3)
        part_ref[phase] = upper[0]
        even = [upper[row + 1] + lower[row] for row in range(rows - 1)]
        even.append(lower[rows - 1] + dot(xs_next_ref[...], kr=1)[0])
        upper = dot(xs_ref[...], kr=2)
        lower = dot(xs_ref[1:], kr=0)
        odd = [upper[row] + lower[row] for row in range(rows - 1)]
        odd.append(upper[rows - 1] + dot(xs_next_ref[...], kr=0)[0])
        for row in range(rows):
            odd[row], even[row] = odd[row].astype(jnp.bfloat16), even[row].astype(jnp.bfloat16)
            u_ref[2 * row, phase] = odd[row]
            u_ref[2 * row + 1, phase] = even[row]
            sums += add_sums(odd[row], width)
            if row < rows - 1:
                sums += add_sums(even[row], width)
        sums += jnp.where(last_here, 0.0, add_sums(even[rows - 1], width))
        sums += jnp.where(first_here, add_sums(part_ref[phase].astype(jnp.bfloat16), width), 0.0)
    half = sums.shape[1] // 2
    halves = []
    for row in range(2):
        own, other = sums[row : row + 1, :half], sums[row : row + 1, half:]
        halves += [jnp.where(column == 0, own, other), jnp.where(column == 0, other, own)]
    stats_ref[...] = jnp.concatenate(halves + [jnp.zeros((4, half), jnp.float32)], axis=0)


def halo_kernel(above_ref, next_ref, next_edge_ref, xs_ref, xs_next_ref, part_ref, own_w, other_w, u_ref, xs_above, xs_below):
    width = next_ref.shape[1]
    for row in range(HALO):
        spread_line(xs_above.at[row], above_ref[row, :width], above_ref[row, width:])
    spread_line(xs_below.at[0], next_ref[1], next_edge_ref[1])
    for phase in range(2):
        dot = functools.partial(tap_dot, phase=phase, own_w=own_w, other_w=other_w)
        outer = dot(xs_above[...], kr=3)
        u_ref[0, phase] = (outer[0] + dot(xs_above[1:2], kr=1)[0]).astype(jnp.bfloat16)
        u_ref[2, phase] = (outer[1] + part_ref[phase]).astype(jnp.bfloat16)
        u_ref[1, phase] = (dot(xs_above[1:2], kr=2)[0] + dot(xs_ref[0:1], kr=0)[0]).astype(jnp.bfloat16)
        u_ref[3, phase] = (dot(xs_next_ref[...], kr=2)[0] + dot(xs_below[...], kr=0)[0]).astype(jnp.bfloat16)


def group_sum(v, width):
    lane = lax.broadcasted_iota(jnp.int32, v.shape, 1)
    size = v.shape[1]
    step = 1
    while step < width:
        v = v + jnp.where(
            (lane & step) == 0, pltpu.roll(v, size - step, 1), pltpu.roll(v, step, 1)
        )
        step *= 2
    return v


def fill(ref, row, even, odd):
    total, channels = even.shape
    ref[row, :, 0:channels] = pltpu.roll(odd, 1, 0).astype(jnp.bfloat16)
    ref[row, :, channels : 2 * channels] = even.astype(jnp.bfloat16)
    ref[row, :, 2 * channels : 3 * channels] = odd.astype(jnp.bfloat16)
    ref[row, :, 3 * channels : 4 * channels] = pltpu.roll(even, total - 1, 0).astype(jnp.bfloat16)


def conv_kernel(
    count, u_ref, halo_ref, stats_ref, params_ref, own_w1, other_w1, own_w2, other_w2, out_ref, g, act, mixed
):
    main, _, total, cout = u_ref.shape
    lines = main + 2 * HALO
    width = total - EDGE
    half = own_w1.shape[-1]
    column = lax.axis_index("fsdp")
    own_at = pl.multiple_of(column * half, half)
    other_at = pl.multiple_of((1 - column) * half, half)

    def own_first(row):
        low, high = row[:, :half], row[:, half:]
        return jnp.concatenate([jnp.where(column == 0, low, high), jnp.where(column == 0, high, low)], axis=1)

    def kernel_row(a, own, other):
        return jnp.concatenate(
            [
                jnp.concatenate([ref[a, b, pl.ds(at, half), :] for b in range(3) for at in (own_at, other_at)], axis=0)
                for ref in (own, other)
            ],
            axis=1,
        )

    block = stats_ref[...]
    width_group = cout // NORM_GROUPS
    sums = jnp.concatenate([block[0:1], block[1:2]], axis=1)
    squares = jnp.concatenate([block[2:3], block[3:4]], axis=1)
    mean = group_sum(sums, width_group) / count
    spread = group_sum(squares, width_group) / count - mean * mean
    scale = lax.rsqrt(spread + 1e-05) * params_ref[0:1]
    shift = own_first(params_ref[1:2] - mean * scale)
    scale = own_first(scale)

    mask = edge_mask(width)
    place = lax.axis_index("rows")
    last = lax.axis_size("rows") - 1

    def inside(row, beyond):
        if row < beyond:
            return mask & (place > 0)
        if row >= lines - 2 * HALO + beyond:
            return mask & (place < last)
        return mask

    def hidden(row):
        if row < 3:
            source = halo_ref.at[row]
        elif row < 3 + main:
            source = u_ref.at[row - 3]
        else:
            source = halo_ref.at[3]
        seen = inside(row, HALO)
        fill(
            g,
            row,
            *[jnp.where(seen, silu(source[phase].astype(jnp.float32) * scale + shift), 0.0) for phase in range(2)],
        )

    def conv(source, start, size, cells, phase, own, other, bias):
        acc = bias
        for a in range(3):
            acc = acc + jnp.dot(
                source[start + a : start + a + size, 0:cells, phase * cout : (phase + 3) * cout].reshape(
                    size * cells, 3 * cout
                ),
                kernel_row(a, own, other),
                preferred_element_type=jnp.float32,
            )
        return acc.reshape(size, cells, cout)

    chunk = 2
    bias1 = own_first(params_ref[2:3])
    bias2 = own_first(params_ref[3:4])

    def first(start):
        results = [silu(conv(g, start, chunk, total, phase, own_w1, other_w1, bias1)) for phase in range(2)]
        for row in range(chunk):
            seen = inside(start + row, 1)
            fill(act, start + row, *[jnp.where(seen, r[row], 0.0) for r in results])

    def second(start):
        for phase in range(2):
            acc = conv(act, start, chunk, width, phase, own_w2, other_w2, bias2)
            for row in range(chunk):
                for side in range(2):
                    mixed[side, start + row, pl.ds(phase, width, stride=2), :] = acc[
                        row, :, side * half : (side + 1) * half
                    ]
        for row in range(start, start + chunk):
            out_ref[row, :, pl.ds(own_at, half)] = mixed[0, row].astype(jnp.bfloat16)
            out_ref[row, :, pl.ds(other_at, half)] = mixed[1, row].astype(jnp.bfloat16)

    for row in range(chunk):
        hidden(row)
    for start in range(0, lines - 2, chunk):
        for row in range(start + chunk, start + 2 * chunk):
            hidden(row)
        first(start)
        if start >= chunk:
            second(start - chunk)


def total_over(block, axis):
    size = lax.axis_size(axis)
    if size & (size - 1):
        return lax.psum(block, axis)
    steps = [2**n for n in range(size.bit_length() - 1)]
    for step in steps[1:] + steps[:1]:
        block = block + lax.ppermute(block, axis, [(i, i ^ step) for i in range(size)])
    return block


def after(value, *others):
    return lax.optimization_barrier((value, *others))[0]


def local(image, deconv_weight, norm_gain, norm_shift, first_weight, first_bias, second_weight, second_bias):
    rows, width, cin = image.shape
    taps, _, _, lanes = deconv_weight.shape
    columns = lax.axis_size("fsdp")
    cout = lanes * columns
    assert columns == 2 and rows == HALO and width % EDGE == 0 and lanes == LANES
    n_rows = lax.axis_size("rows")
    count = float(2 * rows * n_rows * 2 * width * columns * (cout // NORM_GROUPS))
    swap = [(0, 1), (1, 0)]
    to_next = [(i, i + 1) for i in range(n_rows - 1)]
    to_previous = [(i + 1, i) for i in range(n_rows - 1)]
    total = width + EDGE
    hbm = pl.BlockSpec(memory_space=pltpu.HBM)
    vmem = pl.BlockSpec(memory_space=pltpu.VMEM)
    bf16, f32 = jnp.bfloat16, jnp.float32

    def call(kernel, ins, outs, scratch, name, flops=0):
        return pl.pallas_call(
            kernel,
            out_shape=tuple(jax.ShapeDtypeStruct(*o) for o in outs),
            in_specs=ins,
            out_specs=(vmem,) * len(outs),
            scratch_shapes=scratch,
            compiler_params=pltpu.CompilerParams(vmem_limit_bytes=VMEM_BYTES),
            cost_estimate=pl.CostEstimate(flops=flops, bytes_accessed=2**21, transcendentals=0),
            name=name,
        )

    in_hbm = functools.partial(pltpu.with_memory_space_constraint, memory_space=pltpu.HBM)
    shape_w = (taps, taps // 2, 2, cin, lanes)
    at_left = lax.axis_index("fsdp") == 0
    following = lax.ppermute(image, "rows", to_previous)
    near, edges = call(
        cut_kernel,
        [hbm],
        [(image.shape, bf16), ((rows, EDGE, cin), bf16)],
        [pltpu.SemaphoreType.DMA((2,))],
        "cut",
    )(in_hbm(image))
    edge = lax.ppermute(edges, "fsdp", swap)
    other_w = lax.ppermute(deconv_weight, "fsdp", swap).reshape(shape_w)
    first_other = lax.ppermute(after(first_weight, edges), "fsdp", swap)
    second_other = lax.ppermute(after(second_weight, edges), "fsdp", swap)
    (own_w,) = call(near_kernel, [hbm], [(shape_w, bf16)], [pltpu.SemaphoreType.DMA(())], "near_weights")(
        in_hbm(after(deconv_weight, edges).reshape(shape_w))
    )
    lines = jnp.concatenate([after(near, own_w), edge], axis=1)
    above = lax.ppermute(lines, "rows", to_next)
    (xs,) = call(own_kernel, [vmem], [((rows, total, 3 * cin), bf16)], [], "own_lines")(lines)
    next_edge = lax.ppermute(
        jnp.where(at_left, following[:, width - EDGE :], following[:, :EDGE]), "fsdp", swap
    )
    u_line = (2, total, cout)
    u, part, xs_next, stats = call(
        main_kernel,
        [vmem] * 5,
        [((2 * rows, *u_line), bf16), (u_line, f32), ((1, total, 3 * cin), bf16), ((8, cout // 2), f32)],
        [],
        "deconv_main",
        flops=2 * 2 * (2 * rows) * total * 4 * cin * cout,
    )(xs, following, next_edge, own_w, other_w)
    (halo,) = call(
        halo_kernel,
        [vmem] * 8,
        [((4, *u_line), bf16)],
        [pltpu.VMEM((HALO, total, 3 * cin), bf16), pltpu.VMEM((1, total, 3 * cin), bf16)],
        "deconv_halo",
        flops=2 * 2 * 4 * total * 4 * cin * cout,
    )(above, following, next_edge, xs, xs_next, part, own_w, other_w)

    totals = total_over(total_over(stats, "fsdp"), "rows")
    params = jnp.stack([norm_gain, norm_shift, first_bias, second_bias])
    (out,) = call(
        functools.partial(conv_kernel, count),
        [vmem] * 8,
        [((2 * rows, 2 * width, cout), bf16)],
        [
            pltpu.VMEM((2 * rows + 2 * HALO, total, 4 * cout), bf16),
            pltpu.VMEM((2 * rows + 2, total, 4 * cout), bf16),
            pltpu.VMEM((2, 2 * rows, 2 * width, lanes), f32),
        ],
        "convs",
        flops=5 * 10**9,
    )(u, halo, totals, params, first_weight, first_other, second_weight, second_other)
    return out


def solution(mesh):
    placed = (
        P(("groups", "rows"), "fsdp", None),
        P(None, None, None, "fsdp"),
        P(),
        P(),
        P(None, None, None, "fsdp"),
        P(),
        P(None, None, None, "fsdp"),
        P(),
    )
    return jax.shard_map(
        local,
        mesh=mesh,
        in_specs=placed,
        out_specs=P(("groups", "rows"), "fsdp", None),
        check_vma=False,
    )
```

```python
import functools

import jax
import jax.numpy as jnp
from jax import lax
from jax.experimental import pallas as pl
from jax.experimental.pallas import tpu as pltpu
from jax.sharding import PartitionSpec as P

NORM_GROUPS = 32
HALO = 2
EDGE = 16
LANES = 128
VMEM_BYTES = 24 * 2**20


def silu(v):
    h = 0.5 * v
    return h + h * jnp.tanh(h)


def edge_mask(width):
    column = lax.axis_index("fsdp")
    last = lax.axis_size("fsdp") - 1
    cell = lax.broadcasted_iota(jnp.int32, (width + EDGE, 1), 0) - width
    right = (cell < EDGE // 2) & (column < last)
    left = (cell >= EDGE // 2) & (column > 0)
    return (cell < 0) | right | left


def cut_kernel(image_ref, near_ref, edges_ref, sems):
    width = image_ref.shape[1]
    start = pl.multiple_of((1 - lax.axis_index("fsdp")) * (width - EDGE), EDGE)
    copies = [
        pltpu.make_async_copy(image_ref.at[:, pl.ds(start, EDGE), :], edges_ref, sems.at[0]),
        pltpu.make_async_copy(image_ref, near_ref, sems.at[1]),
    ]
    for copy in copies:
        copy.start()
    for copy in copies:
        copy.wait()


def pick_kernel(lines_ref, edges_ref):
    width = lines_ref.shape[1]
    at_left = lax.axis_index("fsdp") == 0

    @pl.when(at_left)
    def _():
        edges_ref[...] = lines_ref[:, width - EDGE :]

    @pl.when(jnp.logical_not(at_left))
    def _():
        edges_ref[...] = lines_ref[:, :EDGE]


def near_kernel(weight_ref, near_ref, sem):
    copy = pltpu.make_async_copy(weight_ref, near_ref, sem)
    copy.start()
    copy.wait()


def spread_line(out, main, edge):
    width, cin = main.shape
    line = jnp.concatenate([main.astype(jnp.float32), edge.astype(jnp.float32)], axis=0)
    line = jnp.where(edge_mask(width), line, 0.0)
    out[:, 0:cin] = pltpu.roll(line, width + EDGE - 1, 0).astype(jnp.bfloat16)
    out[:, cin : 2 * cin] = line.astype(jnp.bfloat16)
    out[:, 2 * cin : 3 * cin] = pltpu.roll(line, 1, 0).astype(jnp.bfloat16)


def tap_dot(lines, phase, kr, own_w, other_w):
    count, total, lanes = lines.shape
    cin = lanes // 3
    low = (1 - phase) * cin
    weight = jnp.concatenate(
        [ref[kr, :, 1 - phase].reshape(2 * cin, ref.shape[-1]) for ref in (own_w, other_w)], axis=1
    )
    out = jnp.dot(
        lines[:, :, low : low + 2 * cin].reshape(count * total, 2 * cin),
        weight,
        preferred_element_type=jnp.float32,
    )
    return out.reshape(count, total, weight.shape[-1])


def add_sums(line, width):
    values = line[:width].astype(jnp.float32)
    return jnp.concatenate(
        [jnp.sum(values, axis=0, keepdims=True), jnp.sum(values * values, axis=0, keepdims=True)], axis=0
    )


def own_kernel(lines_ref, xs_ref):
    rows, total, _ = lines_ref.shape
    width = total - EDGE
    for row in range(rows):
        spread_line(xs_ref.at[row], lines_ref[row, :width], lines_ref[row, width:])


def main_kernel(xs_ref, next_ref, next_edge_ref, own_w, other_w, u_ref, part_ref, xs_next_ref, stats_ref):
    rows, total, _ = xs_ref.shape
    width = total - EDGE
    spread_line(xs_next_ref.at[0], next_ref[0], next_edge_ref[0])
    column = lax.axis_index("fsdp")
    place = lax.axis_index("rows")
    first_here = place == 0
    last_here = place == lax.axis_size("rows") - 1
    sums = jnp.zeros((2, u_ref.shape[-1]), jnp.float32)
    for phase in range(2):
        dot = functools.partial(tap_dot, phase=phase, own_w=own_w, other_w=other_w)
        upper = dot(xs_ref[...], kr=1)
        lower = dot(xs_ref[...], kr=3)
        part_ref[phase] = upper[0]
        even = [upper[row + 1] + lower[row] for row in range(rows - 1)]
        even.append(lower[rows - 1] + dot(xs_next_ref[...], kr=1)[0])
        upper = dot(xs_ref[...], kr=2)
        lower = dot(xs_ref[1:], kr=0)
        odd = [upper[row] + lower[row] for row in range(rows - 1)]
        odd.append(upper[rows - 1] + dot(xs_next_ref[...], kr=0)[0])
        for row in range(rows):
            odd[row], even[row] = odd[row].astype(jnp.bfloat16), even[row].astype(jnp.bfloat16)
            u_ref[2 * row, phase] = odd[row]
            u_ref[2 * row + 1, phase] = even[row]
            sums += add_sums(odd[row], width)
            if row < rows - 1:
                sums += add_sums(even[row], width)
        sums += jnp.where(last_here, 0.0, add_sums(even[rows - 1], width))
        sums += jnp.where(first_here, add_sums(part_ref[phase].astype(jnp.bfloat16), width), 0.0)
    half = sums.shape[1] // 2
    halves = []
    for row in range(2):
        own, other = sums[row : row + 1, :half], sums[row : row + 1, half:]
        halves += [jnp.where(column == 0, own, other), jnp.where(column == 0, other, own)]
    stats_ref[...] = jnp.concatenate(halves + [jnp.zeros((4, half), jnp.float32)], axis=0)


def halo_kernel(above_ref, next_ref, next_edge_ref, xs_ref, xs_next_ref, part_ref, own_w, other_w, u_ref, xs_above, xs_below):
    width = next_ref.shape[1]
    for row in range(HALO):
        spread_line(xs_above.at[row], above_ref[row, :width], above_ref[row, width:])
    spread_line(xs_below.at[0], next_ref[1], next_edge_ref[1])
    for phase in range(2):
        dot = functools.partial(tap_dot, phase=phase, own_w=own_w, other_w=other_w)
        outer = dot(xs_above[...], kr=3)
        u_ref[0, phase] = (outer[0] + dot(xs_above[1:2], kr=1)[0]).astype(jnp.bfloat16)
        u_ref[2, phase] = (outer[1] + part_ref[phase]).astype(jnp.bfloat16)
        u_ref[1, phase] = (dot(xs_above[1:2], kr=2)[0] + dot(xs_ref[0:1], kr=0)[0]).astype(jnp.bfloat16)
        u_ref[3, phase] = (dot(xs_next_ref[...], kr=2)[0] + dot(xs_below[...], kr=0)[0]).astype(jnp.bfloat16)


def group_sum(v, width):
    lane = lax.broadcasted_iota(jnp.int32, v.shape, 1)
    size = v.shape[1]
    step = 1
    while step < width:
        v = v + jnp.where(
            (lane & step) == 0, pltpu.roll(v, size - step, 1), pltpu.roll(v, step, 1)
        )
        step *= 2
    return v


def fill(ref, row, even, odd):
    total, channels = even.shape
    ref[row, :, 0:channels] = pltpu.roll(odd, 1, 0).astype(jnp.bfloat16)
    ref[row, :, channels : 2 * channels] = even.astype(jnp.bfloat16)
    ref[row, :, 2 * channels : 3 * channels] = odd.astype(jnp.bfloat16)
    ref[row, :, 3 * channels : 4 * channels] = pltpu.roll(even, total - 1, 0).astype(jnp.bfloat16)


def conv_kernel(
    count, u_ref, halo_ref, stats_ref, params_ref, own_w1, other_w1, own_w2, other_w2, out_ref, g, act, mixed
):
    main, _, total, cout = u_ref.shape
    lines = main + 2 * HALO
    width = total - EDGE
    half = own_w1.shape[-1]
    column = lax.axis_index("fsdp")
    own_at = pl.multiple_of(column * half, half)
    other_at = pl.multiple_of((1 - column) * half, half)

    def own_first(row):
        low, high = row[:, :half], row[:, half:]
        return jnp.concatenate([jnp.where(column == 0, low, high), jnp.where(column == 0, high, low)], axis=1)

    def kernel_row(a, own, other):
        return jnp.concatenate(
            [
                jnp.concatenate([ref[a, b, pl.ds(at, half), :] for b in range(3) for at in (own_at, other_at)], axis=0)
                for ref in (own, other)
            ],
            axis=1,
        )

    block = stats_ref[...]
    width_group = cout // NORM_GROUPS
    sums = jnp.concatenate([block[0:1], block[1:2]], axis=1)
    squares = jnp.concatenate([block[2:3], block[3:4]], axis=1)
    mean = group_sum(sums, width_group) / count
    spread = group_sum(squares, width_group) / count - mean * mean
    scale = lax.rsqrt(spread + 1e-05) * params_ref[0:1]
    shift = own_first(params_ref[1:2] - mean * scale)
    scale = own_first(scale)

    mask = edge_mask(width)
    place = lax.axis_index("rows")
    last = lax.axis_size("rows") - 1

    def inside(row, beyond):
        if row < beyond:
            return mask & (place > 0)
        if row >= lines - 2 * HALO + beyond:
            return mask & (place < last)
        return mask

    def hidden(row):
        if row < 3:
            source = halo_ref.at[row]
        elif row < 3 + main:
            source = u_ref.at[row - 3]
        else:
            source = halo_ref.at[3]
        seen = inside(row, HALO)
        fill(
            g,
            row,
            *[jnp.where(seen, silu(source[phase].astype(jnp.float32) * scale + shift), 0.0) for phase in range(2)],
        )

    def conv(source, start, size, cells, phase, own, other, bias):
        acc = bias
        for a in range(3):
            acc = acc + jnp.dot(
                source[start + a : start + a + size, 0:cells, phase * cout : (phase + 3) * cout].reshape(
                    size * cells, 3 * cout
                ),
                kernel_row(a, own, other),
                preferred_element_type=jnp.float32,
            )
        return acc.reshape(size, cells, cout)

    chunk = 2
    bias1 = own_first(params_ref[2:3])
    bias2 = own_first(params_ref[3:4])

    def first(start):
        results = [silu(conv(g, start, chunk, total, phase, own_w1, other_w1, bias1)) for phase in range(2)]
        for row in range(chunk):
            seen = inside(start + row, 1)
            fill(act, start + row, *[jnp.where(seen, r[row], 0.0) for r in results])

    def second(start):
        for phase in range(2):
            acc = conv(act, start, chunk, width, phase, own_w2, other_w2, bias2)
            for row in range(chunk):
                for side in range(2):
                    mixed[side, start + row, pl.ds(phase, width, stride=2), :] = acc[
                        row, :, side * half : (side + 1) * half
                    ]
        for row in range(start, start + chunk):
            out_ref[row, :, pl.ds(own_at, half)] = mixed[0, row].astype(jnp.bfloat16)
            out_ref[row, :, pl.ds(other_at, half)] = mixed[1, row].astype(jnp.bfloat16)

    for row in range(chunk):
        hidden(row)
    for start in range(0, lines - 2, chunk):
        for row in range(start + chunk, start + 2 * chunk):
            hidden(row)
        first(start)
        if start >= chunk:
            second(start - chunk)


def total_over(block, axis):
    size = lax.axis_size(axis)
    if size & (size - 1):
        return lax.psum(block, axis)
    steps = [2**n for n in range(size.bit_length() - 1)]
    for step in steps[1:] + steps[:1]:
        block = block + lax.ppermute(block, axis, [(i, i ^ step) for i in range(size)])
    return block


def after(value, *others):
    return lax.optimization_barrier((value, *others))[0]


def local(image, deconv_weight, norm_gain, norm_shift, first_weight, first_bias, second_weight, second_bias):
    rows, width, cin = image.shape
    taps, _, _, lanes = deconv_weight.shape
    columns = lax.axis_size("fsdp")
    cout = lanes * columns
    assert columns == 2 and rows == HALO and width % EDGE == 0 and lanes == LANES
    n_rows = lax.axis_size("rows")
    count = float(2 * rows * n_rows * 2 * width * columns * (cout // NORM_GROUPS))
    swap = [(0, 1), (1, 0)]
    to_next = [(i, i + 1) for i in range(n_rows - 1)]
    to_previous = [(i + 1, i) for i in range(n_rows - 1)]
    total = width + EDGE
    hbm = pl.BlockSpec(memory_space=pltpu.HBM)
    vmem = pl.BlockSpec(memory_space=pltpu.VMEM)
    bf16, f32 = jnp.bfloat16, jnp.float32

    def call(kernel, ins, outs, scratch, name, flops=0):
        return pl.pallas_call(
            kernel,
            out_shape=tuple(jax.ShapeDtypeStruct(*o) for o in outs),
            in_specs=ins,
            out_specs=(vmem,) * len(outs),
            scratch_shapes=scratch,
            compiler_params=pltpu.CompilerParams(vmem_limit_bytes=VMEM_BYTES),
            cost_estimate=pl.CostEstimate(flops=flops, bytes_accessed=2**21, transcendentals=0),
            name=name,
        )

    in_hbm = functools.partial(pltpu.with_memory_space_constraint, memory_space=pltpu.HBM)
    shape_w = (taps, taps // 2, 2, cin, lanes)
    following = lax.ppermute(image, "rows", to_previous)
    near, edges = call(
        cut_kernel,
        [hbm],
        [(image.shape, bf16), ((rows, EDGE, cin), bf16)],
        [pltpu.SemaphoreType.DMA((2,))],
        "cut",
    )(in_hbm(image))
    edge = lax.ppermute(edges, "fsdp", swap)
    other_w = lax.ppermute(deconv_weight, "fsdp", swap).reshape(shape_w)
    first_other = lax.ppermute(after(first_weight, edges), "fsdp", swap)
    second_other = lax.ppermute(after(second_weight, edges), "fsdp", swap)
    (own_w,) = call(near_kernel, [hbm], [(shape_w, bf16)], [pltpu.SemaphoreType.DMA(())], "near_weights")(
        in_hbm(after(deconv_weight, edges).reshape(shape_w))
    )
    lines = jnp.concatenate([after(near, own_w), edge], axis=1)
    above = lax.ppermute(lines, "rows", to_next)
    (xs,) = call(own_kernel, [vmem], [((rows, total, 3 * cin), bf16)], [], "own_lines")(lines)
    (next_edges,) = call(pick_kernel, [vmem], [((rows, EDGE, cin), bf16)], [], "next_edges")(following)
    next_edge = lax.ppermute(next_edges, "fsdp", swap)
    u_line = (2, total, cout)
    u, part, xs_next, stats = call(
        main_kernel,
        [vmem] * 5,
        [((2 * rows, *u_line), bf16), (u_line, f32), ((1, total, 3 * cin), bf16), ((8, cout // 2), f32)],
        [],
        "deconv_main",
        flops=2 * 2 * (2 * rows) * total * 4 * cin * cout,
    )(xs, following, next_edge, own_w, other_w)
    (halo,) = call(
        halo_kernel,
        [vmem] * 8,
        [((4, *u_line), bf16)],
        [pltpu.VMEM((HALO, total, 3 * cin), bf16), pltpu.VMEM((1, total, 3 * cin), bf16)],
        "deconv_halo",
        flops=2 * 2 * 4 * total * 4 * cin * cout,
    )(above, following, next_edge, xs, xs_next, part, own_w, other_w)

    totals = total_over(total_over(stats, "fsdp"), "rows")
    params = jnp.stack([norm_gain, norm_shift, first_bias, second_bias])
    (out,) = call(
        functools.partial(conv_kernel, count),
        [vmem] * 8,
        [((2 * rows, 2 * width, cout), bf16)],
        [
            pltpu.VMEM((2 * rows + 2 * HALO, total, 4 * cout), bf16),
            pltpu.VMEM((2 * rows + 2, total, 4 * cout), bf16),
            pltpu.VMEM((2, 2 * rows, 2 * width, lanes), f32),
        ],
        "convs",
        flops=5 * 10**9,
    )(u, halo, totals, params, first_weight, first_other, second_weight, second_other)
    return out


def solution(mesh):
    placed = (
        P(("groups", "rows"), "fsdp", None),
        P(None, None, None, "fsdp"),
        P(),
        P(),
        P(None, None, None, "fsdp"),
        P(),
        P(None, None, None, "fsdp"),
        P(),
    )
    return jax.shard_map(
        local,
        mesh=mesh,
        in_specs=placed,
        out_specs=P(("groups", "rows"), "fsdp", None),
        check_vma=False,
    )
```

```python
import functools

import jax
import jax.numpy as jnp
from jax import lax
from jax.experimental import pallas as pl
from jax.experimental.pallas import tpu as pltpu
from jax.sharding import PartitionSpec as P

NORM_GROUPS = 32
HALO = 2
EDGE = 16
LANES = 128
VMEM_BYTES = 24 * 2**20


def silu(v):
    h = 0.5 * v
    return h + h * jnp.tanh(h)


def edge_mask(width):
    column = lax.axis_index("fsdp")
    last = lax.axis_size("fsdp") - 1
    cell = lax.broadcasted_iota(jnp.int32, (width + EDGE, 1), 0) - width
    right = (cell < EDGE // 2) & (column < last)
    left = (cell >= EDGE // 2) & (column > 0)
    return (cell < 0) | right | left


def cut_kernel(image_ref, near_ref, edges_ref, sems):
    width = image_ref.shape[1]
    start = pl.multiple_of((1 - lax.axis_index("fsdp")) * (width - EDGE), EDGE)
    copies = [
        pltpu.make_async_copy(image_ref.at[:, pl.ds(start, EDGE), :], edges_ref, sems.at[0]),
        pltpu.make_async_copy(image_ref, near_ref, sems.at[1]),
    ]
    for copy in copies:
        copy.start()
    for copy in copies:
        copy.wait()


def pick_kernel(lines_ref, edges_ref):
    width = lines_ref.shape[1]
    at_left = lax.axis_index("fsdp") == 0

    @pl.when(at_left)
    def _():
        edges_ref[...] = lines_ref[:, width - EDGE :]

    @pl.when(jnp.logical_not(at_left))
    def _():
        edges_ref[...] = lines_ref[:, :EDGE]


def near_kernel(weight_ref, near_ref, sem):
    copy = pltpu.make_async_copy(weight_ref, near_ref, sem)
    copy.start()
    copy.wait()


def spread_line(out, main, edge):
    width, cin = main.shape
    line = jnp.concatenate([main.astype(jnp.float32), edge.astype(jnp.float32)], axis=0)
    line = jnp.where(edge_mask(width), line, 0.0)
    out[:, 0:cin] = pltpu.roll(line, width + EDGE - 1, 0).astype(jnp.bfloat16)
    out[:, cin : 2 * cin] = line.astype(jnp.bfloat16)
    out[:, 2 * cin : 3 * cin] = pltpu.roll(line, 1, 0).astype(jnp.bfloat16)


def tap_dot(lines, phase, kr, own_w, other_w):
    count, total, lanes = lines.shape
    cin = lanes // 3
    low = (1 - phase) * cin
    weight = jnp.concatenate(
        [ref[kr, :, 1 - phase].reshape(2 * cin, ref.shape[-1]) for ref in (own_w, other_w)], axis=1
    )
    out = jnp.dot(
        lines[:, :, low : low + 2 * cin].reshape(count * total, 2 * cin),
        weight,
        preferred_element_type=jnp.float32,
    )
    return out.reshape(count, total, weight.shape[-1])


def add_sums(line, width):
    values = line[:width].astype(jnp.float32)
    return jnp.concatenate(
        [jnp.sum(values, axis=0, keepdims=True), jnp.sum(values * values, axis=0, keepdims=True)], axis=0
    )


def own_kernel(lines_ref, own_w, other_w, xs_ref, u_ref, part_ref, tail_ref, sums_ref):
    rows, total, _ = lines_ref.shape
    width = total - EDGE
    for row in range(rows):
        spread_line(xs_ref.at[row], lines_ref[row, :width], lines_ref[row, width:])
    first_here = lax.axis_index("rows") == 0
    sums = jnp.zeros((2, u_ref.shape[-1]), jnp.float32)
    for phase in range(2):
        dot = functools.partial(tap_dot, phase=phase, own_w=own_w, other_w=other_w)
        upper = dot(xs_ref[...], kr=1)
        lower = dot(xs_ref[...], kr=3)
        part_ref[phase] = upper[0]
        tail_ref[phase, 1] = lower[rows - 1]
        even = [(upper[row + 1] + lower[row]).astype(jnp.bfloat16) for row in range(rows - 1)]
        upper = dot(xs_ref[...], kr=2)
        lower = dot(xs_ref[1:], kr=0)
        tail_ref[phase, 0] = upper[rows - 1]
        odd = [(upper[row] + lower[row]).astype(jnp.bfloat16) for row in range(rows - 1)]
        for row in range(rows - 1):
            u_ref[2 * row, phase] = odd[row]
            u_ref[2 * row + 1, phase] = even[row]
            sums += add_sums(odd[row], width) + add_sums(even[row], width)
        sums += jnp.where(first_here, add_sums(part_ref[phase].astype(jnp.bfloat16), width), 0.0)
    sums_ref[...] = sums


def next_kernel(next_ref, edge_ref, tail_ref, sums_ref, own_w, other_w, u_ref, xs_ref, stats_ref):
    width = next_ref.shape[1]
    spread_line(xs_ref.at[0], next_ref[0], edge_ref[0])
    last_here = lax.axis_index("rows") == lax.axis_size("rows") - 1
    column = lax.axis_index("fsdp")
    sums = sums_ref[...]
    for phase in range(2):
        dot = functools.partial(tap_dot, phase=phase, own_w=own_w, other_w=other_w)
        odd = (tail_ref[phase, 0] + dot(xs_ref[...], kr=0)[0]).astype(jnp.bfloat16)
        even = (tail_ref[phase, 1] + dot(xs_ref[...], kr=1)[0]).astype(jnp.bfloat16)
        u_ref[0, phase] = odd
        u_ref[1, phase] = even
        sums += add_sums(odd, width) + jnp.where(last_here, 0.0, add_sums(even, width))
    half = sums.shape[1] // 2
    halves = []
    for row in range(2):
        own, other = sums[row : row + 1, :half], sums[row : row + 1, half:]
        halves += [jnp.where(column == 0, own, other), jnp.where(column == 0, other, own)]
    stats_ref[...] = jnp.concatenate(halves + [jnp.zeros((4, half), jnp.float32)], axis=0)


def halo_kernel(above_ref, next_ref, next_edge_ref, xs_ref, xs_next_ref, part_ref, own_w, other_w, u_ref, xs_above, xs_below):
    width = next_ref.shape[1]
    for row in range(HALO):
        spread_line(xs_above.at[row], above_ref[row, :width], above_ref[row, width:])
    spread_line(xs_below.at[0], next_ref[1], next_edge_ref[1])
    for phase in range(2):
        dot = functools.partial(tap_dot, phase=phase, own_w=own_w, other_w=other_w)
        outer = dot(xs_above[...], kr=3)
        u_ref[0, phase] = (outer[0] + dot(xs_above[1:2], kr=1)[0]).astype(jnp.bfloat16)
        u_ref[2, phase] = (outer[1] + part_ref[phase]).astype(jnp.bfloat16)
        u_ref[1, phase] = (dot(xs_above[1:2], kr=2)[0] + dot(xs_ref[0:1], kr=0)[0]).astype(jnp.bfloat16)
        u_ref[3, phase] = (dot(xs_next_ref[...], kr=2)[0] + dot(xs_below[...], kr=0)[0]).astype(jnp.bfloat16)


def group_sum(v, width):
    lane = lax.broadcasted_iota(jnp.int32, v.shape, 1)
    size = v.shape[1]
    step = 1
    while step < width:
        v = v + jnp.where(
            (lane & step) == 0, pltpu.roll(v, size - step, 1), pltpu.roll(v, step, 1)
        )
        step *= 2
    return v


def fill(ref, row, even, odd):
    total, channels = even.shape
    ref[row, :, 0:channels] = pltpu.roll(odd, 1, 0).astype(jnp.bfloat16)
    ref[row, :, channels : 2 * channels] = even.astype(jnp.bfloat16)
    ref[row, :, 2 * channels : 3 * channels] = odd.astype(jnp.bfloat16)
    ref[row, :, 3 * channels : 4 * channels] = pltpu.roll(even, total - 1, 0).astype(jnp.bfloat16)


def conv_kernel(
    count, u_ref, u_next_ref, halo_ref, mine_ref, passed_ref, params_ref, own_w1, other_w1, own_w2, other_w2, out_ref, g, act, mixed
):
    early, _, total, cout = u_ref.shape
    main = early + u_next_ref.shape[0]
    lines = main + 2 * HALO
    width = total - EDGE
    half = own_w1.shape[-1]
    column = lax.axis_index("fsdp")
    own_at = pl.multiple_of(column * half, half)
    other_at = pl.multiple_of((1 - column) * half, half)

    def own_first(row):
        low, high = row[:, :half], row[:, half:]
        return jnp.concatenate([jnp.where(column == 0, low, high), jnp.where(column == 0, high, low)], axis=1)

    def kernel_row(a, own, other):
        return jnp.concatenate(
            [
                jnp.concatenate([ref[a, b, pl.ds(at, half), :] for b in range(3) for at in (own_at, other_at)], axis=0)
                for ref in (own, other)
            ],
            axis=1,
        )

    block = jnp.where(column == 1, mine_ref[...], passed_ref[...])
    width_group = cout // NORM_GROUPS
    sums = jnp.concatenate([block[0:1], block[1:2]], axis=1)
    squares = jnp.concatenate([block[2:3], block[3:4]], axis=1)
    mean = group_sum(sums, width_group) / count
    spread = group_sum(squares, width_group) / count - mean * mean
    scale = lax.rsqrt(spread + 1e-05) * params_ref[0:1]
    shift = own_first(params_ref[1:2] - mean * scale)
    scale = own_first(scale)

    mask = edge_mask(width)
    place = lax.axis_index("rows")
    last = lax.axis_size("rows") - 1

    def inside(row, beyond):
        if row < beyond:
            return mask & (place > 0)
        if row >= lines - 2 * HALO + beyond:
            return mask & (place < last)
        return mask

    def hidden(row):
        if row < 3:
            source = halo_ref.at[row]
        elif row < 3 + early:
            source = u_ref.at[row - 3]
        elif row < 3 + main:
            source = u_next_ref.at[row - 3 - early]
        else:
            source = halo_ref.at[3]
        seen = inside(row, HALO)
        fill(
            g,
            row,
            *[jnp.where(seen, silu(source[phase].astype(jnp.float32) * scale + shift), 0.0) for phase in range(2)],
        )

    def conv(source, start, size, cells, phase, own, other, bias):
        acc = bias
        for a in range(3):
            acc = acc + jnp.dot(
                source[start + a : start + a + size, 0:cells, phase * cout : (phase + 3) * cout].reshape(
                    size * cells, 3 * cout
                ),
                kernel_row(a, own, other),
                preferred_element_type=jnp.float32,
            )
        return acc.reshape(size, cells, cout)

    chunk = 2
    bias1 = own_first(params_ref[2:3])
    bias2 = own_first(params_ref[3:4])

    def first(start):
        results = [silu(conv(g, start, chunk, total, phase, own_w1, other_w1, bias1)) for phase in range(2)]
        for row in range(chunk):
            seen = inside(start + row, 1)
            fill(act, start + row, *[jnp.where(seen, r[row], 0.0) for r in results])

    def second(start):
        for phase in range(2):
            acc = conv(act, start, chunk, width, phase, own_w2, other_w2, bias2)
            for row in range(chunk):
                for side in range(2):
                    mixed[side, start + row, pl.ds(phase, width, stride=2), :] = acc[
                        row, :, side * half : (side + 1) * half
                    ]
        for row in range(start, start + chunk):
            out_ref[row, :, pl.ds(own_at, half)] = mixed[0, row].astype(jnp.bfloat16)
            out_ref[row, :, pl.ds(other_at, half)] = mixed[1, row].astype(jnp.bfloat16)

    for row in range(chunk):
        hidden(row)
    for start in range(0, lines - 2, chunk):
        for row in range(start + chunk, start + 2 * chunk):
            hidden(row)
        first(start)
        if start >= chunk:
            second(start - chunk)


def total_over(block, last):
    size = lax.axis_size("rows")
    block = block + lax.ppermute(block, "fsdp", [(0, 1)])
    assert size & (size - 1) == 0
    steps = [2**n for n in range(size.bit_length() - 1)]
    for step in steps[1:] + steps[:1]:
        pairs = [(2 * i + 1, 2 * (i ^ step) + 1) for i in range(size)]
        block = block + lax.ppermute(block, ("rows", "fsdp"), pairs)
    return block, lax.ppermute(after(block, last), "fsdp", [(1, 0)])


def after(value, *others):
    return lax.optimization_barrier((value, *others))[0]


def local(image, deconv_weight, norm_gain, norm_shift, first_weight, first_bias, second_weight, second_bias):
    rows, width, cin = image.shape
    taps, _, _, lanes = deconv_weight.shape
    columns = lax.axis_size("fsdp")
    cout = lanes * columns
    assert columns == 2 and rows == HALO and width % EDGE == 0 and lanes == LANES
    n_rows = lax.axis_size("rows")
    count = float(2 * rows * n_rows * 2 * width * columns * (cout // NORM_GROUPS))
    swap = [(0, 1), (1, 0)]
    to_next = [(i, i + 1) for i in range(n_rows - 1)]
    to_previous = [(i + 1, i) for i in range(n_rows - 1)]
    total = width + EDGE
    hbm = pl.BlockSpec(memory_space=pltpu.HBM)
    vmem = pl.BlockSpec(memory_space=pltpu.VMEM)
    bf16, f32 = jnp.bfloat16, jnp.float32

    def call(kernel, ins, outs, scratch, name, flops=0):
        return pl.pallas_call(
            kernel,
            out_shape=tuple(jax.ShapeDtypeStruct(*o) for o in outs),
            in_specs=ins,
            out_specs=(vmem,) * len(outs),
            scratch_shapes=scratch,
            compiler_params=pltpu.CompilerParams(vmem_limit_bytes=VMEM_BYTES),
            cost_estimate=pl.CostEstimate(flops=flops, bytes_accessed=2**21, transcendentals=0),
            name=name,
        )

    in_hbm = functools.partial(pltpu.with_memory_space_constraint, memory_space=pltpu.HBM)
    shape_w = (taps, taps // 2, 2, cin, lanes)
    following = lax.ppermute(image, "rows", to_previous)
    near, edges = call(
        cut_kernel,
        [hbm],
        [(image.shape, bf16), ((rows, EDGE, cin), bf16)],
        [pltpu.SemaphoreType.DMA((2,))],
        "cut",
    )(in_hbm(image))
    edge = lax.ppermute(edges, "fsdp", swap)
    other_w = lax.ppermute(deconv_weight, "fsdp", swap).reshape(shape_w)
    first_other = lax.ppermute(after(first_weight, edges), "fsdp", swap)
    second_other = lax.ppermute(after(second_weight, edges), "fsdp", swap)
    (own_w,) = call(near_kernel, [hbm], [(shape_w, bf16)], [pltpu.SemaphoreType.DMA(())], "near_weights")(
        in_hbm(after(deconv_weight, edges).reshape(shape_w))
    )
    lines = jnp.concatenate([after(near, own_w), edge], axis=1)
    above = lax.ppermute(lines, "rows", to_next)
    u_line = (2, total, cout)
    xs, u, part, tail, sums = call(
        own_kernel,
        [vmem] * 3,
        [
            ((rows, total, 3 * cin), bf16),
            ((2 * rows - 2, *u_line), bf16),
            (u_line, f32),
            ((2, *u_line), f32),
            ((2, cout), f32),
        ],
        [],
        "deconv_own",
        flops=2 * 2 * (2 * rows - 1) * total * 4 * cin * cout,
    )(lines, own_w, other_w)
    (next_edges,) = call(pick_kernel, [vmem], [((rows, EDGE, cin), bf16)], [], "next_edges")(following)
    next_edge = lax.ppermute(next_edges, "fsdp", swap)
    u_next, xs_next, stats = call(
        next_kernel,
        [vmem] * 6,
        [((2, *u_line), bf16), ((1, total, 3 * cin), bf16), ((8, cout // 2), f32)],
        [],
        "deconv_next",
        flops=2 * 2 * total * 4 * cin * cout,
    )(following, next_edge, tail, sums, own_w, other_w)
    (halo,) = call(
        halo_kernel,
        [vmem] * 8,
        [((4, *u_line), bf16)],
        [pltpu.VMEM((HALO, total, 3 * cin), bf16), pltpu.VMEM((1, total, 3 * cin), bf16)],
        "deconv_halo",
        flops=2 * 2 * 4 * total * 4 * cin * cout,
    )(above, following, next_edge, xs, xs_next, part, own_w, other_w)

    mine, passed = total_over(stats, halo)
    params = jnp.stack([norm_gain, norm_shift, first_bias, second_bias])
    (out,) = call(
        functools.partial(conv_kernel, count),
        [vmem] * 10,
        [((2 * rows, 2 * width, cout), bf16)],
        [
            pltpu.VMEM((2 * rows + 2 * HALO, total, 4 * cout), bf16),
            pltpu.VMEM((2 * rows + 2, total, 4 * cout), bf16),
            pltpu.VMEM((2, 2 * rows, 2 * width, lanes), f32),
        ],
        "convs",
        flops=5 * 10**9,
    )(u, u_next, halo, mine, passed, params, first_weight, first_other, second_weight, second_other)
    return out


def solution(mesh):
    placed = (
        P(("groups", "rows"), "fsdp", None),
        P(None, None, None, "fsdp"),
        P(),
        P(),
        P(None, None, None, "fsdp"),
        P(),
        P(None, None, None, "fsdp"),
        P(),
    )
    return jax.shard_map(
        local,
        mesh=mesh,
        in_specs=placed,
        out_specs=P(("groups", "rows"), "fsdp", None),
        check_vma=False,
    )
```

```python
import functools

import jax
import jax.numpy as jnp
from jax import lax
from jax.experimental import pallas as pl
from jax.experimental.pallas import tpu as pltpu
from jax.sharding import PartitionSpec as P

NORM_GROUPS = 32
HALO = 2
EDGE = 16
LANES = 128
VMEM_BYTES = 24 * 2**20


def silu(v):
    h = 0.5 * v
    return h + h * jnp.tanh(h)


def edge_mask(width):
    column = lax.axis_index("fsdp")
    last = lax.axis_size("fsdp") - 1
    cell = lax.broadcasted_iota(jnp.int32, (width + EDGE, 1), 0) - width
    right = (cell < EDGE // 2) & (column < last)
    left = (cell >= EDGE // 2) & (column > 0)
    return (cell < 0) | right | left


def cut_kernel(image_ref, near_ref, edges_ref, sems):
    width = image_ref.shape[1]
    start = pl.multiple_of((1 - lax.axis_index("fsdp")) * (width - EDGE), EDGE)
    copies = [
        pltpu.make_async_copy(image_ref.at[:, pl.ds(start, EDGE), :], edges_ref, sems.at[0]),
        pltpu.make_async_copy(image_ref, near_ref, sems.at[1]),
    ]
    for copy in copies:
        copy.start()
    for copy in copies:
        copy.wait()


def pick_kernel(lines_ref, edges_ref):
    width = lines_ref.shape[1]
    at_left = lax.axis_index("fsdp") == 0

    @pl.when(at_left)
    def _():
        edges_ref[...] = lines_ref[:, width - EDGE :]

    @pl.when(jnp.logical_not(at_left))
    def _():
        edges_ref[...] = lines_ref[:, :EDGE]


def near_kernel(weight_ref, near_ref, sem):
    copy = pltpu.make_async_copy(weight_ref, near_ref, sem)
    copy.start()
    copy.wait()


def spread_line(out, main, edge, inside=True):
    width, cin = main.shape
    line = jnp.concatenate([main.astype(jnp.float32), edge.astype(jnp.float32)], axis=0)
    line = jnp.where(edge_mask(width) & inside, line, 0.0)
    out[:, 0:cin] = pltpu.roll(line, width + EDGE - 1, 0).astype(jnp.bfloat16)
    out[:, cin : 2 * cin] = line.astype(jnp.bfloat16)
    out[:, 2 * cin : 3 * cin] = pltpu.roll(line, 1, 0).astype(jnp.bfloat16)


def tap_dot(lines, phase, kr, own_w, other_w):
    count, total, lanes = lines.shape
    cin = lanes // 3
    low = (1 - phase) * cin
    weight = jnp.concatenate(
        [ref[kr, :, 1 - phase].reshape(2 * cin, ref.shape[-1]) for ref in (own_w, other_w)], axis=1
    )
    out = jnp.dot(
        lines[:, :, low : low + 2 * cin].reshape(count * total, 2 * cin),
        weight,
        preferred_element_type=jnp.float32,
    )
    return out.reshape(count, total, weight.shape[-1])


def add_sums(line, width):
    values = line[:width].astype(jnp.float32)
    return jnp.concatenate(
        [jnp.sum(values, axis=0, keepdims=True), jnp.sum(values * values, axis=0, keepdims=True)], axis=0
    )


def own_kernel(lines_ref, own_w, other_w, xs_ref, u_ref, part_ref, tail_ref, sums_ref):
    rows, total, _ = lines_ref.shape
    width = total - EDGE
    for row in range(rows):
        spread_line(xs_ref.at[row], lines_ref[row, :width], lines_ref[row, width:])
    first_here = lax.axis_index("rows") == 0
    sums = jnp.zeros((2, u_ref.shape[-1]), jnp.float32)
    for phase in range(2):
        dot = functools.partial(tap_dot, phase=phase, own_w=own_w, other_w=other_w)
        upper = dot(xs_ref[...], kr=1)
        lower = dot(xs_ref[...], kr=3)
        part_ref[phase] = upper[0]
        tail_ref[phase, 1] = lower[rows - 1]
        even = [(upper[row + 1] + lower[row]).astype(jnp.bfloat16) for row in range(rows - 1)]
        upper = dot(xs_ref[...], kr=2)
        lower = dot(xs_ref[1:], kr=0)
        tail_ref[phase, 0] = upper[rows - 1]
        odd = [(upper[row] + lower[row]).astype(jnp.bfloat16) for row in range(rows - 1)]
        for row in range(rows - 1):
            u_ref[2 * row, phase] = odd[row]
            u_ref[2 * row + 1, phase] = even[row]
            sums += add_sums(odd[row], width) + add_sums(even[row], width)
        sums += jnp.where(first_here, add_sums(part_ref[phase].astype(jnp.bfloat16), width), 0.0)
    sums_ref[...] = sums


def next_kernel(next_ref, edge_ref, tail_ref, sums_ref, own_w, other_w, u_ref, xs_ref, stats_ref):
    width = next_ref.shape[1]
    last_here = lax.axis_index("rows") == lax.axis_size("rows") - 1
    spread_line(xs_ref.at[0], next_ref[0], edge_ref[0], jnp.logical_not(last_here))
    column = lax.axis_index("fsdp")
    sums = sums_ref[...]
    for phase in range(2):
        dot = functools.partial(tap_dot, phase=phase, own_w=own_w, other_w=other_w)
        odd = (tail_ref[phase, 0] + dot(xs_ref[...], kr=0)[0]).astype(jnp.bfloat16)
        even = (tail_ref[phase, 1] + dot(xs_ref[...], kr=1)[0]).astype(jnp.bfloat16)
        u_ref[0, phase] = odd
        u_ref[1, phase] = even
        sums += add_sums(odd, width) + jnp.where(last_here, 0.0, add_sums(even, width))
    half = sums.shape[1] // 2
    halves = []
    for row in range(2):
        own, other = sums[row : row + 1, :half], sums[row : row + 1, half:]
        halves += [jnp.where(column == 0, own, other), jnp.where(column == 0, other, own)]
    stats_ref[...] = jnp.concatenate(halves + [jnp.zeros((4, half), jnp.float32)], axis=0)


def halo_kernel(above_ref, next_ref, next_edge_ref, xs_ref, xs_next_ref, part_ref, own_w, other_w, u_ref, xs_above, xs_below):
    width = next_ref.shape[1]
    place = lax.axis_index("rows")
    for row in range(HALO):
        spread_line(xs_above.at[row], above_ref[row, :width], above_ref[row, width:], place > 0)
    spread_line(xs_below.at[0], next_ref[1], next_edge_ref[1], place < lax.axis_size("rows") - 1)
    for phase in range(2):
        dot = functools.partial(tap_dot, phase=phase, own_w=own_w, other_w=other_w)
        outer = dot(xs_above[...], kr=3)
        u_ref[0, phase] = (outer[0] + dot(xs_above[1:2], kr=1)[0]).astype(jnp.bfloat16)
        u_ref[2, phase] = (outer[1] + part_ref[phase]).astype(jnp.bfloat16)
        u_ref[1, phase] = (dot(xs_above[1:2], kr=2)[0] + dot(xs_ref[0:1], kr=0)[0]).astype(jnp.bfloat16)
        u_ref[3, phase] = (dot(xs_next_ref[...], kr=2)[0] + dot(xs_below[...], kr=0)[0]).astype(jnp.bfloat16)


def group_sum(v, width):
    lane = lax.broadcasted_iota(jnp.int32, v.shape, 1)
    size = v.shape[1]
    step = 1
    while step < width:
        v = v + jnp.where(
            (lane & step) == 0, pltpu.roll(v, size - step, 1), pltpu.roll(v, step, 1)
        )
        step *= 2
    return v


def fill(ref, row, even, odd):
    total, channels = even.shape
    ref[row, :, 0:channels] = pltpu.roll(odd, 1, 0).astype(jnp.bfloat16)
    ref[row, :, channels : 2 * channels] = even.astype(jnp.bfloat16)
    ref[row, :, 2 * channels : 3 * channels] = odd.astype(jnp.bfloat16)
    ref[row, :, 3 * channels : 4 * channels] = pltpu.roll(even, total - 1, 0).astype(jnp.bfloat16)


def conv_kernel(
    count, u_ref, u_next_ref, halo_ref, stats_ref, params_ref, own_w1, other_w1, own_w2, other_w2, out_ref, g, act, mixed
):
    early, _, total, cout = u_ref.shape
    main = early + u_next_ref.shape[0]
    lines = main + 2 * HALO
    width = total - EDGE
    half = own_w1.shape[-1]
    column = lax.axis_index("fsdp")
    own_at = pl.multiple_of(column * half, half)
    other_at = pl.multiple_of((1 - column) * half, half)

    def own_first(row):
        low, high = row[:, :half], row[:, half:]
        return jnp.concatenate([jnp.where(column == 0, low, high), jnp.where(column == 0, high, low)], axis=1)

    def kernel_row(a, own, other):
        return jnp.concatenate(
            [
                jnp.concatenate([ref[a, b, pl.ds(at, half), :] for b in range(3) for at in (own_at, other_at)], axis=0)
                for ref in (own, other)
            ],
            axis=1,
        )

    block = stats_ref[...]
    width_group = cout // NORM_GROUPS
    sums = jnp.concatenate([block[0:1], block[1:2]], axis=1)
    squares = jnp.concatenate([block[2:3], block[3:4]], axis=1)
    mean = group_sum(sums, width_group) / count
    spread = group_sum(squares, width_group) / count - mean * mean
    scale = lax.rsqrt(spread + 1e-05) * params_ref[0:1]
    shift = own_first(params_ref[1:2] - mean * scale)
    scale = own_first(scale)

    mask = edge_mask(width)
    place = lax.axis_index("rows")
    last = lax.axis_size("rows") - 1

    def inside(row, beyond):
        if row < beyond:
            return mask & (place > 0)
        if row >= lines - 2 * HALO + beyond:
            return mask & (place < last)
        return mask

    def hidden(row):
        if row < 3:
            source = halo_ref.at[row]
        elif row < 3 + early:
            source = u_ref.at[row - 3]
        elif row < 3 + main:
            source = u_next_ref.at[row - 3 - early]
        else:
            source = halo_ref.at[3]
        seen = inside(row, HALO)
        fill(
            g,
            row,
            *[jnp.where(seen, silu(source[phase].astype(jnp.float32) * scale + shift), 0.0) for phase in range(2)],
        )

    def conv(source, start, size, cells, phase, own, other, bias):
        acc = bias
        for a in range(3):
            acc = acc + jnp.dot(
                source[start + a : start + a + size, 0:cells, phase * cout : (phase + 3) * cout].reshape(
                    size * cells, 3 * cout
                ),
                kernel_row(a, own, other),
                preferred_element_type=jnp.float32,
            )
        return acc.reshape(size, cells, cout)

    chunk = 2
    bias1 = own_first(params_ref[2:3])
    bias2 = own_first(params_ref[3:4])

    def first(start):
        results = [silu(conv(g, start, chunk, total, phase, own_w1, other_w1, bias1)) for phase in range(2)]
        for row in range(chunk):
            seen = inside(start + row, 1)
            fill(act, start + row, *[jnp.where(seen, r[row], 0.0) for r in results])

    def second(start):
        for phase in range(2):
            acc = conv(act, start, chunk, width, phase, own_w2, other_w2, bias2)
            for row in range(chunk):
                for side in range(2):
                    mixed[side, start + row, pl.ds(phase, width, stride=2), :] = acc[
                        row, :, side * half : (side + 1) * half
                    ]
        for row in range(start, start + chunk):
            out_ref[row, :, pl.ds(own_at, half)] = mixed[0, row].astype(jnp.bfloat16)
            out_ref[row, :, pl.ds(other_at, half)] = mixed[1, row].astype(jnp.bfloat16)

    for row in range(chunk):
        hidden(row)
    for start in range(0, lines - 2, chunk):
        for row in range(start + chunk, start + 2 * chunk):
            hidden(row)
        first(start)
        if start >= chunk:
            second(start - chunk)


def total_over(block, axis):
    size = lax.axis_size(axis)
    if size & (size - 1):
        return lax.psum(block, axis)
    steps = [2**n for n in range(size.bit_length() - 1)]
    for step in steps[1:] + steps[:1]:
        block = block + lax.ppermute(block, axis, [(i, i ^ step) for i in range(size)])
    return block


def after(value, *others):
    return lax.optimization_barrier((value, *others))[0]


def local(image, deconv_weight, norm_gain, norm_shift, first_weight, first_bias, second_weight, second_bias):
    rows, width, cin = image.shape
    taps, _, _, lanes = deconv_weight.shape
    columns = lax.axis_size("fsdp")
    cout = lanes * columns
    assert columns == 2 and rows == HALO and width % EDGE == 0 and lanes == LANES
    n_rows = lax.axis_size("rows")
    count = float(2 * rows * n_rows * 2 * width * columns * (cout // NORM_GROUPS))
    swap = [(0, 1), (1, 0)]
    to_next = [(i, (i + 1) % n_rows) for i in range(n_rows)]
    to_previous = [((i + 1) % n_rows, i) for i in range(n_rows)]
    total = width + EDGE
    hbm = pl.BlockSpec(memory_space=pltpu.HBM)
    vmem = pl.BlockSpec(memory_space=pltpu.VMEM)
    bf16, f32 = jnp.bfloat16, jnp.float32

    def call(kernel, ins, outs, scratch, name, flops=0):
        return pl.pallas_call(
            kernel,
            out_shape=tuple(jax.ShapeDtypeStruct(*o) for o in outs),
            in_specs=ins,
            out_specs=(vmem,) * len(outs),
            scratch_shapes=scratch,
            compiler_params=pltpu.CompilerParams(vmem_limit_bytes=VMEM_BYTES),
            cost_estimate=pl.CostEstimate(flops=flops, bytes_accessed=2**21, transcendentals=0),
            name=name,
        )

    in_hbm = functools.partial(pltpu.with_memory_space_constraint, memory_space=pltpu.HBM)
    shape_w = (taps, taps // 2, 2, cin, lanes)
    following = lax.ppermute(image, "rows", to_previous)
    near, edges = call(
        cut_kernel,
        [hbm],
        [(image.shape, bf16), ((rows, EDGE, cin), bf16)],
        [pltpu.SemaphoreType.DMA((2,))],
        "cut",
    )(in_hbm(image))
    edge = lax.ppermute(edges, "fsdp", swap)
    other_w = lax.ppermute(deconv_weight, "fsdp", swap).reshape(shape_w)
    first_other = lax.ppermute(after(first_weight, edges), "fsdp", swap)
    second_other = lax.ppermute(after(second_weight, edges), "fsdp", swap)
    (own_w,) = call(near_kernel, [hbm], [(shape_w, bf16)], [pltpu.SemaphoreType.DMA(())], "near_weights")(
        in_hbm(after(deconv_weight, edges).reshape(shape_w))
    )
    lines = jnp.concatenate([after(near, own_w), edge], axis=1)
    above = lax.ppermute(lines, "rows", to_next)
    u_line = (2, total, cout)
    xs, u, part, tail, sums = call(
        own_kernel,
        [vmem] * 3,
        [
            ((rows, total, 3 * cin), bf16),
            ((2 * rows - 2, *u_line), bf16),
            (u_line, f32),
            ((2, *u_line), f32),
            ((2, cout), f32),
        ],
        [],
        "deconv_own",
        flops=2 * 2 * (2 * rows - 1) * total * 4 * cin * cout,
    )(lines, own_w, other_w)
    (next_edges,) = call(pick_kernel, [vmem], [((rows, EDGE, cin), bf16)], [], "next_edges")(following)
    next_edge = lax.ppermute(next_edges, "fsdp", swap)
    u_next, xs_next, stats = call(
        next_kernel,
        [vmem] * 6,
        [((2, *u_line), bf16), ((1, total, 3 * cin), bf16), ((8, cout // 2), f32)],
        [],
        "deconv_next",
        flops=2 * 2 * total * 4 * cin * cout,
    )(following, next_edge, tail, sums, own_w, other_w)
    (halo,) = call(
        halo_kernel,
        [vmem] * 8,
        [((4, *u_line), bf16)],
        [pltpu.VMEM((HALO, total, 3 * cin), bf16), pltpu.VMEM((1, total, 3 * cin), bf16)],
        "deconv_halo",
        flops=2 * 2 * 4 * total * 4 * cin * cout,
    )(above, following, next_edge, xs, xs_next, part, own_w, other_w)

    totals = total_over(total_over(stats, "fsdp"), "rows")
    params = jnp.stack([norm_gain, norm_shift, first_bias, second_bias])
    (out,) = call(
        functools.partial(conv_kernel, count),
        [vmem] * 9,
        [((2 * rows, 2 * width, cout), bf16)],
        [
            pltpu.VMEM((2 * rows + 2 * HALO, total, 4 * cout), bf16),
            pltpu.VMEM((2 * rows + 2, total, 4 * cout), bf16),
            pltpu.VMEM((2, 2 * rows, 2 * width, lanes), f32),
        ],
        "convs",
        flops=5 * 10**9,
    )(u, u_next, halo, totals, params, first_weight, first_other, second_weight, second_other)
    return out


def solution(mesh):
    placed = (
        P(("groups", "rows"), "fsdp", None),
        P(None, None, None, "fsdp"),
        P(),
        P(),
        P(None, None, None, "fsdp"),
        P(),
        P(None, None, None, "fsdp"),
        P(),
    )
    return jax.shard_map(
        local,
        mesh=mesh,
        in_specs=placed,
        out_specs=P(("groups", "rows"), "fsdp", None),
        check_vma=False,
    )
```

```python
import functools

import jax
import jax.numpy as jnp
from jax import lax
from jax.experimental import pallas as pl
from jax.experimental.pallas import tpu as pltpu
from jax.sharding import PartitionSpec as P

NORM_GROUPS = 32
HALO = 2
EDGE = 16
LANES = 128
VMEM_BYTES = 24 * 2**20


def silu(v):
    h = 0.5 * v
    return h + h * jnp.tanh(h)


def edge_mask(width):
    column = lax.axis_index("fsdp")
    last = lax.axis_size("fsdp") - 1
    cell = lax.broadcasted_iota(jnp.int32, (width + EDGE, 1), 0) - width
    right = (cell < EDGE // 2) & (column < last)
    left = (cell >= EDGE // 2) & (column > 0)
    return (cell < 0) | right | left


def cut_kernel(image_ref, near_ref, edges_ref, sems):
    width = image_ref.shape[1]
    start = pl.multiple_of((1 - lax.axis_index("fsdp")) * (width - EDGE), EDGE)
    copies = [
        pltpu.make_async_copy(image_ref.at[:, pl.ds(start, EDGE), :], edges_ref, sems.at[0]),
        pltpu.make_async_copy(image_ref, near_ref, sems.at[1]),
    ]
    for copy in copies:
        copy.start()
    for copy in copies:
        copy.wait()


def pick_kernel(lines_ref, edges_ref):
    width = lines_ref.shape[1]
    at_left = lax.axis_index("fsdp") == 0

    @pl.when(at_left)
    def _():
        edges_ref[...] = lines_ref[:, width - EDGE :]

    @pl.when(jnp.logical_not(at_left))
    def _():
        edges_ref[...] = lines_ref[:, :EDGE]


def near_kernel(weight_ref, near_ref, sem):
    copy = pltpu.make_async_copy(weight_ref, near_ref, sem)
    copy.start()
    copy.wait()


def spread_line(out, main, edge, inside=True):
    width, cin = main.shape
    line = jnp.concatenate([main.astype(jnp.float32), edge.astype(jnp.float32)], axis=0)
    line = jnp.where(edge_mask(width) & inside, line, 0.0)
    out[:, 0:cin] = pltpu.roll(line, width + EDGE - 1, 0).astype(jnp.bfloat16)
    out[:, cin : 2 * cin] = line.astype(jnp.bfloat16)
    out[:, 2 * cin : 3 * cin] = pltpu.roll(line, 1, 0).astype(jnp.bfloat16)


def tap_dot(lines, phase, kr, own_w, other_w):
    count, total, lanes = lines.shape
    cin = lanes // 3
    low = (1 - phase) * cin
    weight = jnp.concatenate(
        [ref[kr, :, 1 - phase].reshape(2 * cin, ref.shape[-1]) for ref in (own_w, other_w)], axis=1
    )
    out = jnp.dot(
        lines[:, :, low : low + 2 * cin].reshape(count * total, 2 * cin),
        weight,
        preferred_element_type=jnp.float32,
    )
    return out.reshape(count, total, weight.shape[-1])


def add_sums(line, width):
    values = line[:width].astype(jnp.float32)
    return jnp.concatenate(
        [jnp.sum(values, axis=0, keepdims=True), jnp.sum(values * values, axis=0, keepdims=True)], axis=0
    )


def own_kernel(lines_ref, own_w, other_w, xs_ref, u_ref, part_ref, tail_ref, sums_ref):
    rows, total, _ = lines_ref.shape
    width = total - EDGE
    for row in range(rows):
        spread_line(xs_ref.at[row], lines_ref[row, :width], lines_ref[row, width:])
    first_here = lax.axis_index("rows") == 0
    sums = jnp.zeros((2, u_ref.shape[-1]), jnp.float32)
    for phase in range(2):
        dot = functools.partial(tap_dot, phase=phase, own_w=own_w, other_w=other_w)
        upper = dot(xs_ref[...], kr=1)
        lower = dot(xs_ref[...], kr=3)
        part_ref[phase] = upper[0]
        tail_ref[phase, 1] = lower[rows - 1]
        even = [(upper[row + 1] + lower[row]).astype(jnp.bfloat16) for row in range(rows - 1)]
        upper = dot(xs_ref[...], kr=2)
        lower = dot(xs_ref[1:], kr=0)
        tail_ref[phase, 0] = upper[rows - 1]
        odd = [(upper[row] + lower[row]).astype(jnp.bfloat16) for row in range(rows - 1)]
        for row in range(rows - 1):
            u_ref[2 * row, phase] = odd[row]
            u_ref[2 * row + 1, phase] = even[row]
            sums += add_sums(odd[row], width) + add_sums(even[row], width)
        sums += jnp.where(first_here, add_sums(part_ref[phase].astype(jnp.bfloat16), width), 0.0)
    sums_ref[...] = sums


def next_kernel(next_ref, edge_ref, tail_ref, sums_ref, own_w, other_w, u_ref, xs_ref, stats_ref):
    width = next_ref.shape[1]
    last_here = lax.axis_index("rows") == lax.axis_size("rows") - 1
    spread_line(xs_ref.at[0], next_ref[0], edge_ref[0], jnp.logical_not(last_here))
    column = lax.axis_index("fsdp")
    sums = sums_ref[...]
    for phase in range(2):
        dot = functools.partial(tap_dot, phase=phase, own_w=own_w, other_w=other_w)
        odd = (tail_ref[phase, 0] + dot(xs_ref[...], kr=0)[0]).astype(jnp.bfloat16)
        even = (tail_ref[phase, 1] + dot(xs_ref[...], kr=1)[0]).astype(jnp.bfloat16)
        u_ref[0, phase] = odd
        u_ref[1, phase] = even
        sums += add_sums(odd, width) + jnp.where(last_here, 0.0, add_sums(even, width))
    half = sums.shape[1] // 2
    halves = []
    for row in range(2):
        own, other = sums[row : row + 1, :half], sums[row : row + 1, half:]
        halves += [jnp.where(column == 0, own, other), jnp.where(column == 0, other, own)]
    stats_ref[...] = jnp.concatenate(halves + [jnp.zeros((4, half), jnp.float32)], axis=0)


def halo_kernel(above_ref, next_ref, next_edge_ref, xs_ref, xs_next_ref, part_ref, own_w, other_w, u_ref, xs_above, xs_below):
    width = next_ref.shape[1]
    place = lax.axis_index("rows")
    for row in range(HALO):
        spread_line(xs_above.at[row], above_ref[row, :width], above_ref[row, width:], place > 0)
    spread_line(xs_below.at[0], next_ref[1], next_edge_ref[1], place < lax.axis_size("rows") - 1)
    for phase in range(2):
        dot = functools.partial(tap_dot, phase=phase, own_w=own_w, other_w=other_w)
        outer = dot(xs_above[...], kr=3)
        u_ref[0, phase] = (outer[0] + dot(xs_above[1:2], kr=1)[0]).astype(jnp.bfloat16)
        u_ref[2, phase] = (outer[1] + part_ref[phase]).astype(jnp.bfloat16)
        u_ref[1, phase] = (dot(xs_above[1:2], kr=2)[0] + dot(xs_ref[0:1], kr=0)[0]).astype(jnp.bfloat16)
        u_ref[3, phase] = (dot(xs_next_ref[...], kr=2)[0] + dot(xs_below[...], kr=0)[0]).astype(jnp.bfloat16)


def group_sum(v, width):
    lane = lax.broadcasted_iota(jnp.int32, v.shape, 1)
    size = v.shape[1]
    step = 1
    while step < width:
        v = v + jnp.where(
            (lane & step) == 0, pltpu.roll(v, size - step, 1), pltpu.roll(v, step, 1)
        )
        step *= 2
    return v


def fill(ref, row, even, odd):
    total, channels = even.shape
    ref[row, :, 0:channels] = pltpu.roll(odd, 1, 0).astype(jnp.bfloat16)
    ref[row, :, channels : 2 * channels] = even.astype(jnp.bfloat16)
    ref[row, :, 2 * channels : 3 * channels] = odd.astype(jnp.bfloat16)
    ref[row, :, 3 * channels : 4 * channels] = pltpu.roll(even, total - 1, 0).astype(jnp.bfloat16)


def conv_kernel(
    count, u_ref, u_next_ref, halo_ref, stats_ref, params_ref, own_w1, other_w1, own_w2, other_w2, out_ref, g, act, mixed
):
    early, _, total, cout = u_ref.shape
    main = early + u_next_ref.shape[0]
    lines = main + 2 * HALO
    width = total - EDGE
    half = own_w1.shape[-1]
    column = lax.axis_index("fsdp")
    own_at = pl.multiple_of(column * half, half)
    other_at = pl.multiple_of((1 - column) * half, half)

    def own_first(row):
        low, high = row[:, :half], row[:, half:]
        return jnp.concatenate([jnp.where(column == 0, low, high), jnp.where(column == 0, high, low)], axis=1)

    def kernel_row(a, own, other):
        return jnp.concatenate(
            [
                jnp.concatenate([ref[a, b, pl.ds(at, half), :] for b in range(3) for at in (own_at, other_at)], axis=0)
                for ref in (own, other)
            ],
            axis=1,
        )

    block = stats_ref[...]
    width_group = cout // NORM_GROUPS
    sums = jnp.concatenate([block[0:1], block[1:2]], axis=1)
    squares = jnp.concatenate([block[2:3], block[3:4]], axis=1)
    mean = group_sum(sums, width_group) / count
    spread = group_sum(squares, width_group) / count - mean * mean
    scale = lax.rsqrt(spread + 1e-05) * params_ref[0:1]
    shift = own_first(params_ref[1:2] - mean * scale)
    scale = own_first(scale)

    mask = edge_mask(width)
    place = lax.axis_index("rows")
    last = lax.axis_size("rows") - 1

    def inside(row, beyond):
        if row < beyond:
            return mask & (place > 0)
        if row >= lines - 2 * HALO + beyond:
            return mask & (place < last)
        return mask

    def hidden(row):
        if row < 3:
            source = halo_ref.at[row]
        elif row < 3 + early:
            source = u_ref.at[row - 3]
        elif row < 3 + main:
            source = u_next_ref.at[row - 3 - early]
        else:
            source = halo_ref.at[3]
        seen = inside(row, HALO)
        fill(
            g,
            row,
            *[jnp.where(seen, silu(source[phase].astype(jnp.float32) * scale + shift), 0.0) for phase in range(2)],
        )

    def conv(source, start, size, cells, phase, own, other, bias):
        acc = bias
        for a in range(3):
            acc = acc + jnp.dot(
                source[start + a : start + a + size, 0:cells, phase * cout : (phase + 3) * cout].reshape(
                    size * cells, 3 * cout
                ),
                kernel_row(a, own, other),
                preferred_element_type=jnp.float32,
            )
        return acc.reshape(size, cells, cout)

    chunk = 2
    bias1 = own_first(params_ref[2:3])
    bias2 = own_first(params_ref[3:4])

    def first(start):
        results = [silu(conv(g, start, chunk, total, phase, own_w1, other_w1, bias1)) for phase in range(2)]
        for row in range(chunk):
            seen = inside(start + row, 1)
            fill(act, start + row, *[jnp.where(seen, r[row], 0.0) for r in results])

    def second(start):
        for phase in range(2):
            acc = conv(act, start, chunk, width, phase, own_w2, other_w2, bias2)
            for row in range(chunk):
                for side in range(2):
                    mixed[side, start + row, pl.ds(phase, width, stride=2), :] = acc[
                        row, :, side * half : (side + 1) * half
                    ]
        for row in range(start, start + chunk):
            out_ref[row, :, pl.ds(own_at, half)] = mixed[0, row].astype(jnp.bfloat16)
            out_ref[row, :, pl.ds(other_at, half)] = mixed[1, row].astype(jnp.bfloat16)

    for row in range(chunk):
        hidden(row)
    for start in range(0, lines - 2, chunk):
        for row in range(start + chunk, start + 2 * chunk):
            hidden(row)
        first(start)
        if start >= chunk:
            second(start - chunk)


def total_over(block, axis):
    size = lax.axis_size(axis)
    if size & (size - 1):
        return lax.psum(block, axis)
    steps = [2**n for n in range(size.bit_length() - 1)]
    for step in steps[1:] + steps[:1]:
        block = block + lax.ppermute(block, axis, [(i, i ^ step) for i in range(size)])
    return block


def after(value, *others):
    return lax.optimization_barrier((value, *others))[0]


def local(image, deconv_weight, norm_gain, norm_shift, first_weight, first_bias, second_weight, second_bias):
    rows, width, cin = image.shape
    taps, _, _, lanes = deconv_weight.shape
    columns = lax.axis_size("fsdp")
    cout = lanes * columns
    assert columns == 2 and rows == HALO and width % EDGE == 0 and lanes == LANES
    n_rows = lax.axis_size("rows")
    count = float(2 * rows * n_rows * 2 * width * columns * (cout // NORM_GROUPS))
    swap = [(0, 1), (1, 0)]
    to_next = [(i, (i + 1) % n_rows) for i in range(n_rows)]
    to_previous = [((i + 1) % n_rows, i) for i in range(n_rows)]
    total = width + EDGE
    hbm = pl.BlockSpec(memory_space=pltpu.HBM)
    vmem = pl.BlockSpec(memory_space=pltpu.VMEM)
    bf16, f32 = jnp.bfloat16, jnp.float32

    def call(kernel, ins, outs, scratch, name, flops=0):
        return pl.pallas_call(
            kernel,
            out_shape=tuple(jax.ShapeDtypeStruct(*o) for o in outs),
            in_specs=ins,
            out_specs=(vmem,) * len(outs),
            scratch_shapes=scratch,
            compiler_params=pltpu.CompilerParams(vmem_limit_bytes=VMEM_BYTES),
            cost_estimate=pl.CostEstimate(flops=flops, bytes_accessed=2**21, transcendentals=0),
            name=name,
        )

    in_hbm = functools.partial(pltpu.with_memory_space_constraint, memory_space=pltpu.HBM)
    shape_w = (taps, taps // 2, 2, cin, lanes)
    following = lax.ppermute(image, "rows", to_previous)
    near, edges = call(
        cut_kernel,
        [hbm],
        [(image.shape, bf16), ((rows, EDGE, cin), bf16)],
        [pltpu.SemaphoreType.DMA((2,))],
        "cut",
    )(in_hbm(image))
    edge = lax.ppermute(edges, "fsdp", swap)
    other_w = lax.ppermute(deconv_weight, "fsdp", swap).reshape(shape_w)
    first_other = lax.ppermute(after(first_weight, edges), "fsdp", swap)
    second_other = lax.ppermute(after(second_weight, edges), "fsdp", swap)
    (own_w,) = call(near_kernel, [hbm], [(shape_w, bf16)], [pltpu.SemaphoreType.DMA(())], "near_weights")(
        in_hbm(after(deconv_weight, edges).reshape(shape_w))
    )
    lines = jnp.concatenate([after(near, own_w), edge], axis=1)
    above = lax.ppermute(after(lines, following), "rows", to_next)
    u_line = (2, total, cout)
    xs, u, part, tail, sums = call(
        own_kernel,
        [vmem] * 3,
        [
            ((rows, total, 3 * cin), bf16),
            ((2 * rows - 2, *u_line), bf16),
            (u_line, f32),
            ((2, *u_line), f32),
            ((2, cout), f32),
        ],
        [],
        "deconv_own",
        flops=2 * 2 * (2 * rows - 1) * total * 4 * cin * cout,
    )(lines, own_w, other_w)
    (next_edges,) = call(pick_kernel, [vmem], [((rows, EDGE, cin), bf16)], [], "next_edges")(following)
    next_edge = lax.ppermute(next_edges, "fsdp", swap)
    u_next, xs_next, stats = call(
        next_kernel,
        [vmem] * 6,
        [((2, *u_line), bf16), ((1, total, 3 * cin), bf16), ((8, cout // 2), f32)],
        [],
        "deconv_next",
        flops=2 * 2 * total * 4 * cin * cout,
    )(following, next_edge, tail, sums, own_w, other_w)
    (halo,) = call(
        halo_kernel,
        [vmem] * 8,
        [((4, *u_line), bf16)],
        [pltpu.VMEM((HALO, total, 3 * cin), bf16), pltpu.VMEM((1, total, 3 * cin), bf16)],
        "deconv_halo",
        flops=2 * 2 * 4 * total * 4 * cin * cout,
    )(above, following, next_edge, xs, xs_next, part, own_w, other_w)

    totals = total_over(total_over(stats, "fsdp"), "rows")
    params = jnp.stack([norm_gain, norm_shift, first_bias, second_bias])
    (out,) = call(
        functools.partial(conv_kernel, count),
        [vmem] * 9,
        [((2 * rows, 2 * width, cout), bf16)],
        [
            pltpu.VMEM((2 * rows + 2 * HALO, total, 4 * cout), bf16),
            pltpu.VMEM((2 * rows + 2, total, 4 * cout), bf16),
            pltpu.VMEM((2, 2 * rows, 2 * width, lanes), f32),
        ],
        "convs",
        flops=5 * 10**9,
    )(u, u_next, halo, totals, params, first_weight, first_other, second_weight, second_other)
    return out


def solution(mesh):
    placed = (
        P(("groups", "rows"), "fsdp", None),
        P(None, None, None, "fsdp"),
        P(),
        P(),
        P(None, None, None, "fsdp"),
        P(),
        P(None, None, None, "fsdp"),
        P(),
    )
    return jax.shard_map(
        local,
        mesh=mesh,
        in_specs=placed,
        out_specs=P(("groups", "rows"), "fsdp", None),
        check_vma=False,
    )
```

```python
import functools

import jax
import jax.numpy as jnp
from jax import lax
from jax.experimental import pallas as pl
from jax.experimental.pallas import tpu as pltpu
from jax.sharding import PartitionSpec as P

NORM_GROUPS = 32
HALO = 2
EDGE = 16
LANES = 128
VMEM_BYTES = 24 * 2**20


def silu(v):
    h = 0.5 * v
    return h + h * jnp.tanh(h)


def edge_mask(width):
    column = lax.axis_index("fsdp")
    last = lax.axis_size("fsdp") - 1
    cell = lax.broadcasted_iota(jnp.int32, (width + EDGE, 1), 0) - width
    right = (cell < EDGE // 2) & (column < last)
    left = (cell >= EDGE // 2) & (column > 0)
    return (cell < 0) | right | left


def cut_kernel(image_ref, near_ref, edges_ref, sems):
    width = image_ref.shape[1]
    start = pl.multiple_of((1 - lax.axis_index("fsdp")) * (width - EDGE), EDGE)
    copies = [
        pltpu.make_async_copy(image_ref.at[:, pl.ds(start, EDGE), :], edges_ref, sems.at[0]),
        pltpu.make_async_copy(image_ref, near_ref, sems.at[1]),
    ]
    for copy in copies:
        copy.start()
    for copy in copies:
        copy.wait()


def pick_kernel(lines_ref, edges_ref):
    width = lines_ref.shape[1]
    at_left = lax.axis_index("fsdp") == 0

    @pl.when(at_left)
    def _():
        edges_ref[...] = lines_ref[:, width - EDGE :]

    @pl.when(jnp.logical_not(at_left))
    def _():
        edges_ref[...] = lines_ref[:, :EDGE]


def near_kernel(weight_ref, near_ref, sem):
    copy = pltpu.make_async_copy(weight_ref, near_ref, sem)
    copy.start()
    copy.wait()


def spread_line(out, main, edge, inside=True):
    width, cin = main.shape
    line = jnp.concatenate([main.astype(jnp.float32), edge.astype(jnp.float32)], axis=0)
    line = jnp.where(edge_mask(width) & inside, line, 0.0)
    out[:, 0:cin] = pltpu.roll(line, width + EDGE - 1, 0).astype(jnp.bfloat16)
    out[:, cin : 2 * cin] = line.astype(jnp.bfloat16)
    out[:, 2 * cin : 3 * cin] = pltpu.roll(line, 1, 0).astype(jnp.bfloat16)


def tap_dot(lines, phase, kr, own_w, other_w):
    count, total, lanes = lines.shape
    cin = lanes // 3
    low = (1 - phase) * cin
    weight = jnp.concatenate(
        [ref[kr, :, 1 - phase].reshape(2 * cin, ref.shape[-1]) for ref in (own_w, other_w)], axis=1
    )
    out = jnp.dot(
        lines[:, :, low : low + 2 * cin].reshape(count * total, 2 * cin),
        weight,
        preferred_element_type=jnp.float32,
    )
    return out.reshape(count, total, weight.shape[-1])


def add_sums(line, width):
    values = line[:width].astype(jnp.float32)
    return jnp.concatenate(
        [jnp.sum(values, axis=0, keepdims=True), jnp.sum(values * values, axis=0, keepdims=True)], axis=0
    )


def own_kernel(lines_ref, own_w, other_w, xs_ref, u_ref, part_ref, tail_ref, sums_ref):
    rows, total, _ = lines_ref.shape
    width = total - EDGE
    for row in range(rows):
        spread_line(xs_ref.at[row], lines_ref[row, :width], lines_ref[row, width:])
    first_here = lax.axis_index("rows") == 0
    sums = jnp.zeros((2, u_ref.shape[-1]), jnp.float32)
    for phase in range(2):
        dot = functools.partial(tap_dot, phase=phase, own_w=own_w, other_w=other_w)
        upper = dot(xs_ref[...], kr=1)
        lower = dot(xs_ref[...], kr=3)
        part_ref[phase] = upper[0]
        tail_ref[phase, 1] = lower[rows - 1]
        even = [(upper[row + 1] + lower[row]).astype(jnp.bfloat16) for row in range(rows - 1)]
        upper = dot(xs_ref[...], kr=2)
        lower = dot(xs_ref[1:], kr=0)
        tail_ref[phase, 0] = upper[rows - 1]
        odd = [(upper[row] + lower[row]).astype(jnp.bfloat16) for row in range(rows - 1)]
        for row in range(rows - 1):
            u_ref[2 * row, phase] = odd[row]
            u_ref[2 * row + 1, phase] = even[row]
            sums += add_sums(odd[row], width) + add_sums(even[row], width)
        sums += jnp.where(first_here, add_sums(part_ref[phase].astype(jnp.bfloat16), width), 0.0)
    sums_ref[...] = sums


def next_kernel(next_ref, edge_ref, tail_ref, sums_ref, own_w, other_w, u_ref, xs_ref, stats_ref):
    width = next_ref.shape[1]
    last_here = lax.axis_index("rows") == lax.axis_size("rows") - 1
    spread_line(xs_ref.at[0], next_ref[0], edge_ref[0], jnp.logical_not(last_here))
    column = lax.axis_index("fsdp")
    sums = sums_ref[...]
    for phase in range(2):
        dot = functools.partial(tap_dot, phase=phase, own_w=own_w, other_w=other_w)
        odd = (tail_ref[phase, 0] + dot(xs_ref[...], kr=0)[0]).astype(jnp.bfloat16)
        even = (tail_ref[phase, 1] + dot(xs_ref[...], kr=1)[0]).astype(jnp.bfloat16)
        u_ref[0, phase] = odd
        u_ref[1, phase] = even
        sums += add_sums(odd, width) + jnp.where(last_here, 0.0, add_sums(even, width))
    half = sums.shape[1] // 2
    halves = []
    for row in range(2):
        own, other = sums[row : row + 1, :half], sums[row : row + 1, half:]
        halves += [jnp.where(column == 0, own, other), jnp.where(column == 0, other, own)]
    stats_ref[...] = jnp.concatenate(halves + [jnp.zeros((4, half), jnp.float32)], axis=0)


def halo_kernel(above_ref, next_ref, next_edge_ref, xs_ref, xs_next_ref, part_ref, own_w, other_w, u_ref, xs_above, xs_below):
    width = next_ref.shape[1]
    place = lax.axis_index("rows")
    for row in range(HALO):
        spread_line(xs_above.at[row], above_ref[row, :width], above_ref[row, width:], place > 0)
    spread_line(xs_below.at[0], next_ref[1], next_edge_ref[1], place < lax.axis_size("rows") - 1)
    for phase in range(2):
        dot = functools.partial(tap_dot, phase=phase, own_w=own_w, other_w=other_w)
        outer = dot(xs_above[...], kr=3)
        u_ref[0, phase] = (outer[0] + dot(xs_above[1:2], kr=1)[0]).astype(jnp.bfloat16)
        u_ref[2, phase] = (outer[1] + part_ref[phase]).astype(jnp.bfloat16)
        u_ref[1, phase] = (dot(xs_above[1:2], kr=2)[0] + dot(xs_ref[0:1], kr=0)[0]).astype(jnp.bfloat16)
        u_ref[3, phase] = (dot(xs_next_ref[...], kr=2)[0] + dot(xs_below[...], kr=0)[0]).astype(jnp.bfloat16)


def group_sum(v, width):
    lane = lax.broadcasted_iota(jnp.int32, v.shape, 1)
    size = v.shape[1]
    step = 1
    while step < width:
        v = v + jnp.where(
            (lane & step) == 0, pltpu.roll(v, size - step, 1), pltpu.roll(v, step, 1)
        )
        step *= 2
    return v


def fill(ref, row, even, odd):
    total, channels = even.shape
    ref[row, :, 0:channels] = pltpu.roll(odd, 1, 0).astype(jnp.bfloat16)
    ref[row, :, channels : 2 * channels] = even.astype(jnp.bfloat16)
    ref[row, :, 2 * channels : 3 * channels] = odd.astype(jnp.bfloat16)
    ref[row, :, 3 * channels : 4 * channels] = pltpu.roll(even, total - 1, 0).astype(jnp.bfloat16)


def conv_kernel(
    count, u_ref, u_next_ref, halo_ref, mine_ref, passed_ref, params_ref, own_w1, other_w1, own_w2, other_w2, out_ref, g, act, mixed
):
    early, _, total, cout = u_ref.shape
    main = early + u_next_ref.shape[0]
    lines = main + 2 * HALO
    width = total - EDGE
    half = own_w1.shape[-1]
    column = lax.axis_index("fsdp")
    own_at = pl.multiple_of(column * half, half)
    other_at = pl.multiple_of((1 - column) * half, half)

    def own_first(row):
        low, high = row[:, :half], row[:, half:]
        return jnp.concatenate([jnp.where(column == 0, low, high), jnp.where(column == 0, high, low)], axis=1)

    def kernel_row(a, own, other):
        return jnp.concatenate(
            [
                jnp.concatenate([ref[a, b, pl.ds(at, half), :] for b in range(3) for at in (own_at, other_at)], axis=0)
                for ref in (own, other)
            ],
            axis=1,
        )

    block = jnp.where(column == 1, mine_ref[...], passed_ref[...])
    width_group = cout // NORM_GROUPS
    sums = jnp.concatenate([block[0:1], block[1:2]], axis=1)
    squares = jnp.concatenate([block[2:3], block[3:4]], axis=1)
    mean = group_sum(sums, width_group) / count
    spread = group_sum(squares, width_group) / count - mean * mean
    scale = lax.rsqrt(spread + 1e-05) * params_ref[0:1]
    shift = own_first(params_ref[1:2] - mean * scale)
    scale = own_first(scale)

    mask = edge_mask(width)
    place = lax.axis_index("rows")
    last = lax.axis_size("rows") - 1

    def inside(row, beyond):
        if row < beyond:
            return mask & (place > 0)
        if row >= lines - 2 * HALO + beyond:
            return mask & (place < last)
        return mask

    def hidden(row):
        if row < 3:
            source = halo_ref.at[row]
        elif row < 3 + early:
            source = u_ref.at[row - 3]
        elif row < 3 + main:
            source = u_next_ref.at[row - 3 - early]
        else:
            source = halo_ref.at[3]
        seen = inside(row, HALO)
        fill(
            g,
            row,
            *[jnp.where(seen, silu(source[phase].astype(jnp.float32) * scale + shift), 0.0) for phase in range(2)],
        )

    def conv(source, start, size, cells, phase, own, other, bias):
        acc = bias
        for a in range(3):
            acc = acc + jnp.dot(
                source[start + a : start + a + size, 0:cells, phase * cout : (phase + 3) * cout].reshape(
                    size * cells, 3 * cout
                ),
                kernel_row(a, own, other),
                preferred_element_type=jnp.float32,
            )
        return acc.reshape(size, cells, cout)

    chunk = 2
    bias1 = own_first(params_ref[2:3])
    bias2 = own_first(params_ref[3:4])

    def first(start):
        results = [silu(conv(g, start, chunk, total, phase, own_w1, other_w1, bias1)) for phase in range(2)]
        for row in range(chunk):
            seen = inside(start + row, 1)
            fill(act, start + row, *[jnp.where(seen, r[row], 0.0) for r in results])

    def second(start):
        for phase in range(2):
            acc = conv(act, start, chunk, width, phase, own_w2, other_w2, bias2)
            for row in range(chunk):
                for side in range(2):
                    mixed[side, start + row, pl.ds(phase, width, stride=2), :] = acc[
                        row, :, side * half : (side + 1) * half
                    ]
        for row in range(start, start + chunk):
            out_ref[row, :, pl.ds(own_at, half)] = mixed[0, row].astype(jnp.bfloat16)
            out_ref[row, :, pl.ds(other_at, half)] = mixed[1, row].astype(jnp.bfloat16)

    for row in range(chunk):
        hidden(row)
    for start in range(0, lines - 2, chunk):
        for row in range(start + chunk, start + 2 * chunk):
            hidden(row)
        first(start)
        if start >= chunk:
            second(start - chunk)


def total_over(block, last):
    size = lax.axis_size("rows")
    assert size & (size - 1) == 0
    block = block + lax.ppermute(block, "fsdp", [(0, 1), (1, 0)])
    steps = [2**n for n in range(size.bit_length() - 1)]
    for step in steps[1:] + steps[:1]:
        pairs = [(2 * i, 2 * i) for i in range(size)] + [(2 * i + 1, 2 * (i ^ step) + 1) for i in range(size)]
        block = block + lax.ppermute(block, ("rows", "fsdp"), pairs)
    return block, lax.ppermute(after(block, last), "fsdp", [(0, 1), (1, 0)])


def after(value, *others):
    return lax.optimization_barrier((value, *others))[0]


def local(image, deconv_weight, norm_gain, norm_shift, first_weight, first_bias, second_weight, second_bias):
    rows, width, cin = image.shape
    taps, _, _, lanes = deconv_weight.shape
    columns = lax.axis_size("fsdp")
    cout = lanes * columns
    assert columns == 2 and rows == HALO and width % EDGE == 0 and lanes == LANES
    n_rows = lax.axis_size("rows")
    count = float(2 * rows * n_rows * 2 * width * columns * (cout // NORM_GROUPS))
    swap = [(0, 1), (1, 0)]
    to_next = [(i, (i + 1) % n_rows) for i in range(n_rows)]
    to_previous = [((i + 1) % n_rows, i) for i in range(n_rows)]
    total = width + EDGE
    hbm = pl.BlockSpec(memory_space=pltpu.HBM)
    vmem = pl.BlockSpec(memory_space=pltpu.VMEM)
    bf16, f32 = jnp.bfloat16, jnp.float32

    def call(kernel, ins, outs, scratch, name, flops=0):
        return pl.pallas_call(
            kernel,
            out_shape=tuple(jax.ShapeDtypeStruct(*o) for o in outs),
            in_specs=ins,
            out_specs=(vmem,) * len(outs),
            scratch_shapes=scratch,
            compiler_params=pltpu.CompilerParams(vmem_limit_bytes=VMEM_BYTES),
            cost_estimate=pl.CostEstimate(flops=flops, bytes_accessed=2**21, transcendentals=0),
            name=name,
        )

    in_hbm = functools.partial(pltpu.with_memory_space_constraint, memory_space=pltpu.HBM)
    shape_w = (taps, taps // 2, 2, cin, lanes)
    following = lax.ppermute(image, "rows", to_previous)
    near, edges = call(
        cut_kernel,
        [hbm],
        [(image.shape, bf16), ((rows, EDGE, cin), bf16)],
        [pltpu.SemaphoreType.DMA((2,))],
        "cut",
    )(in_hbm(image))
    edge = lax.ppermute(edges, "fsdp", swap)
    other_w = lax.ppermute(deconv_weight, "fsdp", swap).reshape(shape_w)
    first_other = lax.ppermute(after(first_weight, edges), "fsdp", swap)
    second_other = lax.ppermute(after(second_weight, edges), "fsdp", swap)
    (own_w,) = call(near_kernel, [hbm], [(shape_w, bf16)], [pltpu.SemaphoreType.DMA(())], "near_weights")(
        in_hbm(after(deconv_weight, edges).reshape(shape_w))
    )
    lines = jnp.concatenate([after(near, own_w), edge], axis=1)
    above = lax.ppermute(after(lines, following), "rows", to_next)
    u_line = (2, total, cout)
    xs, u, part, tail, sums = call(
        own_kernel,
        [vmem] * 3,
        [
            ((rows, total, 3 * cin), bf16),
            ((2 * rows - 2, *u_line), bf16),
            (u_line, f32),
            ((2, *u_line), f32),
            ((2, cout), f32),
        ],
        [],
        "deconv_own",
        flops=2 * 2 * (2 * rows - 1) * total * 4 * cin * cout,
    )(lines, own_w, other_w)
    (next_edges,) = call(pick_kernel, [vmem], [((rows, EDGE, cin), bf16)], [], "next_edges")(following)
    next_edge = lax.ppermute(next_edges, "fsdp", swap)
    u_next, xs_next, stats = call(
        next_kernel,
        [vmem] * 6,
        [((2, *u_line), bf16), ((1, total, 3 * cin), bf16), ((8, cout // 2), f32)],
        [],
        "deconv_next",
        flops=2 * 2 * total * 4 * cin * cout,
    )(following, next_edge, tail, sums, own_w, other_w)
    (halo,) = call(
        halo_kernel,
        [vmem] * 8,
        [((4, *u_line), bf16)],
        [pltpu.VMEM((HALO, total, 3 * cin), bf16), pltpu.VMEM((1, total, 3 * cin), bf16)],
        "deconv_halo",
        flops=2 * 2 * 4 * total * 4 * cin * cout,
    )(above, following, next_edge, xs, xs_next, part, own_w, other_w)

    mine, passed = total_over(stats, halo)
    params = jnp.stack([norm_gain, norm_shift, first_bias, second_bias])
    (out,) = call(
        functools.partial(conv_kernel, count),
        [vmem] * 10,
        [((2 * rows, 2 * width, cout), bf16)],
        [
            pltpu.VMEM((2 * rows + 2 * HALO, total, 4 * cout), bf16),
            pltpu.VMEM((2 * rows + 2, total, 4 * cout), bf16),
            pltpu.VMEM((2, 2 * rows, 2 * width, lanes), f32),
        ],
        "convs",
        flops=5 * 10**9,
    )(u, u_next, halo, mine, passed, params, first_weight, first_other, second_weight, second_other)
    return out


def solution(mesh):
    placed = (
        P(("groups", "rows"), "fsdp", None),
        P(None, None, None, "fsdp"),
        P(),
        P(),
        P(None, None, None, "fsdp"),
        P(),
        P(None, None, None, "fsdp"),
        P(),
    )
    return jax.shard_map(
        local,
        mesh=mesh,
        in_specs=placed,
        out_specs=P(("groups", "rows"), "fsdp", None),
        check_vma=False,
    )
```

```python
import functools

import jax
import jax.numpy as jnp
from jax import lax
from jax.experimental import pallas as pl
from jax.experimental.pallas import tpu as pltpu
from jax.sharding import PartitionSpec as P

NORM_GROUPS = 32
HALO = 2
EDGE = 16
LANES = 128
VMEM_BYTES = 24 * 2**20


def silu(v):
    h = 0.5 * v
    return h + h * jnp.tanh(h)


def edge_mask(width):
    column = lax.axis_index("fsdp")
    last = lax.axis_size("fsdp") - 1
    cell = lax.broadcasted_iota(jnp.int32, (width + EDGE, 1), 0) - width
    right = (cell < EDGE // 2) & (column < last)
    left = (cell >= EDGE // 2) & (column > 0)
    return (cell < 0) | right | left


def cut_kernel(image_ref, near_ref, edges_ref, sems):
    width = image_ref.shape[1]
    start = pl.multiple_of((1 - lax.axis_index("fsdp")) * (width - EDGE), EDGE)
    copies = [
        pltpu.make_async_copy(image_ref.at[:, pl.ds(start, EDGE), :], edges_ref, sems.at[0]),
        pltpu.make_async_copy(image_ref, near_ref, sems.at[1]),
    ]
    for copy in copies:
        copy.start()
    for copy in copies:
        copy.wait()


def pick_kernel(lines_ref, edges_ref):
    width = lines_ref.shape[1]
    at_left = lax.axis_index("fsdp") == 0

    @pl.when(at_left)
    def _():
        edges_ref[...] = lines_ref[:, width - EDGE :]

    @pl.when(jnp.logical_not(at_left))
    def _():
        edges_ref[...] = lines_ref[:, :EDGE]


def near_kernel(weight_ref, near_ref, sem):
    copy = pltpu.make_async_copy(weight_ref, near_ref, sem)
    copy.start()
    copy.wait()


def spread_line(out, main, edge):
    width, cin = main.shape
    line = jnp.concatenate([main.astype(jnp.float32), edge.astype(jnp.float32)], axis=0)
    line = jnp.where(edge_mask(width), line, 0.0)
    out[:, 0:cin] = pltpu.roll(line, width + EDGE - 1, 0).astype(jnp.bfloat16)
    out[:, cin : 2 * cin] = line.astype(jnp.bfloat16)
    out[:, 2 * cin : 3 * cin] = pltpu.roll(line, 1, 0).astype(jnp.bfloat16)


def tap_dot(lines, phase, kr, own_w, other_w):
    count, total, lanes = lines.shape
    cin = lanes // 3
    low = (1 - phase) * cin
    weight = jnp.concatenate(
        [ref[kr, :, 1 - phase].reshape(2 * cin, ref.shape[-1]) for ref in (own_w, other_w)], axis=1
    )
    out = jnp.dot(
        lines[:, :, low : low + 2 * cin].reshape(count * total, 2 * cin),
        weight,
        preferred_element_type=jnp.float32,
    )
    return out.reshape(count, total, weight.shape[-1])


def add_sums(line, width):
    values = line[:width].astype(jnp.float32)
    return jnp.concatenate(
        [jnp.sum(values, axis=0, keepdims=True), jnp.sum(values * values, axis=0, keepdims=True)], axis=0
    )


def own_kernel(lines_ref, own_w, other_w, xs_ref, u_ref, part_ref, tail_ref, sums_ref):
    rows, total, _ = lines_ref.shape
    width = total - EDGE
    for row in range(rows):
        spread_line(xs_ref.at[row], lines_ref[row, :width], lines_ref[row, width:])
    first_here = lax.axis_index("rows") == 0
    sums = jnp.zeros((2, u_ref.shape[-1]), jnp.float32)
    for phase in range(2):
        dot = functools.partial(tap_dot, phase=phase, own_w=own_w, other_w=other_w)
        upper = dot(xs_ref[...], kr=1)
        lower = dot(xs_ref[...], kr=3)
        part_ref[phase] = upper[0]
        tail_ref[phase, 1] = lower[rows - 1]
        even = [(upper[row + 1] + lower[row]).astype(jnp.bfloat16) for row in range(rows - 1)]
        upper = dot(xs_ref[...], kr=2)
        lower = dot(xs_ref[1:], kr=0)
        tail_ref[phase, 0] = upper[rows - 1]
        odd = [(upper[row] + lower[row]).astype(jnp.bfloat16) for row in range(rows - 1)]
        for row in range(rows - 1):
            u_ref[2 * row, phase] = odd[row]
            u_ref[2 * row + 1, phase] = even[row]
            sums += add_sums(odd[row], width) + add_sums(even[row], width)
        sums += jnp.where(first_here, add_sums(part_ref[phase].astype(jnp.bfloat16), width), 0.0)
    sums_ref[...] = sums


def next_kernel(next_ref, edge_ref, tail_ref, sums_ref, own_w, other_w, u_ref, xs_ref, stats_ref):
    width = next_ref.shape[1]
    last_here = lax.axis_index("rows") == lax.axis_size("rows") - 1
    spread_line(xs_ref.at[0], next_ref[0], edge_ref[0])
    column = lax.axis_index("fsdp")
    sums = sums_ref[...]
    for phase in range(2):
        dot = functools.partial(tap_dot, phase=phase, own_w=own_w, other_w=other_w)
        odd = (tail_ref[phase, 0] + dot(xs_ref[...], kr=0)[0]).astype(jnp.bfloat16)
        even = (tail_ref[phase, 1] + dot(xs_ref[...], kr=1)[0]).astype(jnp.bfloat16)
        u_ref[0, phase] = odd
        u_ref[1, phase] = even
        sums += add_sums(odd, width) + jnp.where(last_here, 0.0, add_sums(even, width))
    half = sums.shape[1] // 2
    halves = []
    for row in range(2):
        own, other = sums[row : row + 1, :half], sums[row : row + 1, half:]
        halves += [jnp.where(column == 0, own, other), jnp.where(column == 0, other, own)]
    stats_ref[...] = jnp.concatenate(halves + [jnp.zeros((4, half), jnp.float32)], axis=0)


def halo_kernel(above_ref, next_ref, next_edge_ref, xs_ref, xs_next_ref, part_ref, own_w, other_w, u_ref, xs_above, xs_below):
    width = next_ref.shape[1]
    for row in range(HALO):
        spread_line(xs_above.at[row], above_ref[row, :width], above_ref[row, width:])
    spread_line(xs_below.at[0], next_ref[1], next_edge_ref[1])
    for phase in range(2):
        dot = functools.partial(tap_dot, phase=phase, own_w=own_w, other_w=other_w)
        outer = dot(xs_above[...], kr=3)
        u_ref[0, phase] = (outer[0] + dot(xs_above[1:2], kr=1)[0]).astype(jnp.bfloat16)
        u_ref[2, phase] = (outer[1] + part_ref[phase]).astype(jnp.bfloat16)
        u_ref[1, phase] = (dot(xs_above[1:2], kr=2)[0] + dot(xs_ref[0:1], kr=0)[0]).astype(jnp.bfloat16)
        u_ref[3, phase] = (dot(xs_next_ref[...], kr=2)[0] + dot(xs_below[...], kr=0)[0]).astype(jnp.bfloat16)


def group_sum(v, width):
    lane = lax.broadcasted_iota(jnp.int32, v.shape, 1)
    size = v.shape[1]
    step = 1
    while step < width:
        v = v + jnp.where(
            (lane & step) == 0, pltpu.roll(v, size - step, 1), pltpu.roll(v, step, 1)
        )
        step *= 2
    return v


def fill(ref, row, even, odd):
    total, channels = even.shape
    ref[row, :, 0:channels] = pltpu.roll(odd, 1, 0).astype(jnp.bfloat16)
    ref[row, :, channels : 2 * channels] = even.astype(jnp.bfloat16)
    ref[row, :, 2 * channels : 3 * channels] = odd.astype(jnp.bfloat16)
    ref[row, :, 3 * channels : 4 * channels] = pltpu.roll(even, total - 1, 0).astype(jnp.bfloat16)


def conv_kernel(
    count, u_ref, u_next_ref, halo_ref, stats_ref, params_ref, own_w1, other_w1, own_w2, other_w2, out_ref, g, act, mixed
):
    early, _, total, cout = u_ref.shape
    main = early + u_next_ref.shape[0]
    lines = main + 2 * HALO
    width = total - EDGE
    half = own_w1.shape[-1]
    column = lax.axis_index("fsdp")
    own_at = pl.multiple_of(column * half, half)
    other_at = pl.multiple_of((1 - column) * half, half)

    def own_first(row):
        low, high = row[:, :half], row[:, half:]
        return jnp.concatenate([jnp.where(column == 0, low, high), jnp.where(column == 0, high, low)], axis=1)

    def kernel_row(a, own, other):
        return jnp.concatenate(
            [
                jnp.concatenate([ref[a, b, pl.ds(at, half), :] for b in range(3) for at in (own_at, other_at)], axis=0)
                for ref in (own, other)
            ],
            axis=1,
        )

    block = stats_ref[...]
    width_group = cout // NORM_GROUPS
    sums = jnp.concatenate([block[0:1], block[1:2]], axis=1)
    squares = jnp.concatenate([block[2:3], block[3:4]], axis=1)
    mean = group_sum(sums, width_group) / count
    spread = group_sum(squares, width_group) / count - mean * mean
    scale = lax.rsqrt(spread + 1e-05) * params_ref[0:1]
    shift = own_first(params_ref[1:2] - mean * scale)
    scale = own_first(scale)

    mask = edge_mask(width)
    place = lax.axis_index("rows")
    last = lax.axis_size("rows") - 1

    def inside(row, beyond):
        if row < beyond:
            return mask & (place > 0)
        if row >= lines - 2 * HALO + beyond:
            return mask & (place < last)
        return mask

    def hidden(row):
        if row < 3:
            source = halo_ref.at[row]
        elif row < 3 + early:
            source = u_ref.at[row - 3]
        elif row < 3 + main:
            source = u_next_ref.at[row - 3 - early]
        else:
            source = halo_ref.at[3]
        seen = inside(row, HALO)
        fill(
            g,
            row,
            *[jnp.where(seen, silu(source[phase].astype(jnp.float32) * scale + shift), 0.0) for phase in range(2)],
        )

    def conv(source, start, size, cells, phase, own, other, bias):
        acc = bias
        for a in range(3):
            acc = acc + jnp.dot(
                source[start + a : start + a + size, 0:cells, phase * cout : (phase + 3) * cout].reshape(
                    size * cells, 3 * cout
                ),
                kernel_row(a, own, other),
                preferred_element_type=jnp.float32,
            )
        return acc.reshape(size, cells, cout)

    chunk = 2
    bias1 = own_first(params_ref[2:3])
    bias2 = own_first(params_ref[3:4])

    def first(start):
        results = [silu(conv(g, start, chunk, total, phase, own_w1, other_w1, bias1)) for phase in range(2)]
        for row in range(chunk):
            seen = inside(start + row, 1)
            fill(act, start + row, *[jnp.where(seen, r[row], 0.0) for r in results])

    def second(start):
        for phase in range(2):
            acc = conv(act, start, chunk, width, phase, own_w2, other_w2, bias2)
            for row in range(chunk):
                for side in range(2):
                    mixed[side, start + row, pl.ds(phase, width, stride=2), :] = acc[
                        row, :, side * half : (side + 1) * half
                    ]
        for row in range(start, start + chunk):
            out_ref[row, :, pl.ds(own_at, half)] = mixed[0, row].astype(jnp.bfloat16)
            out_ref[row, :, pl.ds(other_at, half)] = mixed[1, row].astype(jnp.bfloat16)

    for row in range(chunk):
        hidden(row)
    for start in range(0, lines - 2, chunk):
        for row in range(start + chunk, start + 2 * chunk):
            hidden(row)
        first(start)
        if start >= chunk:
            second(start - chunk)


def total_over(block, axis):
    size = lax.axis_size(axis)
    if size & (size - 1):
        return lax.psum(block, axis)
    steps = [2**n for n in range(size.bit_length() - 1)]
    for step in steps[1:] + steps[:1]:
        block = block + lax.ppermute(block, axis, [(i, i ^ step) for i in range(size)])
    return block


def after(value, *others):
    return lax.optimization_barrier((value, *others))[0]


def local(image, deconv_weight, norm_gain, norm_shift, first_weight, first_bias, second_weight, second_bias):
    rows, width, cin = image.shape
    taps, _, _, lanes = deconv_weight.shape
    columns = lax.axis_size("fsdp")
    cout = lanes * columns
    assert columns == 2 and rows == HALO and width % EDGE == 0 and lanes == LANES
    n_rows = lax.axis_size("rows")
    count = float(2 * rows * n_rows * 2 * width * columns * (cout // NORM_GROUPS))
    swap = [(0, 1), (1, 0)]
    to_next = [(i, i + 1) for i in range(n_rows - 1)]
    to_previous = [(i + 1, i) for i in range(n_rows - 1)]
    total = width + EDGE
    hbm = pl.BlockSpec(memory_space=pltpu.HBM)
    vmem = pl.BlockSpec(memory_space=pltpu.VMEM)
    bf16, f32 = jnp.bfloat16, jnp.float32

    def call(kernel, ins, outs, scratch, name, flops=0):
        return pl.pallas_call(
            kernel,
            out_shape=tuple(jax.ShapeDtypeStruct(*o) for o in outs),
            in_specs=ins,
            out_specs=(vmem,) * len(outs),
            scratch_shapes=scratch,
            compiler_params=pltpu.CompilerParams(vmem_limit_bytes=VMEM_BYTES),
            cost_estimate=pl.CostEstimate(flops=flops, bytes_accessed=2**21, transcendentals=0),
            name=name,
        )

    in_hbm = functools.partial(pltpu.with_memory_space_constraint, memory_space=pltpu.HBM)
    shape_w = (taps, taps // 2, 2, cin, lanes)
    following = lax.ppermute(image, "rows", to_previous)
    near, edges = call(
        cut_kernel,
        [hbm],
        [(image.shape, bf16), ((rows, EDGE, cin), bf16)],
        [pltpu.SemaphoreType.DMA((2,))],
        "cut",
    )(in_hbm(image))
    edge = lax.ppermute(edges, "fsdp", swap)
    other_w = lax.ppermute(deconv_weight, "fsdp", swap).reshape(shape_w)
    first_other = lax.ppermute(after(first_weight, edges), "fsdp", swap)
    second_other = lax.ppermute(after(second_weight, edges), "fsdp", swap)
    (own_w,) = call(near_kernel, [hbm], [(shape_w, bf16)], [pltpu.SemaphoreType.DMA(())], "near_weights")(
        in_hbm(after(deconv_weight, edges).reshape(shape_w))
    )
    lines = jnp.concatenate([after(near, own_w), edge], axis=1)
    above = lax.ppermute(lines, "rows", to_next)
    u_line = (2, total, cout)
    xs, u, part, tail, sums = call(
        own_kernel,
        [vmem] * 3,
        [
            ((rows, total, 3 * cin), bf16),
            ((2 * rows - 2, *u_line), bf16),
            (u_line, f32),
            ((2, *u_line), f32),
            ((2, cout), f32),
        ],
        [],
        "deconv_own",
        flops=2 * 2 * (2 * rows - 1) * total * 4 * cin * cout,
    )(lines, own_w, other_w)
    (next_edges,) = call(pick_kernel, [vmem], [((rows, EDGE, cin), bf16)], [], "next_edges")(following)
    next_edge = lax.ppermute(next_edges, "fsdp", swap)
    u_next, xs_next, stats = call(
        next_kernel,
        [vmem] * 6,
        [((2, *u_line), bf16), ((1, total, 3 * cin), bf16), ((8, cout // 2), f32)],
        [],
        "deconv_next",
        flops=2 * 2 * total * 4 * cin * cout,
    )(following, next_edge, tail, sums, own_w, other_w)
    (halo,) = call(
        halo_kernel,
        [vmem] * 8,
        [((4, *u_line), bf16)],
        [pltpu.VMEM((HALO, total, 3 * cin), bf16), pltpu.VMEM((1, total, 3 * cin), bf16)],
        "deconv_halo",
        flops=2 * 2 * 4 * total * 4 * cin * cout,
    )(above, following, next_edge, xs, xs_next, part, own_w, other_w)

    totals = total_over(total_over(stats, "fsdp"), "rows")
    params = jnp.stack([norm_gain, norm_shift, first_bias, second_bias])
    (out,) = call(
        functools.partial(conv_kernel, count),
        [vmem] * 9,
        [((2 * rows, 2 * width, cout), bf16)],
        [
            pltpu.VMEM((2 * rows + 2 * HALO, total, 4 * cout), bf16),
            pltpu.VMEM((2 * rows + 2, total, 4 * cout), bf16),
            pltpu.VMEM((2, 2 * rows, 2 * width, lanes), f32),
        ],
        "convs",
        flops=5 * 10**9,
    )(u, u_next, halo, totals, params, first_weight, first_other, second_weight, second_other)
    return out


def solution(mesh):
    placed = (
        P(("groups", "rows"), "fsdp", None),
        P(None, None, None, "fsdp"),
        P(),
        P(),
        P(None, None, None, "fsdp"),
        P(),
        P(None, None, None, "fsdp"),
        P(),
    )
    return jax.shard_map(
        local,
        mesh=mesh,
        in_specs=placed,
        out_specs=P(("groups", "rows"), "fsdp", None),
        check_vma=False,
    )
```

```python
import functools

import jax
import jax.numpy as jnp
from jax import lax
from jax.experimental import pallas as pl
from jax.experimental.pallas import tpu as pltpu
from jax.sharding import PartitionSpec as P

NORM_GROUPS = 32
HALO = 2
EDGE = 16
LANES = 128
VMEM_BYTES = 24 * 2**20


def silu_of_half(h):
    return h + h * jnp.tanh(h)


def edge_mask(width):
    column = lax.axis_index("fsdp")
    last = lax.axis_size("fsdp") - 1
    cell = lax.broadcasted_iota(jnp.int32, (width + EDGE, 1), 0) - width
    right = (cell < EDGE // 2) & (column < last)
    left = (cell >= EDGE // 2) & (column > 0)
    return (cell < 0) | right | left


def cut_kernel(image_ref, near_ref, edges_ref, sems):
    width = image_ref.shape[1]
    start = pl.multiple_of((1 - lax.axis_index("fsdp")) * (width - EDGE), EDGE)
    copies = [
        pltpu.make_async_copy(image_ref.at[:, pl.ds(start, EDGE), :], edges_ref, sems.at[0]),
        pltpu.make_async_copy(image_ref, near_ref, sems.at[1]),
    ]
    for copy in copies:
        copy.start()
    for copy in copies:
        copy.wait()


def pick_kernel(lines_ref, edges_ref):
    width = lines_ref.shape[1]
    at_left = lax.axis_index("fsdp") == 0

    @pl.when(at_left)
    def _():
        edges_ref[...] = lines_ref[:, width - EDGE :]

    @pl.when(jnp.logical_not(at_left))
    def _():
        edges_ref[...] = lines_ref[:, :EDGE]


def near_kernel(weight_ref, near_ref, sem):
    copy = pltpu.make_async_copy(weight_ref, near_ref, sem)
    copy.start()
    copy.wait()


def spread_line(out, main, edge):
    width, cin = main.shape
    line = jnp.concatenate([main.astype(jnp.float32), edge.astype(jnp.float32)], axis=0)
    line = jnp.where(edge_mask(width), line, 0.0)
    out[:, 0:cin] = pltpu.roll(line, width + EDGE - 1, 0).astype(jnp.bfloat16)
    out[:, cin : 2 * cin] = line.astype(jnp.bfloat16)
    out[:, 2 * cin : 3 * cin] = pltpu.roll(line, 1, 0).astype(jnp.bfloat16)


def tap_dot(lines, phase, kr, own_w, other_w):
    count, total, lanes = lines.shape
    cin = lanes // 3
    low = (1 - phase) * cin
    weight = jnp.concatenate(
        [ref[kr, :, 1 - phase].reshape(2 * cin, ref.shape[-1]) for ref in (own_w, other_w)], axis=1
    )
    out = jnp.dot(
        lines[:, :, low : low + 2 * cin].reshape(count * total, 2 * cin),
        weight,
        preferred_element_type=jnp.float32,
    )
    return out.reshape(count, total, weight.shape[-1])


def add_sums(line, width):
    values = line[:width].astype(jnp.float32)
    return jnp.concatenate(
        [jnp.sum(values, axis=0, keepdims=True), jnp.sum(values * values, axis=0, keepdims=True)], axis=0
    )


def own_kernel(lines_ref, own_w, other_w, xs_ref, u_ref, part_ref, tail_ref, sums_ref):
    rows, total, _ = lines_ref.shape
    width = total - EDGE
    for row in range(rows):
        spread_line(xs_ref.at[row], lines_ref[row, :width], lines_ref[row, width:])
    first_here = lax.axis_index("rows") == 0
    sums = jnp.zeros((2, u_ref.shape[-1]), jnp.float32)
    for phase in range(2):
        dot = functools.partial(tap_dot, phase=phase, own_w=own_w, other_w=other_w)
        upper = dot(xs_ref[...], kr=1)
        lower = dot(xs_ref[...], kr=3)
        part_ref[phase] = upper[0]
        tail_ref[phase, 1] = lower[rows - 1]
        even = [(upper[row + 1] + lower[row]).astype(jnp.bfloat16) for row in range(rows - 1)]
        upper = dot(xs_ref[...], kr=2)
        lower = dot(xs_ref[1:], kr=0)
        tail_ref[phase, 0] = upper[rows - 1]
        odd = [(upper[row] + lower[row]).astype(jnp.bfloat16) for row in range(rows - 1)]
        for row in range(rows - 1):
            u_ref[2 * row, phase] = odd[row]
            u_ref[2 * row + 1, phase] = even[row]
            sums += add_sums(odd[row], width) + add_sums(even[row], width)
        sums += jnp.where(first_here, add_sums(part_ref[phase].astype(jnp.bfloat16), width), 0.0)
    sums_ref[...] = sums


def next_kernel(next_ref, edge_ref, tail_ref, sums_ref, own_w, other_w, u_ref, xs_ref, stats_ref):
    width = next_ref.shape[1]
    last_here = lax.axis_index("rows") == lax.axis_size("rows") - 1
    spread_line(xs_ref.at[0], next_ref[0], edge_ref[0])
    column = lax.axis_index("fsdp")
    sums = sums_ref[...]
    for phase in range(2):
        dot = functools.partial(tap_dot, phase=phase, own_w=own_w, other_w=other_w)
        odd = (tail_ref[phase, 0] + dot(xs_ref[...], kr=0)[0]).astype(jnp.bfloat16)
        even = (tail_ref[phase, 1] + dot(xs_ref[...], kr=1)[0]).astype(jnp.bfloat16)
        u_ref[0, phase] = odd
        u_ref[1, phase] = even
        sums += add_sums(odd, width) + jnp.where(last_here, 0.0, add_sums(even, width))
    half = sums.shape[1] // 2
    halves = []
    for row in range(2):
        own, other = sums[row : row + 1, :half], sums[row : row + 1, half:]
        halves += [jnp.where(column == 0, own, other), jnp.where(column == 0, other, own)]
    stats_ref[...] = jnp.concatenate(halves + [jnp.zeros((4, half), jnp.float32)], axis=0)


def halo_kernel(above_ref, next_ref, next_edge_ref, xs_ref, xs_next_ref, part_ref, own_w, other_w, u_ref, xs_above, xs_below):
    width = next_ref.shape[1]
    for row in range(HALO):
        spread_line(xs_above.at[row], above_ref[row, :width], above_ref[row, width:])
    spread_line(xs_below.at[0], next_ref[1], next_edge_ref[1])
    for phase in range(2):
        dot = functools.partial(tap_dot, phase=phase, own_w=own_w, other_w=other_w)
        outer = dot(xs_above[...], kr=3)
        u_ref[0, phase] = (outer[0] + dot(xs_above[1:2], kr=1)[0]).astype(jnp.bfloat16)
        u_ref[2, phase] = (outer[1] + part_ref[phase]).astype(jnp.bfloat16)
        u_ref[1, phase] = (dot(xs_above[1:2], kr=2)[0] + dot(xs_ref[0:1], kr=0)[0]).astype(jnp.bfloat16)
        u_ref[3, phase] = (dot(xs_next_ref[...], kr=2)[0] + dot(xs_below[...], kr=0)[0]).astype(jnp.bfloat16)


def group_sum(v, width):
    lane = lax.broadcasted_iota(jnp.int32, v.shape, 1)
    size = v.shape[1]
    step = 1
    while step < width:
        v = v + jnp.where(
            (lane & step) == 0, pltpu.roll(v, size - step, 1), pltpu.roll(v, step, 1)
        )
        step *= 2
    return v


def fill(ref, row, even, odd):
    total, channels = even.shape
    ref[row, :, 0:channels] = pltpu.roll(odd, 1, 0).astype(jnp.bfloat16)
    ref[row, :, channels : 2 * channels] = even.astype(jnp.bfloat16)
    ref[row, :, 2 * channels : 3 * channels] = odd.astype(jnp.bfloat16)
    ref[row, :, 3 * channels : 4 * channels] = pltpu.roll(even, total - 1, 0).astype(jnp.bfloat16)


def conv_kernel(
    count, u_ref, u_next_ref, halo_ref, stats_ref, params_ref, own_w1, other_w1, own_w2, other_w2, out_ref, g, act, mixed
):
    early, _, total, cout = u_ref.shape
    main = early + u_next_ref.shape[0]
    lines = main + 2 * HALO
    width = total - EDGE
    half = own_w1.shape[-1]
    column = lax.axis_index("fsdp")
    own_at = pl.multiple_of(column * half, half)
    other_at = pl.multiple_of((1 - column) * half, half)

    def own_first(row):
        low, high = row[:, :half], row[:, half:]
        return jnp.concatenate([jnp.where(column == 0, low, high), jnp.where(column == 0, high, low)], axis=1)

    def kernel_row(a, own, other):
        return jnp.concatenate(
            [
                jnp.concatenate([ref[a, b, pl.ds(at, half), :] for b in range(3) for at in (own_at, other_at)], axis=0)
                for ref in (own, other)
            ],
            axis=1,
        )

    block = stats_ref[...]
    width_group = cout // NORM_GROUPS
    sums = jnp.concatenate([block[0:1], block[1:2]], axis=1)
    squares = jnp.concatenate([block[2:3], block[3:4]], axis=1)
    mean = group_sum(sums, width_group) / count
    spread = group_sum(squares, width_group) / count - mean * mean
    scale = lax.rsqrt(spread + 1e-05) * params_ref[0:1]
    shift = own_first(0.5 * (params_ref[1:2] - mean * scale))
    scale = own_first(0.5 * scale)
    bias1 = own_first(0.5 * params_ref[2:3])
    bias2 = own_first(params_ref[3:4])

    edge_seen = edge_mask(width)[width:]
    place = lax.axis_index("rows")
    last = lax.axis_size("rows") - 1

    def masked(row, beyond, value):
        value = jnp.concatenate([value[:width], jnp.where(edge_seen, value[width:], 0.0)], axis=0)
        if row < beyond:
            return jnp.where(place > 0, value, 0.0)
        if row >= lines - 2 * HALO + beyond:
            return jnp.where(place < last, value, 0.0)
        return value

    def hidden(row):
        if row < 3:
            source = halo_ref.at[row]
        elif row < 3 + early:
            source = u_ref.at[row - 3]
        elif row < 3 + main:
            source = u_next_ref.at[row - 3 - early]
        else:
            source = halo_ref.at[3]
        fill(
            g,
            row,
            *[
                masked(row, HALO, silu_of_half(source[phase].astype(jnp.float32) * scale + shift))
                for phase in range(2)
            ],
        )

    def dots(source, start, size, cells, phase, own, other):
        total = None
        for a in range(3):
            term = jnp.dot(
                source[start + a : start + a + size, 0:cells, phase * cout : (phase + 3) * cout].reshape(
                    size * cells, 3 * cout
                ),
                kernel_row(a, own, other),
                preferred_element_type=jnp.float32,
            )
            total = term if total is None else total + term
        return total.reshape(size, cells, cout)

    chunk = 2

    def first(start):
        return [dots(g, start, chunk, total, phase, own_w1, other_w1) for phase in range(2)]

    def activate(start, results):
        for row in range(chunk):
            fill(
                act,
                start + row,
                *[masked(start + row, 1, silu_of_half(0.5 * r[row] + bias1)) for r in results],
            )

    def second(start):
        for phase in range(2):
            acc = dots(act, start, chunk, width, phase, own_w2, other_w2) + bias2
            for row in range(chunk):
                for side in range(2):
                    mixed[side, start + row, pl.ds(phase, width, stride=2), :] = acc[
                        row, :, side * half : (side + 1) * half
                    ]
        for row in range(start, start + chunk):
            out_ref[row, :, pl.ds(own_at, half)] = mixed[0, row].astype(jnp.bfloat16)
            out_ref[row, :, pl.ds(other_at, half)] = mixed[1, row].astype(jnp.bfloat16)

    for row in range(2 * chunk):
        hidden(row)
    for start in range(0, lines - 2, chunk):
        results = first(start)
        for row in range(start + 2 * chunk, min(start + 3 * chunk, lines)):
            hidden(row)
        if start >= 2 * chunk:
            second(start - 2 * chunk)
        activate(start, results)
    second(lines - 4 - chunk)


def total_over(block, axis):
    size = lax.axis_size(axis)
    if size & (size - 1):
        return lax.psum(block, axis)
    steps = [2**n for n in range(size.bit_length() - 1)]
    for step in steps[1:] + steps[:1]:
        block = block + lax.ppermute(block, axis, [(i, i ^ step) for i in range(size)])
    return block


def after(value, *others):
    return lax.optimization_barrier((value, *others))[0]


def local(image, deconv_weight, norm_gain, norm_shift, first_weight, first_bias, second_weight, second_bias):
    rows, width, cin = image.shape
    taps, _, _, lanes = deconv_weight.shape
    columns = lax.axis_size("fsdp")
    cout = lanes * columns
    assert columns == 2 and rows == HALO and width % EDGE == 0 and lanes == LANES
    n_rows = lax.axis_size("rows")
    count = float(2 * rows * n_rows * 2 * width * columns * (cout // NORM_GROUPS))
    swap = [(0, 1), (1, 0)]
    to_next = [(i, i + 1) for i in range(n_rows - 1)]
    to_previous = [(i + 1, i) for i in range(n_rows - 1)]
    total = width + EDGE
    hbm = pl.BlockSpec(memory_space=pltpu.HBM)
    vmem = pl.BlockSpec(memory_space=pltpu.VMEM)
    bf16, f32 = jnp.bfloat16, jnp.float32

    def call(kernel, ins, outs, scratch, name, flops=0):
        return pl.pallas_call(
            kernel,
            out_shape=tuple(jax.ShapeDtypeStruct(*o) for o in outs),
            in_specs=ins,
            out_specs=(vmem,) * len(outs),
            scratch_shapes=scratch,
            compiler_params=pltpu.CompilerParams(vmem_limit_bytes=VMEM_BYTES),
            cost_estimate=pl.CostEstimate(flops=flops, bytes_accessed=2**21, transcendentals=0),
            name=name,
        )

    in_hbm = functools.partial(pltpu.with_memory_space_constraint, memory_space=pltpu.HBM)
    shape_w = (taps, taps // 2, 2, cin, lanes)
    following = lax.ppermute(image, "rows", to_previous)
    near, edges = call(
        cut_kernel,
        [hbm],
        [(image.shape, bf16), ((rows, EDGE, cin), bf16)],
        [pltpu.SemaphoreType.DMA((2,))],
        "cut",
    )(in_hbm(image))
    edge = lax.ppermute(edges, "fsdp", swap)
    other_w = lax.ppermute(deconv_weight, "fsdp", swap).reshape(shape_w)
    first_other = lax.ppermute(after(first_weight, edges), "fsdp", swap)
    second_other = lax.ppermute(after(second_weight, edges), "fsdp", swap)
    (own_w,) = call(near_kernel, [hbm], [(shape_w, bf16)], [pltpu.SemaphoreType.DMA(())], "near_weights")(
        in_hbm(after(deconv_weight, edges).reshape(shape_w))
    )
    lines = jnp.concatenate([after(near, own_w), edge], axis=1)
    above = lax.ppermute(lines, "rows", to_next)
    u_line = (2, total, cout)
    xs, u, part, tail, sums = call(
        own_kernel,
        [vmem] * 3,
        [
            ((rows, total, 3 * cin), bf16),
            ((2 * rows - 2, *u_line), bf16),
            (u_line, f32),
            ((2, *u_line), f32),
            ((2, cout), f32),
        ],
        [],
        "deconv_own",
        flops=2 * 2 * (2 * rows - 1) * total * 4 * cin * cout,
    )(lines, own_w, other_w)
    (next_edges,) = call(pick_kernel, [vmem], [((rows, EDGE, cin), bf16)], [], "next_edges")(following)
    next_edge = lax.ppermute(next_edges, "fsdp", swap)
    u_next, xs_next, stats = call(
        next_kernel,
        [vmem] * 6,
        [((2, *u_line), bf16), ((1, total, 3 * cin), bf16), ((8, cout // 2), f32)],
        [],
        "deconv_next",
        flops=2 * 2 * total * 4 * cin * cout,
    )(following, next_edge, tail, sums, own_w, other_w)
    (halo,) = call(
        halo_kernel,
        [vmem] * 8,
        [((4, *u_line), bf16)],
        [pltpu.VMEM((HALO, total, 3 * cin), bf16), pltpu.VMEM((1, total, 3 * cin), bf16)],
        "deconv_halo",
        flops=2 * 2 * 4 * total * 4 * cin * cout,
    )(above, following, next_edge, xs, xs_next, part, own_w, other_w)

    totals = total_over(total_over(stats, "fsdp"), "rows")
    params = jnp.stack([norm_gain, norm_shift, first_bias, second_bias])
    (out,) = call(
        functools.partial(conv_kernel, count),
        [vmem] * 9,
        [((2 * rows, 2 * width, cout), bf16)],
        [
            pltpu.VMEM((2 * rows + 2 * HALO, total, 4 * cout), bf16),
            pltpu.VMEM((2 * rows + 2, total, 4 * cout), bf16),
            pltpu.VMEM((2, 2 * rows, 2 * width, lanes), f32),
        ],
        "convs",
        flops=5 * 10**9,
    )(u, u_next, halo, totals, params, first_weight, first_other, second_weight, second_other)
    return out


def solution(mesh):
    placed = (
        P(("groups", "rows"), "fsdp", None),
        P(None, None, None, "fsdp"),
        P(),
        P(),
        P(None, None, None, "fsdp"),
        P(),
        P(None, None, None, "fsdp"),
        P(),
    )
    return jax.shard_map(
        local,
        mesh=mesh,
        in_specs=placed,
        out_specs=P(("groups", "rows"), "fsdp", None),
        check_vma=False,
    )
```

```python
import functools

import jax
import jax.numpy as jnp
from jax import lax
from jax.experimental import pallas as pl
from jax.experimental.pallas import tpu as pltpu
from jax.sharding import PartitionSpec as P

NORM_GROUPS = 32
HALO = 2
EDGE = 16
LANES = 128
VMEM_BYTES = 24 * 2**20


def silu_of_half(h):
    return h + h * jnp.tanh(h)


def edge_mask(width):
    column = lax.axis_index("fsdp")
    last = lax.axis_size("fsdp") - 1
    cell = lax.broadcasted_iota(jnp.int32, (width + EDGE, 1), 0) - width
    right = (cell < EDGE // 2) & (column < last)
    left = (cell >= EDGE // 2) & (column > 0)
    return (cell < 0) | right | left


def cut_kernel(image_ref, near_ref, edges_ref, sems):
    width = image_ref.shape[1]
    start = pl.multiple_of((1 - lax.axis_index("fsdp")) * (width - EDGE), EDGE)
    copies = [
        pltpu.make_async_copy(image_ref.at[:, pl.ds(start, EDGE), :], edges_ref, sems.at[0]),
        pltpu.make_async_copy(image_ref, near_ref, sems.at[1]),
    ]
    for copy in copies:
        copy.start()
    for copy in copies:
        copy.wait()


def near_kernel(weight_ref, near_ref, sem):
    copy = pltpu.make_async_copy(weight_ref, near_ref, sem)
    copy.start()
    copy.wait()


def spread_line(out, main, edge, inside=True):
    width, cin = main.shape
    line = jnp.concatenate([main.astype(jnp.float32), edge.astype(jnp.float32)], axis=0)
    line = jnp.where(edge_mask(width) & inside, line, 0.0)
    out[:, 0:cin] = pltpu.roll(line, width + EDGE - 1, 0).astype(jnp.bfloat16)
    out[:, cin : 2 * cin] = line.astype(jnp.bfloat16)
    out[:, 2 * cin : 3 * cin] = pltpu.roll(line, 1, 0).astype(jnp.bfloat16)


def tap_dot(lines, phase, kr, own_w, other_w):
    count, total, lanes = lines.shape
    cin = lanes // 3
    low = (1 - phase) * cin
    weight = jnp.concatenate(
        [ref[kr, :, 1 - phase].reshape(2 * cin, ref.shape[-1]) for ref in (own_w, other_w)], axis=1
    )
    out = jnp.dot(
        lines[:, :, low : low + 2 * cin].reshape(count * total, 2 * cin),
        weight,
        preferred_element_type=jnp.float32,
    )
    return out.reshape(count, total, weight.shape[-1])


def add_sums(line, width):
    values = line[:width].astype(jnp.float32)
    return jnp.concatenate(
        [jnp.sum(values, axis=0, keepdims=True), jnp.sum(values * values, axis=0, keepdims=True)], axis=0
    )


def sides():
    place = lax.axis_index("rows")
    return lax.axis_index("fsdp"), place > 0, place < lax.axis_size("rows") - 1


def own_kernel(lines_ref, own_w, other_w, u_ref, shares_ref, sums_ref, xs_ref):
    rows, total, _ = lines_ref.shape
    width = total - EDGE
    for row in range(rows):
        spread_line(xs_ref.at[row], lines_ref[row, :width], lines_ref[row, width:])
    column, above, below = sides()
    sums = jnp.zeros((2, u_ref.shape[-1]), jnp.float32)
    for phase in range(2):
        terms = [tap_dot(xs_ref[...], phase, kr, own_w, other_w) for kr in range(4)]
        shares_ref[0, 0, phase] = terms[0][0]
        shares_ref[0, 1, phase] = terms[1][0]
        shares_ref[1, 0, phase] = terms[2][rows - 1]
        shares_ref[1, 1, phase] = terms[3][rows - 1]
        for row in range(rows - 1):
            odd = (terms[2][row] + terms[0][row + 1]).astype(jnp.bfloat16)
            even = (terms[3][row] + terms[1][row + 1]).astype(jnp.bfloat16)
            u_ref[2 * row, phase] = odd
            u_ref[2 * row + 1, phase] = even
            sums += add_sums(odd, width) + add_sums(even, width)
        bottom = add_sums(shares_ref[1, 0, phase].astype(jnp.bfloat16), width)
        top = add_sums(shares_ref[0, 1, phase].astype(jnp.bfloat16), width)
        sums += jnp.where((column == 0) & jnp.logical_not(below), bottom, 0.0)
        sums += jnp.where((column == 1) & jnp.logical_not(above), top, 0.0)
    sums_ref[...] = sums


def first_kernel(first_ref, shares_ref, sums_ref, own_w, other_w, u_ref, xs_ref, stats_ref):
    width = first_ref.shape[1] - EDGE
    column, above, below = sides()
    near = 1 - column
    inside = jnp.where(column == 0, above, below)
    spread_line(xs_ref.at[0], first_ref[near, :width], first_ref[near, width:], inside)
    sums = sums_ref[...]
    for phase in range(2):
        odd = tap_dot(xs_ref[...], phase, 2 - 2 * column, own_w, other_w)[0]
        odd = (shares_ref[column, 0, phase] + odd).astype(jnp.bfloat16)
        even = tap_dot(xs_ref[...], phase, 3 - 2 * column, own_w, other_w)[0]
        even = (shares_ref[column, 1, phase] + even).astype(jnp.bfloat16)
        u_ref[0, phase] = odd
        u_ref[1, phase] = even
        sums += jnp.where((column == 1) | above, add_sums(odd, width), 0.0)
        sums += jnp.where((column == 0) | below, add_sums(even, width), 0.0)
    half = sums.shape[1] // 2
    halves = []
    for row in range(2):
        own, other = sums[row : row + 1, :half], sums[row : row + 1, half:]
        halves += [jnp.where(column == 0, own, other), jnp.where(column == 0, other, own)]
    stats_ref[...] = jnp.concatenate(halves + [jnp.zeros((4, half), jnp.float32)], axis=0)


def halo_kernel(
    second_ref, first_ref, xs_near_ref, shares_ref, u_own_ref, u_first_ref, own_w, other_w, u_ref, xs_far, xs_second
):
    width = first_ref.shape[1] - EDGE
    early = u_own_ref.shape[0]
    column, above, below = sides()
    inside = jnp.where(column == 0, above, below)
    inside_second = jnp.where(column == 0, below, above)
    end = u_ref.shape[0] - 1
    first_at = jnp.where(column == 0, 1, end - 2)
    second_at = jnp.where(column == 0, end - 2, 1)
    first_end = column * end
    second_end = (1 - column) * end
    spread_line(xs_far.at[0], first_ref[column, :width], first_ref[column, width:], inside)
    for n in range(HALO):
        line = jnp.where(column == 0, n, 1 - n)
        spread_line(xs_second.at[n], second_ref[line, :width], second_ref[line, width:], inside_second)
    for row in range(early):
        u_ref[3 + row] = u_own_ref[row]
    for row in range(2):
        u_ref[first_at + row] = u_first_ref[row]
    for phase in range(2):

        def dot(lines, kr):
            return tap_dot(lines, phase, kr, own_w, other_w)[0]

        near, far = xs_second[0:1], xs_second[1:2]
        far_row = dot(xs_near_ref[...], 1 + column) + dot(xs_far[...], 3 - 3 * column)
        u_ref[first_end, phase] = far_row.astype(jnp.bfloat16)
        u_ref[second_at, phase] = (shares_ref[1 - column, 0, phase] + dot(near, 2 * column)).astype(jnp.bfloat16)
        u_ref[second_at + 1, phase] = (shares_ref[1 - column, 1, phase] + dot(near, 1 + 2 * column)).astype(jnp.bfloat16)
        u_ref[second_end, phase] = (dot(near, 2 - column) + dot(far, 3 * column)).astype(jnp.bfloat16)


def group_sum(v, width):
    lane = lax.broadcasted_iota(jnp.int32, v.shape, 1)
    size = v.shape[1]
    step = 1
    while step < width:
        v = v + jnp.where(
            (lane & step) == 0, pltpu.roll(v, size - step, 1), pltpu.roll(v, step, 1)
        )
        step *= 2
    return v


def fill(ref, row, even, odd):
    total, channels = even.shape
    ref[row, :, 0:channels] = pltpu.roll(odd, 1, 0).astype(jnp.bfloat16)
    ref[row, :, channels : 2 * channels] = even.astype(jnp.bfloat16)
    ref[row, :, 2 * channels : 3 * channels] = odd.astype(jnp.bfloat16)
    ref[row, :, 3 * channels : 4 * channels] = pltpu.roll(even, total - 1, 0).astype(jnp.bfloat16)


def conv_kernel(
    count, u_ref, stats_ref, params_ref, own_w1, other_w1, own_w2, other_w2, out_ref, g, act, mixed
):
    lines, _, total, cout = u_ref.shape
    width = total - EDGE
    half = own_w1.shape[-1]
    column = lax.axis_index("fsdp")
    own_at = pl.multiple_of(column * half, half)
    other_at = pl.multiple_of((1 - column) * half, half)

    def own_first(row):
        low, high = row[:, :half], row[:, half:]
        return jnp.concatenate([jnp.where(column == 0, low, high), jnp.where(column == 0, high, low)], axis=1)

    def kernel_row(a, own, other):
        return jnp.concatenate(
            [
                jnp.concatenate([ref[a, b, pl.ds(at, half), :] for b in range(3) for at in (own_at, other_at)], axis=0)
                for ref in (own, other)
            ],
            axis=1,
        )

    block = stats_ref[...]
    width_group = cout // NORM_GROUPS
    sums = jnp.concatenate([block[0:1], block[1:2]], axis=1)
    squares = jnp.concatenate([block[2:3], block[3:4]], axis=1)
    mean = group_sum(sums, width_group) / count
    spread = group_sum(squares, width_group) / count - mean * mean
    scale = lax.rsqrt(spread + 1e-05) * params_ref[0:1]
    shift = own_first(0.5 * (params_ref[1:2] - mean * scale))
    scale = own_first(0.5 * scale)
    bias1 = own_first(0.5 * params_ref[2:3])
    bias2 = own_first(params_ref[3:4])

    edge_seen = edge_mask(width)[width:]
    place = lax.axis_index("rows")
    last = lax.axis_size("rows") - 1

    def masked(row, beyond, value):
        value = jnp.concatenate([value[:width], jnp.where(edge_seen, value[width:], 0.0)], axis=0)
        if row < beyond:
            return jnp.where(place > 0, value, 0.0)
        if row >= lines - 2 * HALO + beyond:
            return jnp.where(place < last, value, 0.0)
        return value

    def hidden(row):
        fill(
            g,
            row,
            *[
                masked(row, HALO, silu_of_half(u_ref[row, phase].astype(jnp.float32) * scale + shift))
                for phase in range(2)
            ],
        )

    def dots(source, start, size, cells, phase, own, other):
        total = None
        for a in range(3):
            term = jnp.dot(
                source[start + a : start + a + size, 0:cells, phase * cout : (phase + 3) * cout].reshape(
                    size * cells, 3 * cout
                ),
                kernel_row(a, own, other),
                preferred_element_type=jnp.float32,
            )
            total = term if total is None else total + term
        return total.reshape(size, cells, cout)

    chunk = 2

    def first(start):
        return [dots(g, start, chunk, total, phase, own_w1, other_w1) for phase in range(2)]

    def activate(start, results):
        for row in range(chunk):
            fill(
                act,
                start + row,
                *[masked(start + row, 1, silu_of_half(0.5 * r[row] + bias1)) for r in results],
            )

    def second(start):
        for phase in range(2):
            acc = dots(act, start, chunk, width, phase, own_w2, other_w2) + bias2
            for row in range(chunk):
                for side in range(2):
                    mixed[side, start + row, pl.ds(phase, width, stride=2), :] = acc[
                        row, :, side * half : (side + 1) * half
                    ]
        for row in range(start, start + chunk):
            out_ref[row, :, pl.ds(own_at, half)] = mixed[0, row].astype(jnp.bfloat16)
            out_ref[row, :, pl.ds(other_at, half)] = mixed[1, row].astype(jnp.bfloat16)

    for row in range(2 * chunk):
        hidden(row)
    for start in range(0, lines - 2, chunk):
        results = first(start)
        for row in range(start + 2 * chunk, min(start + 3 * chunk, lines)):
            hidden(row)
        if start >= 2 * chunk:
            second(start - 2 * chunk)
        activate(start, results)
    second(lines - 4 - chunk)


def total_over(block, last):
    size = lax.axis_size("rows")
    assert size & (size - 1) == 0
    steps = [2**n for n in range(size.bit_length() - 1)]
    for step in steps[1:] + steps[:1]:
        block = block + lax.ppermute(block, "rows", [(i, i ^ step) for i in range(size)])
    return block + lax.ppermute(after(block, last), "fsdp", [(0, 1), (1, 0)])


def after(value, *others):
    return lax.optimization_barrier((value, *others))[0]


def local(image, deconv_weight, norm_gain, norm_shift, first_weight, first_bias, second_weight, second_bias):
    rows, width, cin = image.shape
    taps, _, _, lanes = deconv_weight.shape
    columns = lax.axis_size("fsdp")
    cout = lanes * columns
    assert columns == 2 and rows == HALO and width % EDGE == 0 and lanes == LANES
    n_rows = lax.axis_size("rows")
    count = float(2 * rows * n_rows * 2 * width * columns * (cout // NORM_GROUPS))
    swap = [(0, 1), (1, 0)]
    ends = range(n_rows - 1)
    bottom = 2 * n_rows - 1
    to_first = [(2 * i, 2 * i + 2) for i in ends] + [(2 * i + 3, 2 * i + 1) for i in ends] + [(bottom - 1, bottom), (1, 0)]
    to_second = [(2 * i + 2, 2 * i) for i in ends] + [(2 * i + 1, 2 * i + 3) for i in ends] + [(bottom, bottom - 1), (0, 1)]
    total = width + EDGE
    hbm = pl.BlockSpec(memory_space=pltpu.HBM)
    vmem = pl.BlockSpec(memory_space=pltpu.VMEM)
    bf16, f32 = jnp.bfloat16, jnp.float32

    def call(kernel, ins, outs, scratch, name, flops=0):
        return pl.pallas_call(
            kernel,
            out_shape=tuple(jax.ShapeDtypeStruct(*o) for o in outs),
            in_specs=ins,
            out_specs=(vmem,) * len(outs),
            scratch_shapes=scratch,
            compiler_params=pltpu.CompilerParams(vmem_limit_bytes=VMEM_BYTES),
            cost_estimate=pl.CostEstimate(flops=flops, bytes_accessed=2**21, transcendentals=0),
            name=name,
        )

    in_hbm = functools.partial(pltpu.with_memory_space_constraint, memory_space=pltpu.HBM)
    shape_w = (taps, taps // 2, 2, cin, lanes)
    both = ("rows", "fsdp")
    near, edges = call(
        cut_kernel,
        [hbm],
        [(image.shape, bf16), ((rows, EDGE, cin), bf16)],
        [pltpu.SemaphoreType.DMA((2,))],
        "cut",
    )(in_hbm(image))
    edge = lax.ppermute(edges, "fsdp", swap)
    lines = jnp.concatenate([near, edge], axis=1)
    first = lax.ppermute(lines, both, to_first)
    other_w = lax.ppermute(after(deconv_weight, edge), "fsdp", swap).reshape(shape_w)
    first_other = lax.ppermute(after(first_weight, edge), "fsdp", swap)
    second_other = lax.ppermute(after(second_weight, edge), "fsdp", swap)
    (own_w,) = call(near_kernel, [hbm], [(shape_w, bf16)], [pltpu.SemaphoreType.DMA(())], "near_weights")(
        in_hbm(after(deconv_weight, edges).reshape(shape_w))
    )
    u_line = (2, total, cout)
    spread = (1, total, 3 * cin)
    u_own, shares, sums = call(
        own_kernel,
        [vmem] * 3,
        [
            ((2 * rows - 2, *u_line), bf16),
            ((2, 2, *u_line), f32),
            ((2, cout), f32),
        ],
        [pltpu.VMEM((rows, total, 3 * cin), bf16)],
        "deconv_own",
        flops=2 * 2 * (2 * rows) * total * 4 * cin * cout,
    )(lines, own_w, other_w)
    second = lax.ppermute(after(lines, first, sums), both, to_second)
    u_first, xs_near, stats = call(
        first_kernel,
        [vmem] * 5,
        [((2, *u_line), bf16), (spread, bf16), ((8, cout // 2), f32)],
        [],
        "deconv_first",
        flops=2 * 2 * total * 4 * cin * cout,
    )(first, shares, sums, own_w, other_w)
    (u,) = call(
        halo_kernel,
        [vmem] * 8,
        [((2 * rows + 2 * HALO, *u_line), bf16)],
        [pltpu.VMEM(spread, bf16), pltpu.VMEM((HALO, *spread[1:]), bf16)],
        "deconv_halo",
        flops=2 * 2 * 3 * total * 4 * cin * cout,
    )(second, first, xs_near, shares, u_own, u_first, own_w, other_w)

    totals = total_over(stats, u)
    params = jnp.stack([norm_gain, norm_shift, first_bias, second_bias])
    (out,) = call(
        functools.partial(conv_kernel, count),
        [vmem] * 7,
        [((2 * rows, 2 * width, cout), bf16)],
        [
            pltpu.VMEM((2 * rows + 2 * HALO, total, 4 * cout), bf16),
            pltpu.VMEM((2 * rows + 2, total, 4 * cout), bf16),
            pltpu.VMEM((2, 2 * rows, 2 * width, lanes), f32),
        ],
        "convs",
        flops=5 * 10**9,
    )(u, totals, params, first_weight, first_other, second_weight, second_other)
    return out


def solution(mesh):
    placed = (
        P(("groups", "rows"), "fsdp", None),
        P(None, None, None, "fsdp"),
        P(),
        P(),
        P(None, None, None, "fsdp"),
        P(),
        P(None, None, None, "fsdp"),
        P(),
    )
    return jax.shard_map(
        local,
        mesh=mesh,
        in_specs=placed,
        out_specs=P(("groups", "rows"), "fsdp", None),
        check_vma=False,
    )
```

```python
import functools

import jax
import jax.numpy as jnp
from jax import lax
from jax.experimental import pallas as pl
from jax.experimental.pallas import tpu as pltpu
from jax.sharding import PartitionSpec as P

NORM_GROUPS = 32
HALO = 2
EDGE = 16
LANES = 128
VMEM_BYTES = 24 * 2**20


def silu_of_half(h):
    return h + h * jnp.tanh(h)


def edge_mask(width):
    column = lax.axis_index("fsdp")
    last = lax.axis_size("fsdp") - 1
    cell = lax.broadcasted_iota(jnp.int32, (width + EDGE, 1), 0) - width
    right = (cell < EDGE // 2) & (column < last)
    left = (cell >= EDGE // 2) & (column > 0)
    return (cell < 0) | right | left


def cut_kernel(image_ref, near_ref, edges_ref, sems):
    width = image_ref.shape[1]
    start = pl.multiple_of((1 - lax.axis_index("fsdp")) * (width - EDGE), EDGE)
    copies = [
        pltpu.make_async_copy(image_ref.at[:, pl.ds(start, EDGE), :], edges_ref, sems.at[0]),
        pltpu.make_async_copy(image_ref, near_ref, sems.at[1]),
    ]
    for copy in copies:
        copy.start()
    for copy in copies:
        copy.wait()


def pick_kernel(lines_ref, edges_ref):
    width = lines_ref.shape[1]
    at_left = lax.axis_index("fsdp") == 0

    @pl.when(at_left)
    def _():
        edges_ref[...] = lines_ref[:, width - EDGE :]

    @pl.when(jnp.logical_not(at_left))
    def _():
        edges_ref[...] = lines_ref[:, :EDGE]


def near_kernel(weight_ref, near_ref, sem):
    copy = pltpu.make_async_copy(weight_ref, near_ref, sem)
    copy.start()
    copy.wait()


def spread_line(out, main, edge):
    width, cin = main.shape
    line = jnp.concatenate([main.astype(jnp.float32), edge.astype(jnp.float32)], axis=0)
    line = jnp.where(edge_mask(width), line, 0.0)
    out[:, 0:cin] = pltpu.roll(line, width + EDGE - 1, 0).astype(jnp.bfloat16)
    out[:, cin : 2 * cin] = line.astype(jnp.bfloat16)
    out[:, 2 * cin : 3 * cin] = pltpu.roll(line, 1, 0).astype(jnp.bfloat16)


def tap_dot(lines, phase, kr, own_w, other_w):
    count, total, lanes = lines.shape
    cin = lanes // 3
    low = (1 - phase) * cin
    weight = jnp.concatenate(
        [ref[kr, :, 1 - phase].reshape(2 * cin, ref.shape[-1]) for ref in (own_w, other_w)], axis=1
    )
    out = jnp.dot(
        lines[:, :, low : low + 2 * cin].reshape(count * total, 2 * cin),
        weight,
        preferred_element_type=jnp.float32,
    )
    return out.reshape(count, total, weight.shape[-1])


def add_sums(line, width):
    values = line[:width].astype(jnp.float32)
    return jnp.concatenate(
        [jnp.sum(values, axis=0, keepdims=True), jnp.sum(values * values, axis=0, keepdims=True)], axis=0
    )


def own_kernel(lines_ref, own_w, other_w, xs_ref, u_ref, part_ref, tail_ref, sums_ref):
    rows, total, _ = lines_ref.shape
    width = total - EDGE
    for row in range(rows):
        spread_line(xs_ref.at[row], lines_ref[row, :width], lines_ref[row, width:])
    first_here = lax.axis_index("rows") == 0
    sums = jnp.zeros((2, u_ref.shape[-1]), jnp.float32)
    for phase in range(2):
        dot = functools.partial(tap_dot, phase=phase, own_w=own_w, other_w=other_w)
        upper = dot(xs_ref[...], kr=1)
        lower = dot(xs_ref[...], kr=3)
        part_ref[phase] = upper[0]
        tail_ref[phase, 1] = lower[rows - 1]
        even = [(upper[row + 1] + lower[row]).astype(jnp.bfloat16) for row in range(rows - 1)]
        upper = dot(xs_ref[...], kr=2)
        lower = dot(xs_ref[1:], kr=0)
        tail_ref[phase, 0] = upper[rows - 1]
        odd = [(upper[row] + lower[row]).astype(jnp.bfloat16) for row in range(rows - 1)]
        for row in range(rows - 1):
            u_ref[2 * row, phase] = odd[row]
            u_ref[2 * row + 1, phase] = even[row]
            sums += add_sums(odd[row], width) + add_sums(even[row], width)
        sums += jnp.where(first_here, add_sums(part_ref[phase].astype(jnp.bfloat16), width), 0.0)
    sums_ref[...] = sums


def next_kernel(next_ref, edge_ref, tail_ref, sums_ref, own_w, other_w, u_ref, xs_ref, stats_ref):
    width = next_ref.shape[1]
    last_here = lax.axis_index("rows") == lax.axis_size("rows") - 1
    spread_line(xs_ref.at[0], next_ref[0], edge_ref[0])
    column = lax.axis_index("fsdp")
    sums = sums_ref[...]
    for phase in range(2):
        dot = functools.partial(tap_dot, phase=phase, own_w=own_w, other_w=other_w)
        odd = (tail_ref[phase, 0] + dot(xs_ref[...], kr=0)[0]).astype(jnp.bfloat16)
        even = (tail_ref[phase, 1] + dot(xs_ref[...], kr=1)[0]).astype(jnp.bfloat16)
        u_ref[0, phase] = odd
        u_ref[1, phase] = even
        sums += add_sums(odd, width) + jnp.where(last_here, 0.0, add_sums(even, width))
    half = sums.shape[1] // 2
    halves = []
    for row in range(2):
        own, other = sums[row : row + 1, :half], sums[row : row + 1, half:]
        halves += [jnp.where(column == 0, own, other), jnp.where(column == 0, other, own)]
    stats_ref[...] = jnp.concatenate(halves + [jnp.zeros((4, half), jnp.float32)], axis=0)


def halo_kernel(above_ref, next_ref, next_edge_ref, xs_ref, xs_next_ref, part_ref, own_w, other_w, u_ref, xs_above, xs_below):
    width = next_ref.shape[1]
    for row in range(HALO):
        spread_line(xs_above.at[row], above_ref[row, :width], above_ref[row, width:])
    spread_line(xs_below.at[0], next_ref[1], next_edge_ref[1])
    for phase in range(2):
        dot = functools.partial(tap_dot, phase=phase, own_w=own_w, other_w=other_w)
        outer = dot(xs_above[...], kr=3)
        u_ref[0, phase] = (outer[0] + dot(xs_above[1:2], kr=1)[0]).astype(jnp.bfloat16)
        u_ref[2, phase] = (outer[1] + part_ref[phase]).astype(jnp.bfloat16)
        u_ref[1, phase] = (dot(xs_above[1:2], kr=2)[0] + dot(xs_ref[0:1], kr=0)[0]).astype(jnp.bfloat16)
        u_ref[3, phase] = (dot(xs_next_ref[...], kr=2)[0] + dot(xs_below[...], kr=0)[0]).astype(jnp.bfloat16)


def group_sum(v, width):
    lane = lax.broadcasted_iota(jnp.int32, v.shape, 1)
    size = v.shape[1]
    step = 1
    while step < width:
        v = v + jnp.where(
            (lane & step) == 0, pltpu.roll(v, size - step, 1), pltpu.roll(v, step, 1)
        )
        step *= 2
    return v


def fill(ref, row, even, odd):
    total, channels = even.shape
    ref[row, :, 0:channels] = pltpu.roll(odd, 1, 0).astype(jnp.bfloat16)
    ref[row, :, channels : 2 * channels] = even.astype(jnp.bfloat16)
    ref[row, :, 2 * channels : 3 * channels] = odd.astype(jnp.bfloat16)
    ref[row, :, 3 * channels : 4 * channels] = pltpu.roll(even, total - 1, 0).astype(jnp.bfloat16)


def conv_kernel(
    count, u_ref, u_next_ref, halo_ref, stats_ref, params_ref, own_w1, other_w1, own_w2, other_w2, out_ref, g, act, mixed
):
    early, _, total, cout = u_ref.shape
    main = early + u_next_ref.shape[0]
    lines = main + 2 * HALO
    width = total - EDGE
    half = own_w1.shape[-1]
    column = lax.axis_index("fsdp")
    own_at = pl.multiple_of(column * half, half)
    other_at = pl.multiple_of((1 - column) * half, half)

    def own_first(row):
        low, high = row[:, :half], row[:, half:]
        return jnp.concatenate([jnp.where(column == 0, low, high), jnp.where(column == 0, high, low)], axis=1)

    def kernel(own, other):
        return jnp.concatenate(
            [
                jnp.concatenate(
                    [
                        ref[a, b, pl.ds(at, half), :]
                        for a in range(3)
                        for b in range(3)
                        for at in (own_at, other_at)
                    ],
                    axis=0,
                )
                for ref in (own, other)
            ],
            axis=1,
        )

    block = stats_ref[...]
    width_group = cout // NORM_GROUPS
    sums = jnp.concatenate([block[0:1], block[1:2]], axis=1)
    squares = jnp.concatenate([block[2:3], block[3:4]], axis=1)
    mean = group_sum(sums, width_group) / count
    spread = group_sum(squares, width_group) / count - mean * mean
    scale = lax.rsqrt(spread + 1e-05) * params_ref[0:1]
    shift = own_first(0.5 * (params_ref[1:2] - mean * scale))
    scale = own_first(0.5 * scale)
    bias1 = own_first(0.5 * params_ref[2:3])
    bias2 = own_first(params_ref[3:4])

    edge_seen = edge_mask(width)[width:]
    place = lax.axis_index("rows")
    last = lax.axis_size("rows") - 1

    def masked(row, beyond, value):
        value = jnp.concatenate([value[:width], jnp.where(edge_seen, value[width:], 0.0)], axis=0)
        if row < beyond:
            return jnp.where(place > 0, value, 0.0)
        if row >= lines - 2 * HALO + beyond:
            return jnp.where(place < last, value, 0.0)
        return value

    def hidden(row):
        if row < 3:
            source = halo_ref.at[row]
        elif row < 3 + early:
            source = u_ref.at[row - 3]
        elif row < 3 + main:
            source = u_next_ref.at[row - 3 - early]
        else:
            source = halo_ref.at[3]
        fill(
            g,
            row,
            *[
                masked(row, HALO, silu_of_half(source[phase].astype(jnp.float32) * scale + shift))
                for phase in range(2)
            ],
        )

    def dots(source, start, size, cells, phase, own, other):
        taps = [
            source[start + a : start + a + size, 0:cells, phase * cout : (phase + 3) * cout].reshape(
                size * cells, 3 * cout
            )
            for a in range(3)
        ]
        out = jnp.dot(jnp.concatenate(taps, axis=1), kernel(own, other), preferred_element_type=jnp.float32)
        return out.reshape(size, cells, cout)

    chunk = 2

    def first(start):
        return [dots(g, start, chunk, total, phase, own_w1, other_w1) for phase in range(2)]

    def activate(start, results):
        for row in range(chunk):
            fill(
                act,
                start + row,
                *[masked(start + row, 1, silu_of_half(0.5 * r[row] + bias1)) for r in results],
            )

    def second(start):
        for phase in range(2):
            acc = dots(act, start, chunk, width, phase, own_w2, other_w2) + bias2
            for row in range(chunk):
                for side in range(2):
                    mixed[side, start + row, pl.ds(phase, width, stride=2), :] = acc[
                        row, :, side * half : (side + 1) * half
                    ]
        for row in range(start, start + chunk):
            out_ref[row, :, pl.ds(own_at, half)] = mixed[0, row].astype(jnp.bfloat16)
            out_ref[row, :, pl.ds(other_at, half)] = mixed[1, row].astype(jnp.bfloat16)

    for row in range(2 * chunk):
        hidden(row)
    for start in range(0, lines - 2, chunk):
        results = first(start)
        for row in range(start + 2 * chunk, min(start + 3 * chunk, lines)):
            hidden(row)
        if start >= 2 * chunk:
            second(start - 2 * chunk)
        activate(start, results)
    second(lines - 4 - chunk)


def total_over(block, axis):
    size = lax.axis_size(axis)
    if size & (size - 1):
        return lax.psum(block, axis)
    steps = [2**n for n in range(size.bit_length() - 1)]
    for step in steps[1:] + steps[:1]:
        block = block + lax.ppermute(block, axis, [(i, i ^ step) for i in range(size)])
    return block


def after(value, *others):
    return lax.optimization_barrier((value, *others))[0]


def local(image, deconv_weight, norm_gain, norm_shift, first_weight, first_bias, second_weight, second_bias):
    rows, width, cin = image.shape
    taps, _, _, lanes = deconv_weight.shape
    columns = lax.axis_size("fsdp")
    cout = lanes * columns
    assert columns == 2 and rows == HALO and width % EDGE == 0 and lanes == LANES
    n_rows = lax.axis_size("rows")
    count = float(2 * rows * n_rows * 2 * width * columns * (cout // NORM_GROUPS))
    swap = [(0, 1), (1, 0)]
    to_next = [(i, i + 1) for i in range(n_rows - 1)]
    to_previous = [(i + 1, i) for i in range(n_rows - 1)]
    total = width + EDGE
    hbm = pl.BlockSpec(memory_space=pltpu.HBM)
    vmem = pl.BlockSpec(memory_space=pltpu.VMEM)
    bf16, f32 = jnp.bfloat16, jnp.float32

    def call(kernel, ins, outs, scratch, name, flops=0):
        return pl.pallas_call(
            kernel,
            out_shape=tuple(jax.ShapeDtypeStruct(*o) for o in outs),
            in_specs=ins,
            out_specs=(vmem,) * len(outs),
            scratch_shapes=scratch,
            compiler_params=pltpu.CompilerParams(vmem_limit_bytes=VMEM_BYTES),
            cost_estimate=pl.CostEstimate(flops=flops, bytes_accessed=2**21, transcendentals=0),
            name=name,
        )

    in_hbm = functools.partial(pltpu.with_memory_space_constraint, memory_space=pltpu.HBM)
    shape_w = (taps, taps // 2, 2, cin, lanes)
    following = lax.ppermute(image, "rows", to_previous)
    near, edges = call(
        cut_kernel,
        [hbm],
        [(image.shape, bf16), ((rows, EDGE, cin), bf16)],
        [pltpu.SemaphoreType.DMA((2,))],
        "cut",
    )(in_hbm(image))
    edge = lax.ppermute(edges, "fsdp", swap)
    other_w = lax.ppermute(deconv_weight, "fsdp", swap).reshape(shape_w)
    first_other = lax.ppermute(after(first_weight, edges), "fsdp", swap)
    second_other = lax.ppermute(after(second_weight, edges), "fsdp", swap)
    (own_w,) = call(near_kernel, [hbm], [(shape_w, bf16)], [pltpu.SemaphoreType.DMA(())], "near_weights")(
        in_hbm(after(deconv_weight, edges).reshape(shape_w))
    )
    lines = jnp.concatenate([after(near, own_w), edge], axis=1)
    above = lax.ppermute(lines, "rows", to_next)
    u_line = (2, total, cout)
    xs, u, part, tail, sums = call(
        own_kernel,
        [vmem] * 3,
        [
            ((rows, total, 3 * cin), bf16),
            ((2 * rows - 2, *u_line), bf16),
            (u_line, f32),
            ((2, *u_line), f32),
            ((2, cout), f32),
        ],
        [],
        "deconv_own",
        flops=2 * 2 * (2 * rows - 1) * total * 4 * cin * cout,
    )(lines, own_w, other_w)
    (next_edges,) = call(pick_kernel, [vmem], [((rows, EDGE, cin), bf16)], [], "next_edges")(following)
    next_edge = lax.ppermute(next_edges, "fsdp", swap)
    u_next, xs_next, stats = call(
        next_kernel,
        [vmem] * 6,
        [((2, *u_line), bf16), ((1, total, 3 * cin), bf16), ((8, cout // 2), f32)],
        [],
        "deconv_next",
        flops=2 * 2 * total * 4 * cin * cout,
    )(following, next_edge, tail, sums, own_w, other_w)
    (halo,) = call(
        halo_kernel,
        [vmem] * 8,
        [((4, *u_line), bf16)],
        [pltpu.VMEM((HALO, total, 3 * cin), bf16), pltpu.VMEM((1, total, 3 * cin), bf16)],
        "deconv_halo",
        flops=2 * 2 * 4 * total * 4 * cin * cout,
    )(above, following, next_edge, xs, xs_next, part, own_w, other_w)

    totals = total_over(total_over(stats, "fsdp"), "rows")
    params = jnp.stack([norm_gain, norm_shift, first_bias, second_bias])
    (out,) = call(
        functools.partial(conv_kernel, count),
        [vmem] * 9,
        [((2 * rows, 2 * width, cout), bf16)],
        [
            pltpu.VMEM((2 * rows + 2 * HALO, total, 4 * cout), bf16),
            pltpu.VMEM((2 * rows + 2, total, 4 * cout), bf16),
            pltpu.VMEM((2, 2 * rows, 2 * width, lanes), f32),
        ],
        "convs",
        flops=5 * 10**9,
    )(u, u_next, halo, totals, params, first_weight, first_other, second_weight, second_other)
    return out


def solution(mesh):
    placed = (
        P(("groups", "rows"), "fsdp", None),
        P(None, None, None, "fsdp"),
        P(),
        P(),
        P(None, None, None, "fsdp"),
        P(),
        P(None, None, None, "fsdp"),
        P(),
    )
    return jax.shard_map(
        local,
        mesh=mesh,
        in_specs=placed,
        out_specs=P(("groups", "rows"), "fsdp", None),
        check_vma=False,
    )
```

```python
import functools

import jax
import jax.numpy as jnp
from jax import lax
from jax.experimental import pallas as pl
from jax.experimental.pallas import tpu as pltpu
from jax.sharding import PartitionSpec as P

NORM_GROUPS = 32
HALO = 2
EDGE = 16
LANES = 128
VMEM_BYTES = 24 * 2**20


def silu_of_half(h):
    return h + h * jnp.tanh(h)


def edge_mask(width):
    column = lax.axis_index("fsdp")
    last = lax.axis_size("fsdp") - 1
    cell = lax.broadcasted_iota(jnp.int32, (width + EDGE, 1), 0) - width
    right = (cell < EDGE // 2) & (column < last)
    left = (cell >= EDGE // 2) & (column > 0)
    return (cell < 0) | right | left


def cut_kernel(image_ref, near_ref, edges_ref, sems):
    width = image_ref.shape[1]
    start = pl.multiple_of((1 - lax.axis_index("fsdp")) * (width - EDGE), EDGE)
    copies = [
        pltpu.make_async_copy(image_ref.at[:, pl.ds(start, EDGE), :], edges_ref, sems.at[0]),
        pltpu.make_async_copy(image_ref, near_ref, sems.at[1]),
    ]
    for copy in copies:
        copy.start()
    for copy in copies:
        copy.wait()


def pick_kernel(lines_ref, edges_ref):
    width = lines_ref.shape[1]
    at_left = lax.axis_index("fsdp") == 0

    @pl.when(at_left)
    def _():
        edges_ref[...] = lines_ref[:, width - EDGE :]

    @pl.when(jnp.logical_not(at_left))
    def _():
        edges_ref[...] = lines_ref[:, :EDGE]


def near_kernel(weight_ref, near_ref, sem):
    copy = pltpu.make_async_copy(weight_ref, near_ref, sem)
    copy.start()
    copy.wait()


def spread_line(out, main, edge):
    width, cin = main.shape
    line = jnp.concatenate([main.astype(jnp.float32), edge.astype(jnp.float32)], axis=0)
    line = jnp.where(edge_mask(width), line, 0.0)
    out[:, 0:cin] = pltpu.roll(line, width + EDGE - 1, 0).astype(jnp.bfloat16)
    out[:, cin : 2 * cin] = line.astype(jnp.bfloat16)
    out[:, 2 * cin : 3 * cin] = pltpu.roll(line, 1, 0).astype(jnp.bfloat16)


def tap_dot(lines, phase, kr, own_w, other_w):
    count, total, lanes = lines.shape
    cin = lanes // 3
    low = (1 - phase) * cin
    weight = jnp.concatenate(
        [ref[kr, :, 1 - phase].reshape(2 * cin, ref.shape[-1]) for ref in (own_w, other_w)], axis=1
    )
    out = jnp.dot(
        lines[:, :, low : low + 2 * cin].reshape(count * total, 2 * cin),
        weight,
        preferred_element_type=jnp.float32,
    )
    return out.reshape(count, total, weight.shape[-1])


def add_sums(line, width):
    values = line[:width].astype(jnp.float32)
    return jnp.concatenate(
        [jnp.sum(values, axis=0, keepdims=True), jnp.sum(values * values, axis=0, keepdims=True)], axis=0
    )


def own_kernel(lines_ref, own_w, other_w, xs_ref, u_ref, part_ref, tail_ref, sums_ref):
    rows, total, _ = lines_ref.shape
    width = total - EDGE
    for row in range(rows):
        spread_line(xs_ref.at[row], lines_ref[row, :width], lines_ref[row, width:])
    first_here = lax.axis_index("rows") == 0
    sums = jnp.zeros((2, u_ref.shape[-1]), jnp.float32)
    for phase in range(2):
        dot = functools.partial(tap_dot, phase=phase, own_w=own_w, other_w=other_w)
        upper = dot(xs_ref[...], kr=1)
        lower = dot(xs_ref[...], kr=3)
        part_ref[phase] = upper[0]
        tail_ref[phase, 1] = lower[rows - 1]
        even = [(upper[row + 1] + lower[row]).astype(jnp.bfloat16) for row in range(rows - 1)]
        upper = dot(xs_ref[...], kr=2)
        lower = dot(xs_ref[1:], kr=0)
        tail_ref[phase, 0] = upper[rows - 1]
        odd = [(upper[row] + lower[row]).astype(jnp.bfloat16) for row in range(rows - 1)]
        for row in range(rows - 1):
            u_ref[2 * row, phase] = odd[row]
            u_ref[2 * row + 1, phase] = even[row]
            sums += add_sums(odd[row], width) + add_sums(even[row], width)
        sums += jnp.where(first_here, add_sums(part_ref[phase].astype(jnp.bfloat16), width), 0.0)
    sums_ref[...] = sums


def next_kernel(next_ref, edge_ref, tail_ref, sums_ref, own_w, other_w, u_ref, xs_ref, stats_ref):
    width = next_ref.shape[1]
    last_here = lax.axis_index("rows") == lax.axis_size("rows") - 1
    spread_line(xs_ref.at[0], next_ref[0], edge_ref[0])
    column = lax.axis_index("fsdp")
    sums = sums_ref[...]
    for phase in range(2):
        dot = functools.partial(tap_dot, phase=phase, own_w=own_w, other_w=other_w)
        odd = (tail_ref[phase, 0] + dot(xs_ref[...], kr=0)[0]).astype(jnp.bfloat16)
        even = (tail_ref[phase, 1] + dot(xs_ref[...], kr=1)[0]).astype(jnp.bfloat16)
        u_ref[0, phase] = odd
        u_ref[1, phase] = even
        sums += add_sums(odd, width) + jnp.where(last_here, 0.0, add_sums(even, width))
    half = sums.shape[1] // 2
    halves = []
    for row in range(2):
        own, other = sums[row : row + 1, :half], sums[row : row + 1, half:]
        halves += [jnp.where(column == 0, own, other), jnp.where(column == 0, other, own)]
    stats_ref[...] = jnp.concatenate(halves + [jnp.zeros((4, half), jnp.float32)], axis=0)


def halo_kernel(above_ref, next_ref, next_edge_ref, xs_ref, xs_next_ref, part_ref, own_w, other_w, u_ref, xs_above, xs_below):
    width = next_ref.shape[1]
    for row in range(HALO):
        spread_line(xs_above.at[row], above_ref[row, :width], above_ref[row, width:])
    spread_line(xs_below.at[0], next_ref[1], next_edge_ref[1])
    for phase in range(2):
        dot = functools.partial(tap_dot, phase=phase, own_w=own_w, other_w=other_w)
        outer = dot(xs_above[...], kr=3)
        u_ref[0, phase] = (outer[0] + dot(xs_above[1:2], kr=1)[0]).astype(jnp.bfloat16)
        u_ref[2, phase] = (outer[1] + part_ref[phase]).astype(jnp.bfloat16)
        u_ref[1, phase] = (dot(xs_above[1:2], kr=2)[0] + dot(xs_ref[0:1], kr=0)[0]).astype(jnp.bfloat16)
        u_ref[3, phase] = (dot(xs_next_ref[...], kr=2)[0] + dot(xs_below[...], kr=0)[0]).astype(jnp.bfloat16)


def group_sum(v, width):
    lane = lax.broadcasted_iota(jnp.int32, v.shape, 1)
    size = v.shape[1]
    step = 1
    while step < width:
        v = v + jnp.where(
            (lane & step) == 0, pltpu.roll(v, size - step, 1), pltpu.roll(v, step, 1)
        )
        step *= 2
    return v


def fill(ref, row, even, odd):
    total, channels = even.shape
    ref[row, :, 0:channels] = pltpu.roll(odd, 1, 0).astype(jnp.bfloat16)
    ref[row, :, channels : 2 * channels] = even.astype(jnp.bfloat16)
    ref[row, :, 2 * channels : 3 * channels] = odd.astype(jnp.bfloat16)
    ref[row, :, 3 * channels : 4 * channels] = pltpu.roll(even, total - 1, 0).astype(jnp.bfloat16)


def conv_kernel(
    count, u_ref, u_next_ref, halo_ref, stats_ref, params_ref, own_w1, other_w1, own_w2, other_w2, out_ref, g, act, mixed
):
    early, _, total, cout = u_ref.shape
    main = early + u_next_ref.shape[0]
    lines = main + 2 * HALO
    width = total - EDGE
    half = own_w1.shape[-1]
    column = lax.axis_index("fsdp")
    own_at = pl.multiple_of(column * half, half)
    other_at = pl.multiple_of((1 - column) * half, half)

    def own_first(row):
        low, high = row[:, :half], row[:, half:]
        return jnp.concatenate([jnp.where(column == 0, low, high), jnp.where(column == 0, high, low)], axis=1)

    def kernel(own, other):
        return jnp.concatenate(
            [
                jnp.concatenate(
                    [
                        ref[a, b, pl.ds(at, half), :]
                        for a in range(3)
                        for b in range(3)
                        for at in (own_at, other_at)
                    ],
                    axis=0,
                )
                for ref in (own, other)
            ],
            axis=1,
        )

    block = stats_ref[...]
    width_group = cout // NORM_GROUPS
    sums = jnp.concatenate([block[0:1], block[1:2]], axis=1)
    squares = jnp.concatenate([block[2:3], block[3:4]], axis=1)
    mean = group_sum(sums, width_group) / count
    spread = group_sum(squares, width_group) / count - mean * mean
    scale = lax.rsqrt(spread + 1e-05) * params_ref[0:1]
    shift = own_first(0.5 * (params_ref[1:2] - mean * scale))
    scale = own_first(0.5 * scale)
    bias1 = own_first(0.5 * params_ref[2:3])
    bias2 = own_first(params_ref[3:4])

    edge_seen = edge_mask(width)[width:]
    place = lax.axis_index("rows")
    last = lax.axis_size("rows") - 1

    def masked(row, beyond, value):
        value = jnp.concatenate([value[:width], jnp.where(edge_seen, value[width:], 0.0)], axis=0)
        if row < beyond:
            return jnp.where(place > 0, value, 0.0)
        if row >= lines - 2 * HALO + beyond:
            return jnp.where(place < last, value, 0.0)
        return value

    def hidden(row):
        if row < 3:
            source = halo_ref.at[row]
        elif row < 3 + early:
            source = u_ref.at[row - 3]
        elif row < 3 + main:
            source = u_next_ref.at[row - 3 - early]
        else:
            source = halo_ref.at[3]
        fill(
            g,
            row,
            *[
                masked(row, HALO, silu_of_half(source[phase].astype(jnp.float32) * scale + shift))
                for phase in range(2)
            ],
        )

    def dots(source, start, size, cells, phase, own, other):
        taps = [
            source[start + a : start + a + size, 0:cells, phase * cout : (phase + 3) * cout].reshape(
                size * cells, 3 * cout
            )
            for a in range(3)
        ]
        out = jnp.dot(jnp.concatenate(taps, axis=1), kernel(own, other), preferred_element_type=jnp.float32)
        return out.reshape(size, cells, cout)

    def first(row):
        return [dots(g, row, 1, total, phase, own_w1, other_w1)[0] for phase in range(2)]

    def activate(row, results):
        fill(act, row, *[masked(row, 1, silu_of_half(0.5 * r + bias1)) for r in results])

    def second(row):
        for phase in range(2):
            acc = dots(act, row, 1, width, phase, own_w2, other_w2)[0] + bias2
            for side in range(2):
                mixed[side, row, pl.ds(phase, width, stride=2), :] = acc[:, side * half : (side + 1) * half]
        out_ref[row, :, pl.ds(own_at, half)] = mixed[0, row].astype(jnp.bfloat16)
        out_ref[row, :, pl.ds(other_at, half)] = mixed[1, row].astype(jnp.bfloat16)

    for row in range(3):
        hidden(row)
    results = None
    for row in range(lines - 2):
        latest = first(row)
        if row >= 4:
            second(row - 4)
        if row + 3 < lines:
            hidden(row + 3)
        if row >= 1:
            activate(row - 1, results)
        results = latest
    if lines >= 6:
        second(lines - 6)
    activate(lines - 3, results)
    second(lines - 5)


def total_over(block, axis):
    size = lax.axis_size(axis)
    if size & (size - 1):
        return lax.psum(block, axis)
    steps = [2**n for n in range(size.bit_length() - 1)]
    for step in steps[1:] + steps[:1]:
        block = block + lax.ppermute(block, axis, [(i, i ^ step) for i in range(size)])
    return block


def after(value, *others):
    return lax.optimization_barrier((value, *others))[0]


def local(image, deconv_weight, norm_gain, norm_shift, first_weight, first_bias, second_weight, second_bias):
    rows, width, cin = image.shape
    taps, _, _, lanes = deconv_weight.shape
    columns = lax.axis_size("fsdp")
    cout = lanes * columns
    assert columns == 2 and rows == HALO and width % EDGE == 0 and lanes == LANES
    n_rows = lax.axis_size("rows")
    count = float(2 * rows * n_rows * 2 * width * columns * (cout // NORM_GROUPS))
    swap = [(0, 1), (1, 0)]
    to_next = [(i, i + 1) for i in range(n_rows - 1)]
    to_previous = [(i + 1, i) for i in range(n_rows - 1)]
    total = width + EDGE
    hbm = pl.BlockSpec(memory_space=pltpu.HBM)
    vmem = pl.BlockSpec(memory_space=pltpu.VMEM)
    bf16, f32 = jnp.bfloat16, jnp.float32

    def call(kernel, ins, outs, scratch, name, flops=0):
        return pl.pallas_call(
            kernel,
            out_shape=tuple(jax.ShapeDtypeStruct(*o) for o in outs),
            in_specs=ins,
            out_specs=(vmem,) * len(outs),
            scratch_shapes=scratch,
            compiler_params=pltpu.CompilerParams(vmem_limit_bytes=VMEM_BYTES),
            cost_estimate=pl.CostEstimate(flops=flops, bytes_accessed=2**21, transcendentals=0),
            name=name,
        )

    in_hbm = functools.partial(pltpu.with_memory_space_constraint, memory_space=pltpu.HBM)
    shape_w = (taps, taps // 2, 2, cin, lanes)
    following = lax.ppermute(image, "rows", to_previous)
    near, edges = call(
        cut_kernel,
        [hbm],
        [(image.shape, bf16), ((rows, EDGE, cin), bf16)],
        [pltpu.SemaphoreType.DMA((2,))],
        "cut",
    )(in_hbm(image))
    edge = lax.ppermute(edges, "fsdp", swap)
    other_w = lax.ppermute(deconv_weight, "fsdp", swap).reshape(shape_w)
    first_other = lax.ppermute(after(first_weight, edges), "fsdp", swap)
    second_other = lax.ppermute(after(second_weight, edges), "fsdp", swap)
    (own_w,) = call(near_kernel, [hbm], [(shape_w, bf16)], [pltpu.SemaphoreType.DMA(())], "near_weights")(
        in_hbm(after(deconv_weight, edges).reshape(shape_w))
    )
    lines = jnp.concatenate([after(near, own_w), edge], axis=1)
    above = lax.ppermute(lines, "rows", to_next)
    u_line = (2, total, cout)
    xs, u, part, tail, sums = call(
        own_kernel,
        [vmem] * 3,
        [
            ((rows, total, 3 * cin), bf16),
            ((2 * rows - 2, *u_line), bf16),
            (u_line, f32),
            ((2, *u_line), f32),
            ((2, cout), f32),
        ],
        [],
        "deconv_own",
        flops=2 * 2 * (2 * rows - 1) * total * 4 * cin * cout,
    )(lines, own_w, other_w)
    (next_edges,) = call(pick_kernel, [vmem], [((rows, EDGE, cin), bf16)], [], "next_edges")(following)
    next_edge = lax.ppermute(next_edges, "fsdp", swap)
    u_next, xs_next, stats = call(
        next_kernel,
        [vmem] * 6,
        [((2, *u_line), bf16), ((1, total, 3 * cin), bf16), ((8, cout // 2), f32)],
        [],
        "deconv_next",
        flops=2 * 2 * total * 4 * cin * cout,
    )(following, next_edge, tail, sums, own_w, other_w)
    (halo,) = call(
        halo_kernel,
        [vmem] * 8,
        [((4, *u_line), bf16)],
        [pltpu.VMEM((HALO, total, 3 * cin), bf16), pltpu.VMEM((1, total, 3 * cin), bf16)],
        "deconv_halo",
        flops=2 * 2 * 4 * total * 4 * cin * cout,
    )(above, following, next_edge, xs, xs_next, part, own_w, other_w)

    totals = total_over(total_over(stats, "fsdp"), "rows")
    params = jnp.stack([norm_gain, norm_shift, first_bias, second_bias])
    (out,) = call(
        functools.partial(conv_kernel, count),
        [vmem] * 9,
        [((2 * rows, 2 * width, cout), bf16)],
        [
            pltpu.VMEM((2 * rows + 2 * HALO, total, 4 * cout), bf16),
            pltpu.VMEM((2 * rows + 2, total, 4 * cout), bf16),
            pltpu.VMEM((2, 2 * rows, 2 * width, lanes), f32),
        ],
        "convs",
        flops=5 * 10**9,
    )(u, u_next, halo, totals, params, first_weight, first_other, second_weight, second_other)
    return out


def solution(mesh):
    placed = (
        P(("groups", "rows"), "fsdp", None),
        P(None, None, None, "fsdp"),
        P(),
        P(),
        P(None, None, None, "fsdp"),
        P(),
        P(None, None, None, "fsdp"),
        P(),
    )
    return jax.shard_map(
        local,
        mesh=mesh,
        in_specs=placed,
        out_specs=P(("groups", "rows"), "fsdp", None),
        check_vma=False,
    )
```

```python
import functools

import jax
import jax.numpy as jnp
from jax import lax
from jax.experimental import pallas as pl
from jax.experimental.pallas import tpu as pltpu
from jax.sharding import PartitionSpec as P

NORM_GROUPS = 32
HALO = 2
EDGE = 16
LANES = 128
VMEM_BYTES = 24 * 2**20


def silu_of_half(h):
    return h + h * jnp.tanh(h)


def edge_mask(width):
    column = lax.axis_index("fsdp")
    last = lax.axis_size("fsdp") - 1
    cell = lax.broadcasted_iota(jnp.int32, (width + EDGE, 1), 0) - width
    right = (cell < EDGE // 2) & (column < last)
    left = (cell >= EDGE // 2) & (column > 0)
    return (cell < 0) | right | left


def cut_kernel(image_ref, near_ref, edges_ref, sems):
    width = image_ref.shape[1]
    start = pl.multiple_of((1 - lax.axis_index("fsdp")) * (width - EDGE), EDGE)
    copies = [
        pltpu.make_async_copy(image_ref.at[:, pl.ds(start, EDGE), :], edges_ref, sems.at[0]),
        pltpu.make_async_copy(image_ref, near_ref, sems.at[1]),
    ]
    for copy in copies:
        copy.start()
    for copy in copies:
        copy.wait()


def pick_kernel(lines_ref, edges_ref):
    width = lines_ref.shape[1]
    at_left = lax.axis_index("fsdp") == 0

    @pl.when(at_left)
    def _():
        edges_ref[...] = lines_ref[:, width - EDGE :]

    @pl.when(jnp.logical_not(at_left))
    def _():
        edges_ref[...] = lines_ref[:, :EDGE]


def near_kernel(weight_ref, near_ref, sem):
    copy = pltpu.make_async_copy(weight_ref, near_ref, sem)
    copy.start()
    copy.wait()


def spread_line(out, main, edge):
    width, cin = main.shape
    line = jnp.concatenate([main.astype(jnp.float32), edge.astype(jnp.float32)], axis=0)
    line = jnp.where(edge_mask(width), line, 0.0)
    out[:, 0:cin] = pltpu.roll(line, width + EDGE - 1, 0).astype(jnp.bfloat16)
    out[:, cin : 2 * cin] = line.astype(jnp.bfloat16)
    out[:, 2 * cin : 3 * cin] = pltpu.roll(line, 1, 0).astype(jnp.bfloat16)


def tap_dot(lines, phase, kr, own_w, other_w):
    count, total, lanes = lines.shape
    cin = lanes // 3
    low = (1 - phase) * cin
    weight = jnp.concatenate(
        [ref[kr, :, 1 - phase].reshape(2 * cin, ref.shape[-1]) for ref in (own_w, other_w)], axis=1
    )
    out = jnp.dot(
        lines[:, :, low : low + 2 * cin].reshape(count * total, 2 * cin),
        weight,
        preferred_element_type=jnp.float32,
    )
    return out.reshape(count, total, weight.shape[-1])


def add_sums(line, width):
    values = line[:width].astype(jnp.float32)
    return jnp.concatenate(
        [jnp.sum(values, axis=0, keepdims=True), jnp.sum(values * values, axis=0, keepdims=True)], axis=0
    )


def own_kernel(lines_ref, own_w, other_w, xs_ref, u_ref, part_ref, tail_ref, sums_ref):
    rows, total, _ = lines_ref.shape
    width = total - EDGE
    for row in range(rows):
        spread_line(xs_ref.at[row], lines_ref[row, :width], lines_ref[row, width:])
    first_here = lax.axis_index("rows") == 0
    sums = jnp.zeros((2, u_ref.shape[-1]), jnp.float32)
    for phase in range(2):
        dot = functools.partial(tap_dot, phase=phase, own_w=own_w, other_w=other_w)
        upper = dot(xs_ref[...], kr=1)
        lower = dot(xs_ref[...], kr=3)
        part_ref[phase] = upper[0]
        tail_ref[phase, 1] = lower[rows - 1]
        even = [(upper[row + 1] + lower[row]).astype(jnp.bfloat16) for row in range(rows - 1)]
        upper = dot(xs_ref[...], kr=2)
        lower = dot(xs_ref[1:], kr=0)
        tail_ref[phase, 0] = upper[rows - 1]
        odd = [(upper[row] + lower[row]).astype(jnp.bfloat16) for row in range(rows - 1)]
        for row in range(rows - 1):
            u_ref[2 * row, phase] = odd[row]
            u_ref[2 * row + 1, phase] = even[row]
            sums += add_sums(odd[row], width) + add_sums(even[row], width)
        sums += jnp.where(first_here, add_sums(part_ref[phase].astype(jnp.bfloat16), width), 0.0)
    sums_ref[...] = sums


def next_kernel(next_ref, edge_ref, tail_ref, sums_ref, own_w, other_w, u_ref, xs_ref, stats_ref):
    width = next_ref.shape[1]
    last_here = lax.axis_index("rows") == lax.axis_size("rows") - 1
    spread_line(xs_ref.at[0], next_ref[0], edge_ref[0])
    column = lax.axis_index("fsdp")
    sums = sums_ref[...]
    for phase in range(2):
        dot = functools.partial(tap_dot, phase=phase, own_w=own_w, other_w=other_w)
        odd = (tail_ref[phase, 0] + dot(xs_ref[...], kr=0)[0]).astype(jnp.bfloat16)
        even = (tail_ref[phase, 1] + dot(xs_ref[...], kr=1)[0]).astype(jnp.bfloat16)
        u_ref[0, phase] = odd
        u_ref[1, phase] = even
        sums += add_sums(odd, width) + jnp.where(last_here, 0.0, add_sums(even, width))
    half = sums.shape[1] // 2
    halves = []
    for row in range(2):
        own, other = sums[row : row + 1, :half], sums[row : row + 1, half:]
        halves += [jnp.where(column == 0, own, other), jnp.where(column == 0, other, own)]
    stats_ref[...] = jnp.concatenate(halves + [jnp.zeros((4, half), jnp.float32)], axis=0)


def halo_kernel(above_ref, next_ref, next_edge_ref, xs_ref, xs_next_ref, part_ref, own_w, other_w, u_ref, xs_above, xs_below):
    width = next_ref.shape[1]
    for row in range(HALO):
        spread_line(xs_above.at[row], above_ref[row, :width], above_ref[row, width:])
    spread_line(xs_below.at[0], next_ref[1], next_edge_ref[1])
    for phase in range(2):
        dot = functools.partial(tap_dot, phase=phase, own_w=own_w, other_w=other_w)
        outer = dot(xs_above[...], kr=3)
        u_ref[0, phase] = (outer[0] + dot(xs_above[1:2], kr=1)[0]).astype(jnp.bfloat16)
        u_ref[2, phase] = (outer[1] + part_ref[phase]).astype(jnp.bfloat16)
        u_ref[1, phase] = (dot(xs_above[1:2], kr=2)[0] + dot(xs_ref[0:1], kr=0)[0]).astype(jnp.bfloat16)
        u_ref[3, phase] = (dot(xs_next_ref[...], kr=2)[0] + dot(xs_below[...], kr=0)[0]).astype(jnp.bfloat16)


def group_sum(v, width):
    lane = lax.broadcasted_iota(jnp.int32, v.shape, 1)
    size = v.shape[1]
    step = 1
    while step < width:
        v = v + jnp.where(
            (lane & step) == 0, pltpu.roll(v, size - step, 1), pltpu.roll(v, step, 1)
        )
        step *= 2
    return v


def fill(ref, row, phase, lane, value):
    total, size = value.shape
    channels = ref.shape[-1] // 4
    own, shifted, by = ((1, 3, total - 1), (2, 0, 1))[phase]
    ref[row, :, own * channels + lane : own * channels + lane + size] = value.astype(jnp.bfloat16)
    ref[row, :, shifted * channels + lane : shifted * channels + lane + size] = pltpu.roll(value, by, 0).astype(
        jnp.bfloat16
    )


def weave(dots, rest):
    done = 0
    for n, dot in enumerate(dots):
        dot()
        upto = len(rest) * (n + 1) // len(dots)
        for step in rest[done:upto]:
            step()
        done = upto


def conv_kernel(
    count, u_ref, u_next_ref, halo_ref, stats_ref, params_ref, own_w1, other_w1, own_w2, other_w2, out_ref, g, act, mixed
):
    early, _, total, cout = u_ref.shape
    main = early + u_next_ref.shape[0]
    lines = main + 2 * HALO
    width = total - EDGE
    half = own_w1.shape[-1]
    column = lax.axis_index("fsdp")
    own_at = pl.multiple_of(column * half, half)
    other_at = pl.multiple_of((1 - column) * half, half)

    def own_first(row):
        low, high = row[:, :half], row[:, half:]
        return jnp.concatenate([jnp.where(column == 0, low, high), jnp.where(column == 0, high, low)], axis=1)

    def kernel_row(a, own, other):
        return jnp.concatenate(
            [
                jnp.concatenate([ref[a, b, pl.ds(at, half), :] for b in range(3) for at in (own_at, other_at)], axis=0)
                for ref in (own, other)
            ],
            axis=1,
        )

    block = stats_ref[...]
    width_group = cout // NORM_GROUPS
    sums = jnp.concatenate([block[0:1], block[1:2]], axis=1)
    squares = jnp.concatenate([block[2:3], block[3:4]], axis=1)
    mean = group_sum(sums, width_group) / count
    spread = group_sum(squares, width_group) / count - mean * mean
    scale = lax.rsqrt(spread + 1e-05) * params_ref[0:1]
    shift = own_first(0.5 * (params_ref[1:2] - mean * scale))
    scale = own_first(0.5 * scale)
    bias1 = own_first(0.5 * params_ref[2:3])
    bias2 = own_first(params_ref[3:4])

    edge_seen = edge_mask(width)[width:]
    place = lax.axis_index("rows")
    last = lax.axis_size("rows") - 1

    def masked(row, beyond, value):
        value = jnp.concatenate([value[:width], jnp.where(edge_seen, value[width:], 0.0)], axis=0)
        if row < beyond:
            return jnp.where(place > 0, value, 0.0)
        if row >= lines - 2 * HALO + beyond:
            return jnp.where(place < last, value, 0.0)
        return value

    quarters = [(phase, lane) for phase in range(2) for lane in range(0, cout, half)]

    def hidden(row):
        if row < 3:
            source = halo_ref.at[row]
        elif row < 3 + early:
            source = u_ref.at[row - 3]
        elif row < 3 + main:
            source = u_next_ref.at[row - 3 - early]
        else:
            source = halo_ref.at[3]

        def step(phase, lane):
            part = slice(lane, lane + half)
            value = source[phase, :, part].astype(jnp.float32) * scale[:, part] + shift[:, part]
            fill(g, row, phase, lane, masked(row, HALO, silu_of_half(value)))

        return [functools.partial(step, *quarter) for quarter in quarters]

    def activate(row, results):
        def step(phase, lane):
            part = slice(lane, lane + half)
            value = silu_of_half(0.5 * results[phase][:, part] + bias1[:, part])
            fill(act, row, phase, lane, masked(row, 1, value))

        return [functools.partial(step, *quarter) for quarter in quarters]

    def store(row, results):
        def step(phase, lane):
            part = slice(lane, lane + half)
            mixed[lane // half, row, pl.ds(phase, width, stride=2), :] = results[phase][:, part] + bias2[:, part]

        def last():
            out_ref[row, :, pl.ds(own_at, half)] = mixed[0, row].astype(jnp.bfloat16)
            out_ref[row, :, pl.ds(other_at, half)] = mixed[1, row].astype(jnp.bfloat16)

        return [functools.partial(step, *quarter) for quarter in quarters] + [last]

    def dots(source, row, cells, own, other, results):
        def step(phase, a):
            term = jnp.dot(
                source[row + a, 0:cells, phase * cout : (phase + 3) * cout],
                kernel_row(a, own, other),
                preferred_element_type=jnp.float32,
            )
            results[phase] = term if a == 0 else results[phase] + term

        return [functools.partial(step, phase, a) for phase in range(2) for a in range(3)]

    for row in range(3):
        for step in hidden(row):
            step()
    ones = [{} for _ in range(lines - 2)]
    twos = [{} for _ in range(lines - 4)]
    for row in range(lines + 1):
        work, rest = [], []
        if row < lines - 2:
            work += dots(g, row, total, own_w1, other_w1, ones[row])
        if 4 <= row < lines:
            work += dots(act, row - 4, width, own_w2, other_w2, twos[row - 4])
        if row + 3 < lines:
            rest += hidden(row + 3)
        if 1 <= row < lines - 1:
            rest += activate(row - 1, ones[row - 1])
        if row >= 5:
            rest += store(row - 5, twos[row - 5])
        weave(work or [lambda: None], rest)


def total_over(block, axis):
    size = lax.axis_size(axis)
    if size & (size - 1):
        return lax.psum(block, axis)
    steps = [2**n for n in range(size.bit_length() - 1)]
    for step in steps[1:] + steps[:1]:
        block = block + lax.ppermute(block, axis, [(i, i ^ step) for i in range(size)])
    return block


def after(value, *others):
    return lax.optimization_barrier((value, *others))[0]


def local(image, deconv_weight, norm_gain, norm_shift, first_weight, first_bias, second_weight, second_bias):
    rows, width, cin = image.shape
    taps, _, _, lanes = deconv_weight.shape
    columns = lax.axis_size("fsdp")
    cout = lanes * columns
    assert columns == 2 and rows == HALO and width % EDGE == 0 and lanes == LANES
    n_rows = lax.axis_size("rows")
    count = float(2 * rows * n_rows * 2 * width * columns * (cout // NORM_GROUPS))
    swap = [(0, 1), (1, 0)]
    to_next = [(i, i + 1) for i in range(n_rows - 1)]
    to_previous = [(i + 1, i) for i in range(n_rows - 1)]
    total = width + EDGE
    hbm = pl.BlockSpec(memory_space=pltpu.HBM)
    vmem = pl.BlockSpec(memory_space=pltpu.VMEM)
    bf16, f32 = jnp.bfloat16, jnp.float32

    def call(kernel, ins, outs, scratch, name, flops=0):
        return pl.pallas_call(
            kernel,
            out_shape=tuple(jax.ShapeDtypeStruct(*o) for o in outs),
            in_specs=ins,
            out_specs=(vmem,) * len(outs),
            scratch_shapes=scratch,
            compiler_params=pltpu.CompilerParams(vmem_limit_bytes=VMEM_BYTES),
            cost_estimate=pl.CostEstimate(flops=flops, bytes_accessed=2**21, transcendentals=0),
            name=name,
        )

    in_hbm = functools.partial(pltpu.with_memory_space_constraint, memory_space=pltpu.HBM)
    shape_w = (taps, taps // 2, 2, cin, lanes)
    following = lax.ppermute(image, "rows", to_previous)
    near, edges = call(
        cut_kernel,
        [hbm],
        [(image.shape, bf16), ((rows, EDGE, cin), bf16)],
        [pltpu.SemaphoreType.DMA((2,))],
        "cut",
    )(in_hbm(image))
    edge = lax.ppermute(edges, "fsdp", swap)
    other_w = lax.ppermute(deconv_weight, "fsdp", swap).reshape(shape_w)
    first_other = lax.ppermute(after(first_weight, edges), "fsdp", swap)
    second_other = lax.ppermute(after(second_weight, edges), "fsdp", swap)
    (own_w,) = call(near_kernel, [hbm], [(shape_w, bf16)], [pltpu.SemaphoreType.DMA(())], "near_weights")(
        in_hbm(after(deconv_weight, edges).reshape(shape_w))
    )
    lines = jnp.concatenate([after(near, own_w), edge], axis=1)
    above = lax.ppermute(lines, "rows", to_next)
    u_line = (2, total, cout)
    xs, u, part, tail, sums = call(
        own_kernel,
        [vmem] * 3,
        [
            ((rows, total, 3 * cin), bf16),
            ((2 * rows - 2, *u_line), bf16),
            (u_line, f32),
            ((2, *u_line), f32),
            ((2, cout), f32),
        ],
        [],
        "deconv_own",
        flops=2 * 2 * (2 * rows - 1) * total * 4 * cin * cout,
    )(lines, own_w, other_w)
    (next_edges,) = call(pick_kernel, [vmem], [((rows, EDGE, cin), bf16)], [], "next_edges")(following)
    next_edge = lax.ppermute(next_edges, "fsdp", swap)
    u_next, xs_next, stats = call(
        next_kernel,
        [vmem] * 6,
        [((2, *u_line), bf16), ((1, total, 3 * cin), bf16), ((8, cout // 2), f32)],
        [],
        "deconv_next",
        flops=2 * 2 * total * 4 * cin * cout,
    )(following, next_edge, tail, sums, own_w, other_w)
    (halo,) = call(
        halo_kernel,
        [vmem] * 8,
        [((4, *u_line), bf16)],
        [pltpu.VMEM((HALO, total, 3 * cin), bf16), pltpu.VMEM((1, total, 3 * cin), bf16)],
        "deconv_halo",
        flops=2 * 2 * 4 * total * 4 * cin * cout,
    )(above, following, next_edge, xs, xs_next, part, own_w, other_w)

    totals = total_over(total_over(stats, "fsdp"), "rows")
    params = jnp.stack([norm_gain, norm_shift, first_bias, second_bias])
    (out,) = call(
        functools.partial(conv_kernel, count),
        [vmem] * 9,
        [((2 * rows, 2 * width, cout), bf16)],
        [
            pltpu.VMEM((2 * rows + 2 * HALO, total, 4 * cout), bf16),
            pltpu.VMEM((2 * rows + 2, total, 4 * cout), bf16),
            pltpu.VMEM((2, 2 * rows, 2 * width, lanes), f32),
        ],
        "convs",
        flops=5 * 10**9,
    )(u, u_next, halo, totals, params, first_weight, first_other, second_weight, second_other)
    return out


def solution(mesh):
    placed = (
        P(("groups", "rows"), "fsdp", None),
        P(None, None, None, "fsdp"),
        P(),
        P(),
        P(None, None, None, "fsdp"),
        P(),
        P(None, None, None, "fsdp"),
        P(),
    )
    return jax.shard_map(
        local,
        mesh=mesh,
        in_specs=placed,
        out_specs=P(("groups", "rows"), "fsdp", None),
        check_vma=False,
    )
```

```python
import functools

import jax
import jax.numpy as jnp
from jax import lax
from jax.experimental import pallas as pl
from jax.experimental.pallas import tpu as pltpu
from jax.sharding import PartitionSpec as P

NORM_GROUPS = 32
HALO = 2
EDGE = 16
LANES = 128
VMEM_BYTES = 24 * 2**20


def silu_of_half(h):
    return h + h * jnp.tanh(h)


def edge_mask(width):
    column = lax.axis_index("fsdp")
    last = lax.axis_size("fsdp") - 1
    cell = lax.broadcasted_iota(jnp.int32, (width + EDGE, 1), 0) - width
    right = (cell < EDGE // 2) & (column < last)
    left = (cell >= EDGE // 2) & (column > 0)
    return (cell < 0) | right | left


def cut_kernel(image_ref, near_ref, edges_ref, sems):
    width = image_ref.shape[1]
    start = pl.multiple_of((1 - lax.axis_index("fsdp")) * (width - EDGE), EDGE)
    copies = [
        pltpu.make_async_copy(image_ref.at[:, pl.ds(start, EDGE), :], edges_ref, sems.at[0]),
        pltpu.make_async_copy(image_ref, near_ref, sems.at[1]),
    ]
    for copy in copies:
        copy.start()
    for copy in copies:
        copy.wait()


def pick_kernel(lines_ref, edges_ref):
    width = lines_ref.shape[1]
    at_left = lax.axis_index("fsdp") == 0

    @pl.when(at_left)
    def _():
        edges_ref[...] = lines_ref[:, width - EDGE :]

    @pl.when(jnp.logical_not(at_left))
    def _():
        edges_ref[...] = lines_ref[:, :EDGE]


def near_kernel(weight_ref, near_ref, sem):
    copy = pltpu.make_async_copy(weight_ref, near_ref, sem)
    copy.start()
    copy.wait()


def spread_line(out, main, edge, inside=True):
    width, cin = main.shape
    line = jnp.concatenate([main.astype(jnp.float32), edge.astype(jnp.float32)], axis=0)
    line = jnp.where(edge_mask(width) & inside, line, 0.0)
    out[:, 0:cin] = pltpu.roll(line, width + EDGE - 1, 0).astype(jnp.bfloat16)
    out[:, cin : 2 * cin] = line.astype(jnp.bfloat16)
    out[:, 2 * cin : 3 * cin] = pltpu.roll(line, 1, 0).astype(jnp.bfloat16)


def tap_dot(lines, phase, kr, own_w, other_w):
    count, total, lanes = lines.shape
    cin = lanes // 3
    low = (1 - phase) * cin
    weight = jnp.concatenate(
        [ref[kr, :, 1 - phase].reshape(2 * cin, ref.shape[-1]) for ref in (own_w, other_w)], axis=1
    )
    out = jnp.dot(
        lines[:, :, low : low + 2 * cin].reshape(count * total, 2 * cin),
        weight,
        preferred_element_type=jnp.float32,
    )
    return out.reshape(count, total, weight.shape[-1])


def add_sums(line, width):
    values = line[:width].astype(jnp.float32)
    return jnp.concatenate(
        [jnp.sum(values, axis=0, keepdims=True), jnp.sum(values * values, axis=0, keepdims=True)], axis=0
    )


def own_kernel(lines_ref, own_w, other_w, xs_ref, u_ref, part_ref, tail_ref, sums_ref):
    rows, total, _ = lines_ref.shape
    width = total - EDGE
    for row in range(rows):
        spread_line(xs_ref.at[row], lines_ref[row, :width], lines_ref[row, width:])
    first_here = lax.axis_index("rows") == 0
    sums = jnp.zeros((2, u_ref.shape[-1]), jnp.float32)
    for phase in range(2):
        dot = functools.partial(tap_dot, phase=phase, own_w=own_w, other_w=other_w)
        upper = dot(xs_ref[...], kr=1)
        lower = dot(xs_ref[...], kr=3)
        part_ref[phase] = upper[0]
        tail_ref[phase, 1] = lower[rows - 1]
        even = [(upper[row + 1] + lower[row]).astype(jnp.bfloat16) for row in range(rows - 1)]
        upper = dot(xs_ref[...], kr=2)
        lower = dot(xs_ref[1:], kr=0)
        tail_ref[phase, 0] = upper[rows - 1]
        odd = [(upper[row] + lower[row]).astype(jnp.bfloat16) for row in range(rows - 1)]
        for row in range(rows - 1):
            u_ref[2 * row, phase] = odd[row]
            u_ref[2 * row + 1, phase] = even[row]
            sums += add_sums(odd[row], width) + add_sums(even[row], width)
        sums += jnp.where(first_here, add_sums(part_ref[phase].astype(jnp.bfloat16), width), 0.0)
    sums_ref[...] = sums


def next_kernel(next_ref, edge_ref, tail_ref, sums_ref, own_w, other_w, u_ref, xs_ref, stats_ref):
    width = next_ref.shape[1]
    last_here = lax.axis_index("rows") == lax.axis_size("rows") - 1
    spread_line(xs_ref.at[0], next_ref[0], edge_ref[0], jnp.logical_not(last_here))
    column = lax.axis_index("fsdp")
    sums = sums_ref[...]
    for phase in range(2):
        dot = functools.partial(tap_dot, phase=phase, own_w=own_w, other_w=other_w)
        odd = (tail_ref[phase, 0] + dot(xs_ref[...], kr=0)[0]).astype(jnp.bfloat16)
        even = (tail_ref[phase, 1] + dot(xs_ref[...], kr=1)[0]).astype(jnp.bfloat16)
        u_ref[0, phase] = odd
        u_ref[1, phase] = even
        sums += add_sums(odd, width) + jnp.where(last_here, 0.0, add_sums(even, width))
    half = sums.shape[1] // 2
    halves = []
    for row in range(2):
        own, other = sums[row : row + 1, :half], sums[row : row + 1, half:]
        halves += [jnp.where(column == 0, own, other), jnp.where(column == 0, other, own)]
    stats_ref[...] = jnp.concatenate(halves + [jnp.zeros((4, half), jnp.float32)], axis=0)


def halo_kernel(above_ref, next_ref, next_edge_ref, xs_ref, xs_next_ref, part_ref, own_w, other_w, u_ref, xs_above, xs_below):
    width = next_ref.shape[1]
    for row in range(HALO):
        spread_line(xs_above.at[row], above_ref[row, :width], above_ref[row, width:])
    more_below = lax.axis_index("rows") < lax.axis_size("rows") - 1
    spread_line(xs_below.at[0], next_ref[1], next_edge_ref[1], more_below)
    for phase in range(2):
        dot = functools.partial(tap_dot, phase=phase, own_w=own_w, other_w=other_w)
        outer = dot(xs_above[...], kr=3)
        u_ref[0, phase] = (outer[0] + dot(xs_above[1:2], kr=1)[0]).astype(jnp.bfloat16)
        u_ref[2, phase] = (outer[1] + part_ref[phase]).astype(jnp.bfloat16)
        u_ref[1, phase] = (dot(xs_above[1:2], kr=2)[0] + dot(xs_ref[0:1], kr=0)[0]).astype(jnp.bfloat16)
        u_ref[3, phase] = (dot(xs_next_ref[...], kr=2)[0] + dot(xs_below[...], kr=0)[0]).astype(jnp.bfloat16)


def group_sum(v, width):
    lane = lax.broadcasted_iota(jnp.int32, v.shape, 1)
    size = v.shape[1]
    step = 1
    while step < width:
        v = v + jnp.where(
            (lane & step) == 0, pltpu.roll(v, size - step, 1), pltpu.roll(v, step, 1)
        )
        step *= 2
    return v


def fill(ref, row, even, odd):
    total, channels = even.shape
    ref[row, :, 0:channels] = pltpu.roll(odd, 1, 0).astype(jnp.bfloat16)
    ref[row, :, channels : 2 * channels] = even.astype(jnp.bfloat16)
    ref[row, :, 2 * channels : 3 * channels] = odd.astype(jnp.bfloat16)
    ref[row, :, 3 * channels : 4 * channels] = pltpu.roll(even, total - 1, 0).astype(jnp.bfloat16)


def conv_kernel(
    count, u_ref, u_next_ref, halo_ref, stats_ref, params_ref, own_w1, other_w1, own_w2, other_w2, out_ref, g, act, mixed
):
    early, _, total, cout = u_ref.shape
    main = early + u_next_ref.shape[0]
    lines = main + 2 * HALO
    width = total - EDGE
    half = own_w1.shape[-1]
    column = lax.axis_index("fsdp")
    own_at = pl.multiple_of(column * half, half)
    other_at = pl.multiple_of((1 - column) * half, half)

    def own_first(row):
        low, high = row[:, :half], row[:, half:]
        return jnp.concatenate([jnp.where(column == 0, low, high), jnp.where(column == 0, high, low)], axis=1)

    def kernel_row(a, own, other):
        return jnp.concatenate(
            [
                jnp.concatenate([ref[a, b, pl.ds(at, half), :] for b in range(3) for at in (own_at, other_at)], axis=0)
                for ref in (own, other)
            ],
            axis=1,
        )

    block = stats_ref[...]
    width_group = cout // NORM_GROUPS
    sums = jnp.concatenate([block[0:1], block[1:2]], axis=1)
    squares = jnp.concatenate([block[2:3], block[3:4]], axis=1)
    mean = group_sum(sums, width_group) / count
    spread = group_sum(squares, width_group) / count - mean * mean
    scale = lax.rsqrt(spread + 1e-05) * params_ref[0:1]
    shift = own_first(0.5 * (params_ref[1:2] - mean * scale))
    scale = own_first(0.5 * scale)
    bias1 = own_first(0.5 * params_ref[2:3])
    bias2 = own_first(params_ref[3:4])

    edge_seen = edge_mask(width)[width:]
    place = lax.axis_index("rows")
    last = lax.axis_size("rows") - 1

    def masked(row, beyond, value):
        value = jnp.concatenate([value[:width], jnp.where(edge_seen, value[width:], 0.0)], axis=0)
        if row < beyond:
            return jnp.where(place > 0, value, 0.0)
        if row >= lines - 2 * HALO + beyond:
            return jnp.where(place < last, value, 0.0)
        return value

    def hidden(row):
        if row < 3:
            source = halo_ref.at[row]
        elif row < 3 + early:
            source = u_ref.at[row - 3]
        elif row < 3 + main:
            source = u_next_ref.at[row - 3 - early]
        else:
            source = halo_ref.at[3]
        fill(
            g,
            row,
            *[
                masked(row, HALO, silu_of_half(source[phase].astype(jnp.float32) * scale + shift))
                for phase in range(2)
            ],
        )

    def dots(source, start, size, cells, phase, own, other):
        total = None
        for a in range(3):
            term = jnp.dot(
                source[start + a : start + a + size, 0:cells, phase * cout : (phase + 3) * cout].reshape(
                    size * cells, 3 * cout
                ),
                kernel_row(a, own, other),
                preferred_element_type=jnp.float32,
            )
            total = term if total is None else total + term
        return total.reshape(size, cells, cout)

    chunk = 2

    def first(start):
        return [dots(g, start, chunk, total, phase, own_w1, other_w1) for phase in range(2)]

    def activate(start, results):
        for row in range(chunk):
            fill(
                act,
                start + row,
                *[masked(start + row, 1, silu_of_half(0.5 * r[row] + bias1)) for r in results],
            )

    def second(start):
        for phase in range(2):
            acc = dots(act, start, chunk, width, phase, own_w2, other_w2) + bias2
            for row in range(chunk):
                for side in range(2):
                    mixed[side, start + row, pl.ds(phase, width, stride=2), :] = acc[
                        row, :, side * half : (side + 1) * half
                    ]
        for row in range(start, start + chunk):
            out_ref[row, :, pl.ds(own_at, half)] = mixed[0, row].astype(jnp.bfloat16)
            out_ref[row, :, pl.ds(other_at, half)] = mixed[1, row].astype(jnp.bfloat16)

    for row in range(2 * chunk):
        hidden(row)
    for start in range(0, lines - 2, chunk):
        results = first(start)
        for row in range(start + 2 * chunk, min(start + 3 * chunk, lines)):
            hidden(row)
        if start >= 2 * chunk:
            second(start - 2 * chunk)
        activate(start, results)
    second(lines - 4 - chunk)


def total_over(block, axis):
    size = lax.axis_size(axis)
    if size & (size - 1):
        return lax.psum(block, axis)
    steps = [2**n for n in range(size.bit_length() - 1)]
    for step in steps[1:] + steps[:1]:
        block = block + lax.ppermute(block, axis, [(i, i ^ step) for i in range(size)])
    return block


def after(value, *others):
    return lax.optimization_barrier((value, *others))[0]


def local(image, deconv_weight, norm_gain, norm_shift, first_weight, first_bias, second_weight, second_bias):
    rows, width, cin = image.shape
    taps, _, _, lanes = deconv_weight.shape
    columns = lax.axis_size("fsdp")
    cout = lanes * columns
    assert columns == 2 and rows == HALO and width % EDGE == 0 and lanes == LANES
    n_rows = lax.axis_size("rows")
    count = float(2 * rows * n_rows * 2 * width * columns * (cout // NORM_GROUPS))
    swap = [(0, 1), (1, 0)]
    to_next = [(i, i + 1) for i in range(n_rows - 1)]
    to_previous = [((i + 1) % n_rows, i) for i in range(n_rows)]
    total = width + EDGE
    hbm = pl.BlockSpec(memory_space=pltpu.HBM)
    vmem = pl.BlockSpec(memory_space=pltpu.VMEM)
    bf16, f32 = jnp.bfloat16, jnp.float32

    def call(kernel, ins, outs, scratch, name, flops=0):
        return pl.pallas_call(
            kernel,
            out_shape=tuple(jax.ShapeDtypeStruct(*o) for o in outs),
            in_specs=ins,
            out_specs=(vmem,) * len(outs),
            scratch_shapes=scratch,
            compiler_params=pltpu.CompilerParams(vmem_limit_bytes=VMEM_BYTES),
            cost_estimate=pl.CostEstimate(flops=flops, bytes_accessed=2**21, transcendentals=0),
            name=name,
        )

    in_hbm = functools.partial(pltpu.with_memory_space_constraint, memory_space=pltpu.HBM)
    shape_w = (taps, taps // 2, 2, cin, lanes)
    following = lax.ppermute(image, "rows", to_previous)
    near, edges = call(
        cut_kernel,
        [hbm],
        [(image.shape, bf16), ((rows, EDGE, cin), bf16)],
        [pltpu.SemaphoreType.DMA((2,))],
        "cut",
    )(in_hbm(image))
    edge = lax.ppermute(edges, "fsdp", swap)
    other_w = lax.ppermute(deconv_weight, "fsdp", swap).reshape(shape_w)
    first_other = lax.ppermute(after(first_weight, edges), "fsdp", swap)
    second_other = lax.ppermute(after(second_weight, edges), "fsdp", swap)
    (own_w,) = call(near_kernel, [hbm], [(shape_w, bf16)], [pltpu.SemaphoreType.DMA(())], "near_weights")(
        in_hbm(after(deconv_weight, edges).reshape(shape_w))
    )
    lines = jnp.concatenate([after(near, own_w), edge], axis=1)
    above = lax.ppermute(lines, "rows", to_next)
    u_line = (2, total, cout)
    xs, u, part, tail, sums = call(
        own_kernel,
        [vmem] * 3,
        [
            ((rows, total, 3 * cin), bf16),
            ((2 * rows - 2, *u_line), bf16),
            (u_line, f32),
            ((2, *u_line), f32),
            ((2, cout), f32),
        ],
        [],
        "deconv_own",
        flops=2 * 2 * (2 * rows - 1) * total * 4 * cin * cout,
    )(lines, own_w, other_w)
    (next_edges,) = call(pick_kernel, [vmem], [((rows, EDGE, cin), bf16)], [], "next_edges")(following)
    next_edge = lax.ppermute(next_edges, "fsdp", swap)
    u_next, xs_next, stats = call(
        next_kernel,
        [vmem] * 6,
        [((2, *u_line), bf16), ((1, total, 3 * cin), bf16), ((8, cout // 2), f32)],
        [],
        "deconv_next",
        flops=2 * 2 * total * 4 * cin * cout,
    )(following, next_edge, tail, sums, own_w, other_w)
    (halo,) = call(
        halo_kernel,
        [vmem] * 8,
        [((4, *u_line), bf16)],
        [pltpu.VMEM((HALO, total, 3 * cin), bf16), pltpu.VMEM((1, total, 3 * cin), bf16)],
        "deconv_halo",
        flops=2 * 2 * 4 * total * 4 * cin * cout,
    )(above, following, next_edge, xs, xs_next, part, own_w, other_w)

    totals = total_over(total_over(stats, "fsdp"), "rows")
    params = jnp.stack([norm_gain, norm_shift, first_bias, second_bias])
    (out,) = call(
        functools.partial(conv_kernel, count),
        [vmem] * 9,
        [((2 * rows, 2 * width, cout), bf16)],
        [
            pltpu.VMEM((2 * rows + 2 * HALO, total, 4 * cout), bf16),
            pltpu.VMEM((2 * rows + 2, total, 4 * cout), bf16),
            pltpu.VMEM((2, 2 * rows, 2 * width, lanes), f32),
        ],
        "convs",
        flops=5 * 10**9,
    )(u, u_next, halo, totals, params, first_weight, first_other, second_weight, second_other)
    return out


def solution(mesh):
    placed = (
        P(("groups", "rows"), "fsdp", None),
        P(None, None, None, "fsdp"),
        P(),
        P(),
        P(None, None, None, "fsdp"),
        P(),
        P(None, None, None, "fsdp"),
        P(),
    )
    return jax.shard_map(
        local,
        mesh=mesh,
        in_specs=placed,
        out_specs=P(("groups", "rows"), "fsdp", None),
        check_vma=False,
    )
```

```python
import functools

import jax
import jax.numpy as jnp
from jax import lax
from jax.experimental import pallas as pl
from jax.experimental.pallas import tpu as pltpu
from jax.sharding import PartitionSpec as P

NORM_GROUPS = 32
HALO = 2
EDGE = 16
LANES = 128
VMEM_BYTES = 24 * 2**20


def silu_of_half(h):
    return h + h * jnp.tanh(h)


def edge_mask(width):
    column = lax.axis_index("fsdp")
    last = lax.axis_size("fsdp") - 1
    cell = lax.broadcasted_iota(jnp.int32, (width + EDGE, 1), 0) - width
    right = (cell < EDGE // 2) & (column < last)
    left = (cell >= EDGE // 2) & (column > 0)
    return (cell < 0) | right | left


def cut_kernel(image_ref, near_ref, edges_ref, sems):
    width = image_ref.shape[1]
    start = pl.multiple_of((1 - lax.axis_index("fsdp")) * (width - EDGE), EDGE)
    copies = [
        pltpu.make_async_copy(image_ref.at[:, pl.ds(start, EDGE), :], edges_ref, sems.at[0]),
        pltpu.make_async_copy(image_ref, near_ref, sems.at[1]),
    ]
    for copy in copies:
        copy.start()
    for copy in copies:
        copy.wait()


def pick_kernel(lines_ref, edges_ref):
    width = lines_ref.shape[1]
    at_left = lax.axis_index("fsdp") == 0

    @pl.when(at_left)
    def _():
        edges_ref[...] = lines_ref[:, width - EDGE :]

    @pl.when(jnp.logical_not(at_left))
    def _():
        edges_ref[...] = lines_ref[:, :EDGE]


def near_kernel(weight_ref, near_ref, sem):
    copy = pltpu.make_async_copy(weight_ref, near_ref, sem)
    copy.start()
    copy.wait()


def spread_line(out, main, edge, inside=True):
    width, cin = main.shape
    line = jnp.concatenate([main.astype(jnp.float32), edge.astype(jnp.float32)], axis=0)
    line = jnp.where(edge_mask(width) & inside, line, 0.0)
    out[:, 0:cin] = pltpu.roll(line, width + EDGE - 1, 0).astype(jnp.bfloat16)
    out[:, cin : 2 * cin] = line.astype(jnp.bfloat16)
    out[:, 2 * cin : 3 * cin] = pltpu.roll(line, 1, 0).astype(jnp.bfloat16)


def tap_dot(lines, phase, kr, own_w, other_w):
    count, total, lanes = lines.shape
    cin = lanes // 3
    low = (1 - phase) * cin
    weight = jnp.concatenate(
        [ref[kr, :, 1 - phase].reshape(2 * cin, ref.shape[-1]) for ref in (own_w, other_w)], axis=1
    )
    out = jnp.dot(
        lines[:, :, low : low + 2 * cin].reshape(count * total, 2 * cin),
        weight,
        preferred_element_type=jnp.float32,
    )
    return out.reshape(count, total, weight.shape[-1])


def add_sums(line, width):
    values = line[:width].astype(jnp.float32)
    return jnp.concatenate(
        [jnp.sum(values, axis=0, keepdims=True), jnp.sum(values * values, axis=0, keepdims=True)], axis=0
    )


def own_kernel(lines_ref, own_w, other_w, xs_ref, u_ref, part_ref, tail_ref, sums_ref):
    rows, total, _ = lines_ref.shape
    width = total - EDGE
    for row in range(rows):
        spread_line(xs_ref.at[row], lines_ref[row, :width], lines_ref[row, width:])
    first_here = lax.axis_index("rows") == 0
    sums = jnp.zeros((2, u_ref.shape[-1]), jnp.float32)
    for phase in range(2):
        dot = functools.partial(tap_dot, phase=phase, own_w=own_w, other_w=other_w)
        upper = dot(xs_ref[...], kr=1)
        lower = dot(xs_ref[...], kr=3)
        part_ref[phase] = upper[0]
        tail_ref[phase, 1] = lower[rows - 1]
        even = [(upper[row + 1] + lower[row]).astype(jnp.bfloat16) for row in range(rows - 1)]
        upper = dot(xs_ref[...], kr=2)
        lower = dot(xs_ref[1:], kr=0)
        tail_ref[phase, 0] = upper[rows - 1]
        odd = [(upper[row] + lower[row]).astype(jnp.bfloat16) for row in range(rows - 1)]
        for row in range(rows - 1):
            u_ref[2 * row, phase] = odd[row]
            u_ref[2 * row + 1, phase] = even[row]
            sums += add_sums(odd[row], width) + add_sums(even[row], width)
        sums += jnp.where(first_here, add_sums(part_ref[phase].astype(jnp.bfloat16), width), 0.0)
    sums_ref[...] = sums


def next_kernel(next_ref, edge_ref, tail_ref, sums_ref, own_w, other_w, u_ref, xs_ref, stats_ref):
    width = next_ref.shape[1]
    last_here = lax.axis_index("rows") == lax.axis_size("rows") - 1
    spread_line(xs_ref.at[0], next_ref[0], edge_ref[0], jnp.logical_not(last_here))
    column = lax.axis_index("fsdp")
    sums = sums_ref[...]
    for phase in range(2):
        dot = functools.partial(tap_dot, phase=phase, own_w=own_w, other_w=other_w)
        odd = (tail_ref[phase, 0] + dot(xs_ref[...], kr=0)[0]).astype(jnp.bfloat16)
        even = (tail_ref[phase, 1] + dot(xs_ref[...], kr=1)[0]).astype(jnp.bfloat16)
        u_ref[0, phase] = odd
        u_ref[1, phase] = even
        sums += add_sums(odd, width) + jnp.where(last_here, 0.0, add_sums(even, width))
    half = sums.shape[1] // 2
    halves = []
    for row in range(2):
        own, other = sums[row : row + 1, :half], sums[row : row + 1, half:]
        halves += [jnp.where(column == 0, own, other), jnp.where(column == 0, other, own)]
    stats_ref[...] = jnp.concatenate(halves + [jnp.zeros((4, half), jnp.float32)], axis=0)


def halo_kernel(above_ref, next_ref, next_edge_ref, xs_ref, xs_next_ref, part_ref, own_w, other_w, u_ref, xs_above, xs_below):
    width = next_ref.shape[1]
    for row in range(HALO):
        spread_line(xs_above.at[row], above_ref[row, :width], above_ref[row, width:])
    more_below = lax.axis_index("rows") < lax.axis_size("rows") - 1
    spread_line(xs_below.at[0], next_ref[1], next_edge_ref[1], more_below)
    for phase in range(2):
        dot = functools.partial(tap_dot, phase=phase, own_w=own_w, other_w=other_w)
        outer = dot(xs_above[...], kr=3)
        u_ref[0, phase] = (outer[0] + dot(xs_above[1:2], kr=1)[0]).astype(jnp.bfloat16)
        u_ref[2, phase] = (outer[1] + part_ref[phase]).astype(jnp.bfloat16)
        u_ref[1, phase] = (dot(xs_above[1:2], kr=2)[0] + dot(xs_ref[0:1], kr=0)[0]).astype(jnp.bfloat16)
        u_ref[3, phase] = (dot(xs_next_ref[...], kr=2)[0] + dot(xs_below[...], kr=0)[0]).astype(jnp.bfloat16)


def group_sum(v, width):
    lane = lax.broadcasted_iota(jnp.int32, v.shape, 1)
    size = v.shape[1]
    step = 1
    while step < width:
        v = v + jnp.where(
            (lane & step) == 0, pltpu.roll(v, size - step, 1), pltpu.roll(v, step, 1)
        )
        step *= 2
    return v


def fill(ref, row, even, odd):
    total, channels = even.shape
    ref[row, :, 0:channels] = pltpu.roll(odd, 1, 0).astype(jnp.bfloat16)
    ref[row, :, channels : 2 * channels] = even.astype(jnp.bfloat16)
    ref[row, :, 2 * channels : 3 * channels] = odd.astype(jnp.bfloat16)
    ref[row, :, 3 * channels : 4 * channels] = pltpu.roll(even, total - 1, 0).astype(jnp.bfloat16)


def conv_kernel(
    count, u_ref, u_next_ref, halo_ref, stats_ref, params_ref, own_w1, other_w1, own_w2, other_w2, out_ref, g, act, mixed
):
    early, _, total, cout = u_ref.shape
    main = early + u_next_ref.shape[0]
    lines = main + 2 * HALO
    width = total - EDGE
    half = own_w1.shape[-1]
    column = lax.axis_index("fsdp")
    own_at = pl.multiple_of(column * half, half)
    other_at = pl.multiple_of((1 - column) * half, half)

    def own_first(row):
        low, high = row[:, :half], row[:, half:]
        return jnp.concatenate([jnp.where(column == 0, low, high), jnp.where(column == 0, high, low)], axis=1)

    def kernel_row(a, own, other):
        return jnp.concatenate(
            [
                jnp.concatenate([ref[a, b, pl.ds(at, half), :] for b in range(3) for at in (own_at, other_at)], axis=0)
                for ref in (own, other)
            ],
            axis=1,
        )

    block = stats_ref[...]
    width_group = cout // NORM_GROUPS
    sums = jnp.concatenate([block[0:1], block[1:2]], axis=1)
    squares = jnp.concatenate([block[2:3], block[3:4]], axis=1)
    mean = group_sum(sums, width_group) / count
    spread = group_sum(squares, width_group) / count - mean * mean
    scale = lax.rsqrt(spread + 1e-05) * params_ref[0:1]
    shift = own_first(0.5 * (params_ref[1:2] - mean * scale))
    scale = own_first(0.5 * scale)
    bias1 = own_first(0.5 * params_ref[2:3])
    bias2 = own_first(params_ref[3:4])

    edge_seen = edge_mask(width)[width:]
    place = lax.axis_index("rows")
    last = lax.axis_size("rows") - 1

    def masked(row, beyond, value):
        value = jnp.concatenate([value[:width], jnp.where(edge_seen, value[width:], 0.0)], axis=0)
        if row < beyond:
            return jnp.where(place > 0, value, 0.0)
        if row >= lines - 2 * HALO + beyond:
            return jnp.where(place < last, value, 0.0)
        return value

    def hidden(row):
        if row < 3:
            source = halo_ref.at[row]
        elif row < 3 + early:
            source = u_ref.at[row - 3]
        elif row < 3 + main:
            source = u_next_ref.at[row - 3 - early]
        else:
            source = halo_ref.at[3]
        fill(
            g,
            row,
            *[
                masked(row, HALO, silu_of_half(source[phase].astype(jnp.float32) * scale + shift))
                for phase in range(2)
            ],
        )

    def dots(source, start, size, cells, phase, own, other):
        total = None
        for a in range(3):
            term = jnp.dot(
                source[start + a : start + a + size, 0:cells, phase * cout : (phase + 3) * cout].reshape(
                    size * cells, 3 * cout
                ),
                kernel_row(a, own, other),
                preferred_element_type=jnp.float32,
            )
            total = term if total is None else total + term
        return total.reshape(size, cells, cout)

    chunk = 2

    def first(start):
        return [dots(g, start, chunk, total, phase, own_w1, other_w1) for phase in range(2)]

    def activate(start, results):
        for row in range(chunk):
            fill(
                act,
                start + row,
                *[masked(start + row, 1, silu_of_half(0.5 * r[row] + bias1)) for r in results],
            )

    def second(start):
        for phase in range(2):
            acc = dots(act, start, chunk, width, phase, own_w2, other_w2) + bias2
            for row in range(chunk):
                for side in range(2):
                    mixed[side, start + row, pl.ds(phase, width, stride=2), :] = acc[
                        row, :, side * half : (side + 1) * half
                    ]
        for row in range(start, start + chunk):
            out_ref[row, :, pl.ds(own_at, half)] = mixed[0, row].astype(jnp.bfloat16)
            out_ref[row, :, pl.ds(other_at, half)] = mixed[1, row].astype(jnp.bfloat16)

    for row in range(2 * chunk):
        hidden(row)
    for start in range(0, lines - 2, chunk):
        results = first(start)
        for row in range(start + 2 * chunk, min(start + 3 * chunk, lines)):
            hidden(row)
        if start >= 2 * chunk:
            second(start - 2 * chunk)
        activate(start, results)
    second(lines - 4 - chunk)


def total_over(block, axis):
    size = lax.axis_size(axis)
    if size & (size - 1):
        return lax.psum(block, axis)
    steps = [2**n for n in range(size.bit_length() - 1)]
    for step in steps[1:2] + steps[:1] + steps[2:]:
        block = block + lax.ppermute(block, axis, [(i, i ^ step) for i in range(size)])
    return block


def after(value, *others):
    return lax.optimization_barrier((value, *others))[0]


def local(image, deconv_weight, norm_gain, norm_shift, first_weight, first_bias, second_weight, second_bias):
    rows, width, cin = image.shape
    taps, _, _, lanes = deconv_weight.shape
    columns = lax.axis_size("fsdp")
    cout = lanes * columns
    assert columns == 2 and rows == HALO and width % EDGE == 0 and lanes == LANES
    n_rows = lax.axis_size("rows")
    count = float(2 * rows * n_rows * 2 * width * columns * (cout // NORM_GROUPS))
    swap = [(0, 1), (1, 0)]
    to_next = [(i, i + 1) for i in range(n_rows - 1)]
    to_previous = [((i + 1) % n_rows, i) for i in range(n_rows)]
    total = width + EDGE
    hbm = pl.BlockSpec(memory_space=pltpu.HBM)
    vmem = pl.BlockSpec(memory_space=pltpu.VMEM)
    bf16, f32 = jnp.bfloat16, jnp.float32

    def call(kernel, ins, outs, scratch, name, flops=0):
        return pl.pallas_call(
            kernel,
            out_shape=tuple(jax.ShapeDtypeStruct(*o) for o in outs),
            in_specs=ins,
            out_specs=(vmem,) * len(outs),
            scratch_shapes=scratch,
            compiler_params=pltpu.CompilerParams(vmem_limit_bytes=VMEM_BYTES),
            cost_estimate=pl.CostEstimate(flops=flops, bytes_accessed=2**21, transcendentals=0),
            name=name,
        )

    in_hbm = functools.partial(pltpu.with_memory_space_constraint, memory_space=pltpu.HBM)
    shape_w = (taps, taps // 2, 2, cin, lanes)
    following = lax.ppermute(image, "rows", to_previous)
    near, edges = call(
        cut_kernel,
        [hbm],
        [(image.shape, bf16), ((rows, EDGE, cin), bf16)],
        [pltpu.SemaphoreType.DMA((2,))],
        "cut",
    )(in_hbm(image))
    edge = lax.ppermute(edges, "fsdp", swap)
    other_w = lax.ppermute(deconv_weight, "fsdp", swap).reshape(shape_w)
    first_other = lax.ppermute(after(first_weight, edges), "fsdp", swap)
    second_other = lax.ppermute(after(second_weight, edges), "fsdp", swap)
    (own_w,) = call(near_kernel, [hbm], [(shape_w, bf16)], [pltpu.SemaphoreType.DMA(())], "near_weights")(
        in_hbm(after(deconv_weight, edges).reshape(shape_w))
    )
    lines = jnp.concatenate([after(near, own_w), edge], axis=1)
    above = lax.ppermute(lines, "rows", to_next)
    u_line = (2, total, cout)
    xs, u, part, tail, sums = call(
        own_kernel,
        [vmem] * 3,
        [
            ((rows, total, 3 * cin), bf16),
            ((2 * rows - 2, *u_line), bf16),
            (u_line, f32),
            ((2, *u_line), f32),
            ((2, cout), f32),
        ],
        [],
        "deconv_own",
        flops=2 * 2 * (2 * rows - 1) * total * 4 * cin * cout,
    )(lines, own_w, other_w)
    (next_edges,) = call(pick_kernel, [vmem], [((rows, EDGE, cin), bf16)], [], "next_edges")(following)
    next_edge = lax.ppermute(next_edges, "fsdp", swap)
    u_next, xs_next, stats = call(
        next_kernel,
        [vmem] * 6,
        [((2, *u_line), bf16), ((1, total, 3 * cin), bf16), ((8, cout // 2), f32)],
        [],
        "deconv_next",
        flops=2 * 2 * total * 4 * cin * cout,
    )(following, next_edge, tail, sums, own_w, other_w)
    (halo,) = call(
        halo_kernel,
        [vmem] * 8,
        [((4, *u_line), bf16)],
        [pltpu.VMEM((HALO, total, 3 * cin), bf16), pltpu.VMEM((1, total, 3 * cin), bf16)],
        "deconv_halo",
        flops=2 * 2 * 4 * total * 4 * cin * cout,
    )(above, following, next_edge, xs, xs_next, part, own_w, other_w)

    totals = total_over(total_over(stats, "fsdp"), "rows")
    params = jnp.stack([norm_gain, norm_shift, first_bias, second_bias])
    (out,) = call(
        functools.partial(conv_kernel, count),
        [vmem] * 9,
        [((2 * rows, 2 * width, cout), bf16)],
        [
            pltpu.VMEM((2 * rows + 2 * HALO, total, 4 * cout), bf16),
            pltpu.VMEM((2 * rows + 2, total, 4 * cout), bf16),
            pltpu.VMEM((2, 2 * rows, 2 * width, lanes), f32),
        ],
        "convs",
        flops=5 * 10**9,
    )(u, u_next, halo, totals, params, first_weight, first_other, second_weight, second_other)
    return out


def solution(mesh):
    placed = (
        P(("groups", "rows"), "fsdp", None),
        P(None, None, None, "fsdp"),
        P(),
        P(),
        P(None, None, None, "fsdp"),
        P(),
        P(None, None, None, "fsdp"),
        P(),
    )
    return jax.shard_map(
        local,
        mesh=mesh,
        in_specs=placed,
        out_specs=P(("groups", "rows"), "fsdp", None),
        check_vma=False,
    )
```
